32 devices in a mesh: task: 4 (over y, core), feat: 8 (over z, x).
Axes of the slice: x: 2, y: 2, z: 4, core: 2. Of those that a mesh axis runs over, the one named last changes fastest.
Arguments:
- tokens: bfloat16 [4, 32, 512, 512], P('task', 'feat'), may hold values from -6 to 6
- cotangent: bfloat16 [4, 32, 512, 512], P('task', 'feat'), may hold values from -6 to 6
- attn_weights: bfloat16 [4096, 512], replicated
- weight_in: bfloat16 [512, 2048], replicated, may hold values from -0.25 to 0.25
- weight_out: bfloat16 [2048, 512], replicated, may hold values from -0.125 to 0.125
- norm_params: float32 [6, 512], replicated
- master_attn: float32 [4096, 512], P(('task', 'feat')), may hold values from -0.25 to 0.25
- master_in: float32 [512, 2048], P(None, ('task', 'feat')), may hold values from -0.25 to 0.25
- master_out: float32 [2048, 512], P(('task', 'feat')), may hold values from -0.125 to 0.125
- first_attn: float32 [4096, 512], P(('task', 'feat')), may hold values from -0.0008544922 to 0.0008544922
- first_in: float32 [512, 2048], P(None, ('task', 'feat')), may hold values from -0.0008544922 to 0.0008544922
- first_out: float32 [2048, 512], P(('task', 'feat')), may hold values from -0.0008544922 to 0.0008544922
- first_norms: float32 [6, 512], replicated, may hold values from -0.0034179688 to 0.0034179688
- second_attn: float32 [4096, 512], P(('task', 'feat')), may hold values from 2.384186e-10 to 9.536744e-10
- second_in: float32 [512, 2048], P(None, ('task', 'feat')), may hold values from 2.384186e-10 to 9.536744e-10
- second_out: float32 [2048, 512], P(('task', 'feat')), may hold values from 2.384186e-10 to 9.536744e-10
- second_norms: float32 [6, 512], replicated, may hold values from 3.8146974e-09 to 1.525879e-08
- sample_count: int32 [4], P('task'), may hold values from 64 to 512, as said below
- feature_count: int32 [4], P('task'), may hold values from 4 to 32, as said below
Outputs:
- block_out: bfloat16 [4, 32, 512, 512], P('task', 'feat')
- input_grad: bfloat16 [4, 32, 512, 512], P('task', 'feat')
- grad_norm: float32 [1], replicated
- new_attn: float32 [4096, 512], P(('task', 'feat'))
- new_in: float32 [512, 2048], P(None, ('task', 'feat'))
- new_out: float32 [2048, 512], P(('task', 'feat'))
- new_norms: float32 [6, 512], replicated
- moment_attn: float32 [4096, 512], P(('task', 'feat'))
- moment_in: float32 [512, 2048], P(None, ('task', 'feat'))
- moment_out: float32 [2048, 512], P(('task', 'feat'))
- moment_norms: float32 [6, 512], replicated
- square_attn: float32 [4096, 512], P(('task', 'feat'))
- square_in: float32 [512, 2048], P(None, ('task', 'feat'))
- square_out: float32 [2048, 512], P(('task', 'feat'))
- square_norms: float32 [6, 512], replicated
- copy_attn: bfloat16 [4096, 512], replicated
- copy_in: bfloat16 [512, 2048], replicated
- copy_out: bfloat16 [2048, 512], replicated
The draws below stay inside these ranges and needn't reach their ends.
Inputs may be any that keep to these rules, and one draw needn't show every extreme that they name: `sample_count`: each task uses at least 64 samples, and some task uses all 512. `feature_count`: each task uses at least 4 features, and some task uses all 32.
All inputs are finite; a program needn't handle non-finite values.
Results may differ from the reference program's by a relative error of at most 0.015.
Values may be sent and summed in bfloat16 or wider, within the bound.
No kernel may reach another device: no remote copies, remote signals or barrier semaphores. Data moves between devices by JAX's collectives and lax.ppermute only.
A program may use at most 384 MiB of HBM per device.

```python
import math
import jax
import jax.numpy as jnp
from jax import lax

D = 512
HEADS = 8
FF = 2048
SAMPLES = 512
FEATS = 32
STEP = 5
TASKS = 4


def draw_attn_weights(key, part):
    noise = jnp.clip(jax.random.normal(jax.random.fold_in(key, 101), (8 * D, D), jnp.float32), -6.0, 6.0)
    block_index = jnp.arange(8 * D) // D
    factor = jnp.where(block_index == 3, 3.0, jnp.where(block_index == 7, 2.0, 1.0)) / jnp.sqrt(jnp.float32(D))
    return (noise * factor[:, None]).astype(jnp.bfloat16)


def draw_norm_params(key, part):
    gains = 1.0 + 0.1 * jax.random.uniform(jax.random.fold_in(key, 202), (6, D), jnp.float32, -1.0, 1.0)
    shifts = 0.3 * jnp.clip(jax.random.normal(jax.random.fold_in(key, 203), (6, D), jnp.float32), -4.0, 4.0)
    is_gain = (jnp.arange(6) % 2 == 0)[:, None]
    return jnp.where(is_gain, gains, shifts).astype(jnp.float32)


def ragged_counts(key, most):
    key_base, key_level, key_top = jax.random.split(key, 3)
    base = jax.random.randint(key_base, (TASKS,), most // 8, most + 1)
    level = jax.random.randint(key_level, (TASKS,), 0, 3)
    divisor = jnp.array([1, 2, 4], jnp.int32)[level]
    counts = jnp.maximum(base // divisor, most // 8)
    chosen = jax.random.randint(key_top, (), 0, TASKS)
    return counts.at[chosen].set(most).astype(jnp.int32)


def draw_sample_count(key, part):
    return ragged_counts(jax.random.fold_in(key, 301), SAMPLES)


def draw_feature_count(key, part):
    return ragged_counts(jax.random.fold_in(key, 302), FEATS)


def block_levels(rng, shape, cuts, least, top_value):
    def one(axis_at, blocks):
        draws = jax.random.uniform(jax.random.fold_in(jax.random.fold_in(rng, 6), axis_at), (blocks,), jnp.float32, least / len(cuts), top_value / len(cuts))
        return jnp.repeat(jnp.exp(draws), shape[axis_at] // blocks).reshape((-1,) + (1,) * (len(shape) - axis_at - 1))

    level = one(*cuts[0])
    for cut in cuts[1:]:
        level = level * one(*cut)
    return level


def gaussian(key, extent, scale, reach, cuts=(), held_as=jnp.bfloat16):
    values = scale * jax.random.normal(key, extent, jnp.float32)
    if cuts:
        values = values * block_levels(key, extent, cuts, -0.22, 0.18)
    return jnp.clip(values, -reach, reach).astype(held_as)


def setup_inputs(seed: int = 0) -> dict:
    key_of = jax.random.split(jax.random.key(seed), 20)
    return {
        "tokens": gaussian(key_of[0], (TASKS, FEATS, SAMPLES, D), 1.0, 6.0, ((0, 4), (1, 8))),
        "cotangent": gaussian(key_of[1], (TASKS, FEATS, SAMPLES, D), 1.0, 6.0, ((0, 4), (1, 8))),
        "attn_weights": draw_attn_weights(jax.random.fold_in(key_of[19], 71), 0),
        "weight_in": gaussian(key_of[3], (D, FF), D ** -0.5, 0.25),
        "weight_out": gaussian(key_of[4], (FF, D), FF ** -0.5, 0.125),
        "norm_params": draw_norm_params(jax.random.fold_in(key_of[19], 71), 0),
        "master_attn": gaussian(key_of[6], (8 * D, D), D ** -0.5, 0.25, ((0, 32),), jnp.float32),
        "master_in": gaussian(key_of[7], (D, FF), D ** -0.5, 0.25, ((1, 32),), jnp.float32),
        "master_out": gaussian(key_of[8], (FF, D), FF ** -0.5, 0.125, ((0, 32),), jnp.float32),
        "first_attn": gaussian(key_of[9], (8 * D, D), (0.11 / (8 * D * D + 2 * D * FF) ** 0.5), 0.0008544922, ((0, 32),), jnp.float32),
        "first_in": gaussian(key_of[10], (D, FF), (0.11 / (8 * D * D + 2 * D * FF) ** 0.5), 0.0008544922, ((1, 32),), jnp.float32),
        "first_out": gaussian(key_of[11], (FF, D), (0.11 / (8 * D * D + 2 * D * FF) ** 0.5), 0.0008544922, ((0, 32),), jnp.float32),
        "first_norms": gaussian(key_of[12], (6, D), (0.44 / (8 * D * D + 2 * D * FF) ** 0.5), 0.0034179688, (), jnp.float32),
        "second_attn": jnp.clip(jnp.exp(math.log(9.536743617033494e-10) - 1.3862944 * jax.random.uniform(key_of[13], (8 * D, D), jnp.float32) ** block_levels(key_of[13], (8 * D, D), ((0, 32),), -0.2, 0.2)), 2.3841859042583735e-10, 9.536743617033494e-10),
        "second_in": jnp.clip(jnp.exp(math.log(9.536743617033494e-10) - 1.3862944 * jax.random.uniform(key_of[14], (D, FF), jnp.float32) ** block_levels(key_of[14], (D, FF), ((1, 32),), -0.2, 0.2)), 2.3841859042583735e-10, 9.536743617033494e-10),
        "second_out": jnp.clip(jnp.exp(math.log(9.536743617033494e-10) - 1.3862944 * jax.random.uniform(key_of[15], (FF, D), jnp.float32) ** block_levels(key_of[15], (FF, D), ((0, 32),), -0.2, 0.2)), 2.3841859042583735e-10, 9.536743617033494e-10),
        "second_norms": jnp.clip(jnp.exp(jax.random.uniform(key_of[16], (6, D), jnp.float32, math.log(3.814697446813398e-09), math.log(1.525878978725359e-08))), 3.814697446813398e-09, 1.525878978725359e-08),
        "sample_count": draw_sample_count(jax.random.fold_in(key_of[19], 71), 0),
        "feature_count": draw_feature_count(jax.random.fold_in(key_of[19], 71), 0),
    }


@jax.custom_vjp
def low(v):
    return lax.optimization_barrier(v.astype(jnp.bfloat16)).astype(jnp.float32)

@jax.custom_vjp
def low_back(v):
    return v

def low_keep(v):
    return (low(v), None)

def low_pass(kept, grad):
    return (grad,)

def back_keep(v):
    return (v, None)

def back_low(kept, grad):
    return (low(grad),)
low.defvjp(low_keep, low_pass)
low_back.defvjp(back_keep, back_low)
HIGHEST = lax.Precision.HIGHEST
NEGATIVE = -1e+30
LN_EPS = 1e-05
CLIP_AT = 1.0
BETA_ONE = 0.9
BETA_TWO = 0.999
RATE = 0.02
NORM_RATE = 0.25
DECAY = 0.1
ADAM_EPS = 1e-08

def layer_norm(values, gain, shift):
    center = lax.optimization_barrier(jnp.mean(values, axis=-1, keepdims=True))
    centred = values - center
    spread = lax.optimization_barrier(jnp.mean(centred * centred, axis=-1, keepdims=True))
    return centred * lax.rsqrt(spread + LN_EPS) * gain + shift

def project(values, matrix):
    return jnp.einsum('...d,de->...e', values, matrix, precision=HIGHEST)

def attend(rows, weights, key_live):
    batch, length, model_width = rows.shape
    head_size = model_width // HEADS
    queries = low(low_back(project(rows, weights[0]))).reshape(batch, length, HEADS, head_size)
    key_rows = low(low_back(project(rows, weights[1]))).reshape(batch, length, HEADS, head_size)
    values = low(low_back(project(rows, weights[2]))).reshape(batch, length, HEADS, head_size)
    scores = low_back(jnp.einsum('bqhe,bkhe->bhqk', queries, key_rows, precision=HIGHEST) * head_size ** (-0.5))
    scores = jnp.where(key_live[None, None, None, :], scores, NEGATIVE)
    probs = low(jax.nn.softmax(scores, axis=-1))
    mixed = jnp.einsum('bhqk,bkhe->bqhe', probs, values, precision=HIGHEST).reshape(batch, length, model_width)
    mixed = low(low_back(mixed))
    return low_back(project(mixed, weights[3]))

def forward(inputs, attn, weight_one, weight_two, norms, sample_live, feat_live):
    feat_total, samples, model_width = inputs.shape
    weights = attn.reshape(2, 4, model_width, model_width)
    first = low(layer_norm(inputs, norms[0], norms[1]))

    def sample_block(rows):
        return attend(rows, weights[0], sample_live)
    after_one = inputs + lax.map(jax.checkpoint(sample_block), first[:, None]).reshape(feat_total, samples, model_width)
    second = low(layer_norm(after_one, norms[2], norms[3]))
    group_size = min(64, samples)
    grouped = second.transpose(1, 0, 2).reshape(samples // group_size, group_size, feat_total, model_width)

    def feature_block(rows):
        return attend(rows, weights[1], feat_live)
    mixed_two = lax.map(jax.checkpoint(feature_block), grouped)
    mixed_two = mixed_two.reshape(samples, feat_total, model_width).transpose(1, 0, 2)
    after_two = after_one + mixed_two
    third = low(layer_norm(after_two, norms[4], norms[5]))
    pre = low_back(project(third, weight_one))
    hidden = low(jax.nn.gelu(pre))
    return after_two + low_back(project(hidden, weight_two))

def adam_step(weight, grad, first_m, second_m, rate):
    moment = BETA_ONE * first_m + (1.0 - BETA_ONE) * grad
    square = BETA_TWO * second_m + (1.0 - BETA_TWO) * grad * grad
    fix_one = 1.0 - BETA_ONE ** STEP
    fix_two = 1.0 - BETA_TWO ** STEP
    fresh = weight - rate * (moment / fix_one / (jnp.sqrt(square / fix_two) + ADAM_EPS) + DECAY * weight)
    return (fresh, moment, square)

def reference(tokens, cotangent, attn_weights, weight_in, weight_out, norm_params, master_attn, master_in, master_out, first_attn, first_in, first_out, first_norms, second_attn, second_in, second_out, second_norms, sample_count, feature_count):
    params = (attn_weights.astype(jnp.float32), weight_in.astype(jnp.float32), weight_out.astype(jnp.float32), norm_params)

    def one_task(carry, item):
        task_tokens, task_cot, samples_used, feats_used = item
        sample_live = jnp.arange(SAMPLES) < samples_used
        feat_live = jnp.arange(FEATS) < feats_used
        live_mask = (feat_live[:, None] & sample_live[None, :]).astype(jnp.float32)[:, :, None]

        def run(inputs, attn, weight_one, weight_two, norms):
            return forward(inputs, attn, weight_one, weight_two, norms, sample_live, feat_live)
        result, pull = jax.vjp(run, task_tokens.astype(jnp.float32), *params)
        grads = pull(task_cot.astype(jnp.float32) * live_mask)
        carry = jax.tree.map(jnp.add, carry, tuple(grads[1:]))
        return (carry, (result.astype(jnp.bfloat16), grads[0].astype(jnp.bfloat16)))
    zeros = tuple((jnp.zeros(item.shape, jnp.float32) for item in params))
    sums, outputs = lax.scan(one_task, zeros, (tokens, cotangent, sample_count, feature_count))
    block_out, input_grad = outputs
    grad_attn, grad_in, grad_out, grad_norms = sums
    squares = jnp.sum(grad_attn * grad_attn) + jnp.sum(grad_in * grad_in) + jnp.sum(grad_out * grad_out) + jnp.sum(grad_norms * grad_norms)
    grad_norm = jnp.sqrt(squares)
    factor = jnp.minimum(1.0, CLIP_AT / (grad_norm + 1e-06))
    new_attn, moment_attn, square_attn = adam_step(master_attn, factor * grad_attn, first_attn, second_attn, RATE)
    new_in, moment_in, square_in = adam_step(master_in, factor * grad_in, first_in, second_in, RATE)
    new_out, moment_out, square_out = adam_step(master_out, factor * grad_out, first_out, second_out, RATE)
    new_norms, moment_norms, square_norms = adam_step(norm_params, factor * grad_norms, first_norms, second_norms, NORM_RATE)
    return (block_out, input_grad, grad_norm.reshape(1), new_attn, new_in, new_out, new_norms, moment_attn, moment_in, moment_out, moment_norms, square_attn, square_in, square_out, square_norms, new_attn.astype(jnp.bfloat16), new_in.astype(jnp.bfloat16), new_out.astype(jnp.bfloat16))
```

```python
import functools

import jax
import jax.numpy as jnp
from jax import lax
from jax.experimental import pallas as pl
from jax.experimental.pallas import tpu as pltpu
from jax.sharding import PartitionSpec as P

HEADS = 8
STEP = 5
NEGATIVE = -1e30
LN_EPS = 1e-05
CLIP_AT = 1.0
BETA_ONE = 0.9
BETA_TWO = 0.999
RATE = 0.02
NORM_RATE = 0.25
DECAY = 0.1
ADAM_EPS = 1e-08

BLOCK = 16
UNIT = 128
ROWS = 128
QUERIES = 256
VMEM_BYTES = 60 * 1024 * 1024

BF = jnp.bfloat16
F32 = jnp.float32
NN = ((1,), (0,))
NT = ((1,), (1,))
TN = ((0,), (0,))


def dot(left, right, dims=NN):
    return lax.dot_general(left, right, (dims, ((), ())), preferred_element_type=F32)


def normalize(values):
    center = jnp.mean(values, axis=-1, keepdims=True)
    centred = values - center
    spread = jnp.mean(centred * centred, axis=-1, keepdims=True)
    scale = lax.rsqrt(spread + LN_EPS)
    return centred * scale, scale


def normalize_back(normal, scale, grad, gain):
    d_normal = grad * gain
    mean_one = jnp.mean(d_normal, axis=-1, keepdims=True)
    mean_two = jnp.mean(d_normal * normal, axis=-1, keepdims=True)
    return scale * (d_normal - mean_one - normal * mean_two)


def column_sum(values):
    return jnp.sum(values, axis=0, keepdims=True)


def row_index(shape):
    return lax.broadcasted_iota(jnp.int32, shape, 0)


def sample_forward(
    counts, tokens, weights, norms, x_out, first_out, heads_out, mixed_out, log_out, turned
):
    samples, width = tokens.shape[1:]
    head_size = width // HEADS
    score_scale = head_size ** (-0.5)
    group = x_out.shape[0] * BLOCK

    @pl.when(pl.program_id(0) == 0)
    def _():
        for which in range(3):
            turned[which] = weights[which].T

    for low in range(0, samples, ROWS):
        rows = slice(low, low + ROWS)
        normal, _ = normalize(tokens[0, rows].astype(F32))
        first_out[0, rows] = (normal * norms[0:1] + norms[1:2]).astype(BF)
    first = first_out[0]
    for which in range(3):
        heads_out[0, which] = dot(turned[which], first, NT).astype(BF)
    live = row_index((samples, 1)) < counts[0]
    for head in range(HEADS):
        lanes = slice(head * head_size, (head + 1) * head_size)
        keys = heads_out[0, 1, lanes]
        values = heads_out[0, 2, lanes]
        for low in range(0, samples, QUERIES):
            cols = slice(low, low + QUERIES)
            scores = dot(keys, heads_out[0, 0, lanes, cols], TN) * score_scale
            scores = jnp.where(live, scores, NEGATIVE)
            top = jnp.max(scores, axis=0, keepdims=True)
            powers = jnp.exp(scores - top)
            total = jnp.sum(powers, axis=0, keepdims=True)
            mixed = dot(values, powers.astype(BF)) * (1.0 / total)
            mixed_out[0, lanes, cols] = mixed.astype(BF)
            log_out[0, head : head + 1, cols] = top + jnp.log(total)
    for low in range(0, samples, group):
        rows = slice(low, low + group)
        part = tokens[0, rows].astype(F32) + dot(mixed_out[0, :, rows], weights[3], TN)
        x_out[:, low // group, 0] = part.astype(BF).reshape(group // BLOCK, BLOCK, width)


def sample_backward(
    counts,
    d_x,
    tokens,
    first,
    heads,
    mixed,
    logs,
    weights,
    norms,
    grad_out,
    weight_out,
    norm_out,
    d_rows,
    d_mix,
    d_heads,
    d_turned,
    total,
    norm_total,
):
    samples, width = tokens.shape[1:]
    head_size = width // HEADS
    score_scale = head_size ** (-0.5)
    group = d_x.shape[0] * BLOCK
    step = pl.program_id(0)

    @pl.when(step == 0)
    def _():
        total[...] = jnp.zeros_like(total)
        norm_total[...] = jnp.zeros_like(norm_total)

    feature_live = counts[2] + step < counts[1]

    @pl.when(jnp.logical_not(feature_live))
    def _():
        grad_out[...] = jnp.zeros_like(grad_out)

    @pl.when(feature_live)
    def _():
        for low in range(0, samples, group):
            d_rows[low : low + group] = d_x[:, low // group, 0].reshape(group, width)
        d_mix[...] = dot(weights[3], d_rows[...], NT).astype(BF)
        total[3] += dot(mixed[0], d_rows[...])
        live = row_index((samples, 1)) < counts[0]
        for head in range(HEADS):
            lanes = slice(head * head_size, (head + 1) * head_size)
            keys = heads[0, 1, lanes]
            values = heads[0, 2, lanes]
            d_key = jnp.zeros((head_size, samples), F32)
            d_value = jnp.zeros((head_size, samples), F32)
            for low in range(0, samples, QUERIES):
                cols = slice(low, low + QUERIES)
                queries = heads[0, 0, lanes, cols]
                grads = d_mix[lanes, cols]
                shared = column_sum(grads.astype(F32) * mixed[0, lanes, cols].astype(F32))
                scores = dot(keys, queries, TN) * score_scale
                scores = jnp.where(live, scores, NEGATIVE)
                probs = jnp.exp(scores - logs[0, head : head + 1, cols])
                d_probs = dot(values, grads, TN)
                d_scores = (probs * (d_probs - shared)).astype(BF)
                d_heads[0, lanes, cols] = (dot(keys, d_scores) * score_scale).astype(BF)
                d_key = d_key + dot(queries, d_scores, NT)
                d_value = d_value + dot(grads, probs.astype(BF), NT)
            d_heads[1, lanes] = (d_key * score_scale).astype(BF)
            d_heads[2, lanes] = d_value.astype(BF)
        for which in range(3):
            d_turned[which] = d_heads[which].T
        for which in range(3):
            total[which] += dot(first[0], d_turned[which], TN)
        for low in range(0, samples, ROWS):
            rows = slice(low, low + ROWS)
            d_first = dot(d_turned[0, rows], weights[0], NT)
            d_first = d_first + dot(d_turned[1, rows], weights[1], NT)
            d_first = d_first + dot(d_turned[2, rows], weights[2], NT)
            normal, scale = normalize(tokens[0, rows].astype(F32))
            norm_total[0:1] += column_sum(d_first * normal)
            norm_total[1:2] += column_sum(d_first)
            back = normalize_back(normal, scale, d_first, norms[0:1])
            grad_out[0, rows] = (d_rows[rows].astype(F32) + back).astype(BF)

    @pl.when(step == pl.num_programs(0) - 1)
    def _():
        weight_out[...] = total[...].astype(BF)
        norm_out[...] = norm_total[...]


def gelu_parts(pre):
    root = 0.7978845608028654
    square = pre * pre
    curve = jnp.tanh(root * pre * (1.0 + 0.044715 * square))
    half = 0.5 * (1.0 + curve)
    slope = half + (0.5 * root) * pre * (1.0 - curve * curve) * (1.0 + 3 * 0.044715 * square)
    return pre * half, slope


def middle(
    counts,
    x_in,
    cot_in,
    weights,
    weight_in,
    weight_out,
    norms,
    y_out,
    d_out,
    grad_in_out,
    grad_out_out,
    grad_attn_out,
    norm_out,
    turned,
    order,
    back_order,
    x_one,
    normal_one,
    scale_one,
    normal_two,
    scale_two,
    x_two,
    low_rows,
    heads,
    d_heads,
    d_turned,
    mixed,
    d_mix,
    probs,
    live_grad,
    third,
    grad_rows,
    total_attn,
    total_in,
    total_out,
    norm_total,
):
    devices, _, local, _, width = x_in.shape
    features = devices * local
    cells = features * BLOCK
    head_size = width // HEADS
    score_scale = head_size ** (-0.5)
    hidden_width = weight_in.shape[1]
    step = pl.program_id(0)
    first_sample = (step * devices + counts[3]) * BLOCK

    @pl.when(step == 0)
    def _():
        for which in range(3):
            turned[which] = weights[which].T
        here = row_index((cells, cells))
        there = lax.broadcasted_iota(jnp.int32, (cells, cells), 1)
        source = (here % features) * BLOCK + here // features
        order[...] = jnp.where(source == there, 1.0, 0.0).astype(BF)
        source = (here % BLOCK) * features + here // BLOCK
        back_order[...] = jnp.where(source == there, 1.0, 0.0).astype(BF)
        total_attn[...] = jnp.zeros_like(total_attn)
        total_in[...] = jnp.zeros_like(total_in)
        total_out[...] = jnp.zeros_like(total_out)
        norm_total[...] = jnp.zeros_like(norm_total)

    x_one[...] = dot(order[...], x_in[:, 0].reshape(cells, width))
    for low in range(0, cells, ROWS):
        rows = slice(low, low + ROWS)
        normal, scale = normalize(x_one[rows])
        normal_one[rows] = normal
        scale_one[rows] = scale
        low_rows[rows] = (normal * norms[2:3] + norms[3:4]).astype(BF)
    for which in range(3):
        heads[which] = dot(turned[which], low_rows[...], NT).astype(BF)

    unit = (UNIT, UNIT)
    key_row = row_index(unit)
    query_row = lax.broadcasted_iota(jnp.int32, unit, 1)
    mask = (key_row // features == query_row // features) & (key_row % features < counts[1])
    for head in range(HEADS):
        lanes = slice(head * head_size, (head + 1) * head_size)
        for place in range(cells // UNIT):
            cols = slice(place * UNIT, (place + 1) * UNIT)
            scores = dot(heads[1, lanes, cols], heads[0, lanes, cols], TN) * score_scale
            scores = jnp.where(mask, scores, NEGATIVE)
            top = jnp.max(scores, axis=0, keepdims=True)
            powers = jnp.exp(scores - top)
            total = jnp.sum(powers, axis=0, keepdims=True)
            prob = powers * (1.0 / total)
            probs[head * (cells // UNIT) + place] = prob
            mixed[lanes, cols] = dot(heads[2, lanes, cols], prob.astype(BF)).astype(BF)
    for low in range(0, cells, ROWS):
        rows = slice(low, low + ROWS)
        part = x_one[rows] + dot(mixed[:, rows], weights[3], TN)
        x_two[rows] = part
        normal, scale = normalize(part)
        normal_two[rows] = normal
        scale_two[rows] = scale
        third[rows] = (normal * norms[4:5] + norms[5:6]).astype(BF)

    alive = first_sample < counts[0]

    @pl.when(jnp.logical_not(alive))
    def _():
        for low in range(0, hidden_width, width):
            cols = slice(low, low + width)
            hidden, _ = gelu_parts(dot(third[...], weight_in[:, cols]))
            x_two[...] += dot(hidden.astype(BF), weight_out[cols])
        d_out[...] = jnp.zeros_like(d_out)

    @pl.when(alive)
    def _():
        place = row_index((cells, 1))
        cell_live = (place % features < counts[1]) & (
            first_sample + place // features < counts[0]
        )
        grads = dot(order[...], cot_in[:, 0].reshape(cells, width))
        live_grad[...] = jnp.where(cell_live, grads, 0.0).astype(BF)
        for low in range(0, hidden_width, width):
            cols = slice(low, low + width)
            hidden, slope = gelu_parts(dot(third[...], weight_in[:, cols]))
            hidden = hidden.astype(BF)
            x_two[...] += dot(hidden, weight_out[cols])
            total_out[cols] += dot(hidden, live_grad[...], TN)
            d_pre = (dot(live_grad[...], weight_out[cols], NT) * slope).astype(BF)
            total_in[cols] += dot(d_pre, third[...], TN)
            d_third = dot(d_pre, weight_in[:, cols], NT)
            if low:
                grad_rows[...] += d_third
            else:
                grad_rows[...] = d_third
        for low in range(0, cells, ROWS):
            rows = slice(low, low + ROWS)
            normal = normal_two[rows]
            d_third = grad_rows[rows]
            norm_total[2:3] += column_sum(d_third * normal)
            norm_total[3:4] += column_sum(d_third)
            back = normalize_back(normal, scale_two[rows], d_third, norms[4:5])
            back = back + live_grad[rows].astype(F32)
            grad_rows[rows] = back
            live_grad[rows] = back.astype(BF)
        d_mix[...] = dot(weights[3], live_grad[...], NT).astype(BF)
        total_attn[3] += dot(mixed[...], live_grad[...])
        for head in range(HEADS):
            lanes = slice(head * head_size, (head + 1) * head_size)
            for place in range(cells // UNIT):
                cols = slice(place * UNIT, (place + 1) * UNIT)
                prob = probs[head * (cells // UNIT) + place]
                grads = d_mix[lanes, cols]
                shared = column_sum(grads.astype(F32) * mixed[lanes, cols].astype(F32))
                d_probs = dot(heads[2, lanes, cols], grads, TN)
                d_scores = (prob * (d_probs - shared)).astype(BF)
                d_query = dot(heads[1, lanes, cols], d_scores) * score_scale
                d_heads[0, lanes, cols] = d_query.astype(BF)
                d_key = dot(heads[0, lanes, cols], d_scores, NT) * score_scale
                d_heads[1, lanes, cols] = d_key.astype(BF)
                d_value = dot(grads, prob.astype(BF), NT)
                d_heads[2, lanes, cols] = d_value.astype(BF)
        for which in range(3):
            d_turned[which] = d_heads[which].T
        for which in range(3):
            total_attn[which] += dot(low_rows[...], d_turned[which], TN)
        for low in range(0, cells, ROWS):
            rows = slice(low, low + ROWS)
            d_second = dot(d_turned[0, rows], weights[0], NT)
            d_second = d_second + dot(d_turned[1, rows], weights[1], NT)
            d_second = d_second + dot(d_turned[2, rows], weights[2], NT)
            normal = normal_one[rows]
            norm_total[0:1] += column_sum(d_second * normal)
            norm_total[1:2] += column_sum(d_second)
            back = normalize_back(normal, scale_one[rows], d_second, norms[2:3])
            live_grad[rows] = (grad_rows[rows] + back).astype(BF)
        moved = dot(back_order[...], live_grad[...]).astype(BF)
        d_out[:, 0] = moved.reshape(devices, local, BLOCK, width)

    moved = dot(back_order[...], x_two[...].astype(BF)).astype(BF)
    y_out[:, 0] = moved.reshape(devices, local, BLOCK, width)

    @pl.when(step == pl.num_programs(0) - 1)
    def _():
        grad_in_out[...] = total_in[...].astype(BF)
        grad_out_out[...] = total_out[...].astype(BF)
        grad_attn_out[...] = total_attn[...].astype(BF)
        norm_out[...] = norm_total[...]


def whole(shape):
    zeros = (0,) * len(shape)
    return pl.BlockSpec(shape, lambda step: zeros, pipeline_mode=pl.Buffered(1))


def once(shape):
    zeros = (0,) * len(shape)
    return pl.BlockSpec(shape, lambda step: zeros)


def lead(shape):
    zeros = (0,) * (len(shape) - 1)
    return pl.BlockSpec((1,) + tuple(shape[1:]), lambda step: (step,) + zeros)


def call(body, grid, in_specs, outs, scratch, flops, name):
    return pl.pallas_call(
        body,
        grid=(grid,),
        in_specs=[pl.BlockSpec(memory_space=pltpu.SMEM)] + in_specs,
        out_specs=[spec for spec, _, _ in outs],
        out_shape=[jax.ShapeDtypeStruct(shape, kind) for _, shape, kind in outs],
        scratch_shapes=[pltpu.VMEM(shape, kind) for shape, kind in scratch],
        compiler_params=pltpu.CompilerParams(vmem_limit_bytes=VMEM_BYTES),
        cost_estimate=pl.CostEstimate(flops=flops, bytes_accessed=1 << 24, transcendentals=0),
        name=name,
    )


def run_sample_forward(counts, tokens, weights, norms, devices):
    local, samples, width = tokens.shape
    deals = samples // (devices * BLOCK)
    dealt = (devices, deals, local, BLOCK, width)
    square = (local, samples, width)
    three = (local, 3, width, samples)
    stats = (local, HEADS, samples)
    return call(
        sample_forward,
        local,
        [lead(square), whole((4, width, width)), whole(norms.shape)],
        [
            (
                pl.BlockSpec(
                    (devices, deals, 1, BLOCK, width), lambda step: (0, 0, step, 0, 0)
                ),
                dealt,
                BF,
            ),
            (lead(square), square, BF),
            (lead(three), three, BF),
            (lead(square), (local, width, samples), BF),
            (lead(stats), stats, F32),
        ],
        [((3, width, width), BF)],
        local * 8 * samples * width * (width + samples // 2),
        "sample_forward",
    )(counts, tokens, weights, norms)


def run_middle(counts, x_dealt, cot_dealt, weights, weight_in, weight_out, norms):
    devices, deals, local, _, width = x_dealt.shape
    cells = devices * local * BLOCK
    hidden_width = weight_in.shape[1]
    dealt = pl.BlockSpec(
        (devices, 1, local, BLOCK, width), lambda step: (0, step, 0, 0, 0)
    )
    square = (cells, width)
    turned = (width, cells)
    units = HEADS * (cells // UNIT)
    return call(
        middle,
        deals,
        [
            dealt,
            dealt,
            whole((4, width, width)),
            whole(weight_in.shape),
            whole(weight_out.shape),
            whole(norms.shape),
        ],
        [
            (dealt, x_dealt.shape, BF),
            (dealt, x_dealt.shape, BF),
            (once((hidden_width, width)), (hidden_width, width), BF),
            (once((hidden_width, width)), (hidden_width, width), BF),
            (once((4, width, width)), (4, width, width), BF),
            (once((4, width)), (4, width), F32),
        ],
        [
            ((3, width, width), BF),
            ((cells, cells), BF),
            ((cells, cells), BF),
            (square, F32),
            (square, F32),
            ((cells, 1), F32),
            (square, F32),
            ((cells, 1), F32),
            (square, F32),
            (square, BF),
            ((3,) + turned, BF),
            ((3,) + turned, BF),
            ((3,) + square, BF),
            (turned, BF),
            (turned, BF),
            ((units, UNIT, UNIT), F32),
            (square, BF),
            (square, BF),
            (square, F32),
            ((4, width, width), F32),
            ((hidden_width, width), F32),
            ((hidden_width, width), F32),
            ((4, width), F32),
        ],
        deals * cells * 6 * width * (4 * width + 2 * hidden_width),
        "middle",
    )(counts, x_dealt, cot_dealt, weights, weight_in, weight_out, norms)


def run_sample_backward(counts, d_dealt, tokens, first, heads, mixed, logs, weights, norms):
    devices, deals, local, _, width = d_dealt.shape
    samples = tokens.shape[1]
    square = (local, samples, width)
    three = (local, 3, width, samples)
    return call(
        sample_backward,
        local,
        [
            pl.BlockSpec((devices, deals, 1, BLOCK, width), lambda step: (0, 0, step, 0, 0)),
            lead(square),
            lead(square),
            lead(three),
            lead(mixed.shape),
            lead(logs.shape),
            whole((4, width, width)),
            whole(norms.shape),
        ],
        [
            (lead(square), square, BF),
            (once((4, width, width)), (4, width, width), BF),
            (once((2, width)), (2, width), F32),
        ],
        [
            ((samples, width), BF),
            ((width, samples), BF),
            ((3, width, samples), BF),
            ((3, samples, width), BF),
            ((4, width, width), F32),
            ((2, width), F32),
        ],
        local * 16 * samples * width * (width + samples),
        "sample_backward",
    )(counts, d_dealt, tokens, first, heads, mixed, logs, weights, norms)


def adam_step(weight, grad, first_m, second_m, rate):
    moment = BETA_ONE * first_m + (1.0 - BETA_ONE) * grad
    square = BETA_TWO * second_m + (1.0 - BETA_TWO) * grad * grad
    fix_one = 1.0 - BETA_ONE**STEP
    fix_two = 1.0 - BETA_TWO**STEP
    fresh = weight - rate * (
        moment / fix_one / (jnp.sqrt(square / fix_two) + ADAM_EPS) + DECAY * weight
    )
    return (fresh, moment, square)


def exchange(values, axis, groups=None):
    return lax.all_to_all(values, axis, 0, 0, axis_index_groups=groups, tiled=True)


def reduce_core(values):
    tasks = lax.axis_size("task")
    core = lax.axis_index("task") % 2
    pairs = [(place, place ^ 1) for place in range(tasks)]
    other = lax.dynamic_index_in_dim(values, 1 - core, 0, keepdims=False)
    mine = lax.dynamic_index_in_dim(values, core, 0, keepdims=False)
    came = lax.ppermute(other, "task", pairs)
    return (mine.astype(F32) + came.astype(F32)).astype(BF)


def reduce_feat(values):
    return jnp.sum(exchange(values, "feat").astype(F32), axis=0)


def reduce_chips(values):
    tasks = lax.axis_size("task")
    chips = tasks // 2
    chip = lax.axis_index("task") // 2
    if chips == 2:
        pairs = [(place, (place + 2) % tasks) for place in range(tasks)]
        other = lax.dynamic_index_in_dim(values, 1 - chip, 0, keepdims=False)
        mine = lax.dynamic_index_in_dim(values, chip, 0, keepdims=False)
        came = lax.ppermute(other, "task", pairs)
        return mine.astype(F32) + came.astype(F32)
    groups = [[2 * place + core for place in range(chips)] for core in range(2)]
    return jnp.sum(exchange(values, "task", groups).astype(F32), axis=0)


def total_of(values):
    count = lax.axis_size("task") * lax.axis_size("feat")
    copies = jnp.broadcast_to(values[None], (count,) + values.shape)
    return jnp.sum(exchange(copies, ("task", "feat")), axis=0)


def shards(
    tokens,
    cotangent,
    attn_weights,
    weight_in,
    weight_out,
    norm_params,
    master_attn,
    master_in,
    master_out,
    first_attn,
    first_in,
    first_out,
    first_norms,
    second_attn,
    second_in,
    second_out,
    second_norms,
    sample_count,
    feature_count,
):
    local, samples, width = tokens.shape[1:]
    devices = lax.axis_size("feat")
    tasks = lax.axis_size("task")
    chips = tasks // 2
    place = lax.axis_index("feat")
    deals = samples // (devices * BLOCK)
    counts = jnp.stack(
        [sample_count[0], feature_count[0], place * local, place]
    ).astype(jnp.int32)
    weights = attn_weights.reshape(8, width, width)
    weights_one, weights_two = weights[:4], weights[4:]

    dealt_cot = cotangent[0].reshape(local, deals, devices, BLOCK, width).transpose(2, 1, 0, 3, 4)
    came_cot = exchange(dealt_cot, "feat")
    dealt_x, first, heads, mixed, logs = run_sample_forward(
        counts, tokens[0], weights_one, norm_params, devices
    )
    came_x = exchange(dealt_x, "feat")
    dealt_y, dealt_d, grad_in, grad_out, grad_two, norms_two = run_middle(
        counts, came_x, came_cot, weights_two, weight_in, weight_out, norm_params
    )
    came_d = exchange(dealt_d, "feat")
    input_grad, grad_one, norms_one = run_sample_backward(
        counts, came_d, tokens[0], first, heads, mixed, logs, weights_one, norm_params
    )
    came_y = exchange(dealt_y, "feat")
    block_out = came_y.transpose(2, 1, 0, 3, 4).reshape(1, local, samples, width)

    own_ff = grad_in.shape[0] // (tasks * devices)
    both = jnp.concatenate(
        [
            grad_in.reshape(chips, 2, devices, own_ff, width),
            grad_out.reshape(chips, 2, devices, own_ff, width),
        ],
        axis=3,
    )
    both = reduce_core(jnp.moveaxis(both, 1, 0))
    both = reduce_chips(both).astype(BF)
    share_ff = reduce_feat(both)

    own_attn = attn_weights.shape[0] // (tasks * devices)
    halves = []
    for grad in (grad_one, grad_two):
        part = grad.reshape(chips // 2, 2, devices, own_attn, width)
        part = reduce_core(jnp.moveaxis(part, 1, 0))
        halves.append(reduce_feat(jnp.moveaxis(part, 1, 0)).astype(BF))
    share_attn = reduce_chips(jnp.concatenate(halves, axis=0))
    total_norms = total_of(jnp.concatenate([norms_one, norms_two], axis=0))

    share_in_turned, share_out = share_ff[:own_ff], share_ff[own_ff:]
    local_squares = jnp.sum(share_ff * share_ff) + jnp.sum(share_attn * share_attn)
    squares = total_of(jnp.full((8, 128), local_squares, F32))[0, 0]
    squares = squares + jnp.sum(total_norms * total_norms)
    grad_norm = jnp.sqrt(squares)
    factor = jnp.minimum(1.0, CLIP_AT / (grad_norm + 1e-06))
    new_attn, moment_attn, square_attn = adam_step(
        master_attn, factor * share_attn, first_attn, second_attn, RATE
    )
    new_in, moment_in, square_in = adam_step(
        master_in, factor * share_in_turned.T, first_in, second_in, RATE
    )
    new_out, moment_out, square_out = adam_step(
        master_out, factor * share_out, first_out, second_out, RATE
    )
    new_norms, moment_norms, square_norms = adam_step(
        norm_params, factor * total_norms, first_norms, second_norms, NORM_RATE
    )
    own = jnp.concatenate(
        [new_attn.astype(BF), new_in.astype(BF).T, new_out.astype(BF)], axis=0
    )
    copies = lax.all_gather(own, ("task", "feat"), axis=0, tiled=False)
    copy_attn = copies[:, :own_attn].reshape(-1, width)
    copy_in = copies[:, own_attn : own_attn + own_ff].reshape(-1, width).T
    copy_out = copies[:, own_attn + own_ff :].reshape(-1, width)
    return (
        block_out,
        input_grad[None],
        grad_norm.reshape(1),
        new_attn,
        new_in,
        new_out,
        new_norms,
        moment_attn,
        moment_in,
        moment_out,
        moment_norms,
        square_attn,
        square_in,
        square_out,
        square_norms,
        copy_attn,
        copy_in,
        copy_out,
    )


def solution(mesh):
    cells = P("task", "feat", None, None)
    rows = P(("task", "feat"), None)
    columns = P(None, ("task", "feat"))
    return jax.shard_map(
        shards,
        mesh=mesh,
        in_specs=(cells, cells, P(), P(), P(), P())
        + (rows, columns, rows)
        + (rows, columns, rows, P())
        + (rows, columns, rows, P())
        + (P("task"), P("task")),
        out_specs=(cells, cells, P())
        + (rows, columns, rows, P())
        + (rows, columns, rows, P())
        + (rows, columns, rows, P())
        + (P(), P(), P()),
        check_vma=False,
    )
```

```python
import functools

import jax
import jax.numpy as jnp
from jax import lax
from jax.experimental import pallas as pl
from jax.experimental.pallas import tpu as pltpu
from jax.sharding import PartitionSpec as P

HEADS = 8
STEP = 5
NEGATIVE = -1e30
LN_EPS = 1e-05
CLIP_AT = 1.0
BETA_ONE = 0.9
BETA_TWO = 0.999
RATE = 0.02
NORM_RATE = 0.25
DECAY = 0.1
ADAM_EPS = 1e-08

BLOCK = 16
UNIT = 128
ROWS = 128
QUERIES = 512
VMEM_BYTES = 60 * 1024 * 1024

BF = jnp.bfloat16
F32 = jnp.float32
NN = ((1,), (0,))
NT = ((1,), (1,))
TN = ((0,), (0,))


def dot(left, right, dims=NN):
    return lax.dot_general(left, right, (dims, ((), ())), preferred_element_type=F32)


def normalize(values):
    center = jnp.mean(values, axis=-1, keepdims=True)
    centred = values - center
    spread = jnp.mean(centred * centred, axis=-1, keepdims=True)
    scale = lax.rsqrt(spread + LN_EPS)
    return centred * scale, scale


def normalize_back(normal, scale, grad, gain):
    d_normal = grad * gain
    mean_one = jnp.mean(d_normal, axis=-1, keepdims=True)
    mean_two = jnp.mean(d_normal * normal, axis=-1, keepdims=True)
    return scale * (d_normal - mean_one - normal * mean_two)


def column_sum(values):
    return jnp.sum(values, axis=0, keepdims=True)


def by_unit(units, one):
    parts = [one(slice(place * UNIT, (place + 1) * UNIT)) for place in range(units)]
    return jnp.concatenate(parts, axis=1)


def scaled(values, head_size):
    return (values.astype(BF).astype(F32) * head_size ** (-0.5)).astype(BF)


def row_index(shape):
    return lax.broadcasted_iota(jnp.int32, shape, 0)


def sample_forward(
    counts, tokens, weights, norms, x_out, first_out, heads_out, mixed_out, log_out, turned
):
    samples, width = tokens.shape[1:]
    head_size = width // HEADS
    group = x_out.shape[0] * BLOCK

    @pl.when(pl.program_id(0) == 0)
    def _():
        for which in range(3):
            turned[which] = weights[which].T

    for low in range(0, samples, ROWS):
        rows = slice(low, low + ROWS)
        normal, _ = normalize(tokens[0, rows].astype(F32))
        first_out[0, rows] = (normal * norms[0:1] + norms[1:2]).astype(BF)
    first = first_out[0]
    heads_out[0, 0] = scaled(dot(turned[0], first, NT), head_size)
    for which in range(1, 3):
        heads_out[0, which] = dot(turned[which], first, NT).astype(BF)
    live = row_index((samples, 1)) < counts[0]
    for head in range(HEADS):
        lanes = slice(head * head_size, (head + 1) * head_size)
        keys = heads_out[0, 1, lanes]
        values = heads_out[0, 2, lanes]
        for low in range(0, samples, QUERIES):
            cols = slice(low, low + QUERIES)
            scores = dot(keys, heads_out[0, 0, lanes, cols], TN)
            scores = jnp.where(live, scores, NEGATIVE)
            top = jnp.max(scores, axis=0, keepdims=True)
            powers = jnp.exp(scores - top)
            total = jnp.sum(powers, axis=0, keepdims=True)
            mixed = dot(values, powers.astype(BF)) * (1.0 / total)
            mixed_out[0, lanes, cols] = mixed.astype(BF)
            log_out[0, head : head + 1, cols] = top + jnp.log(total)
    for low in range(0, samples, group):
        rows = slice(low, low + group)
        part = tokens[0, rows].astype(F32) + dot(mixed_out[0, :, rows], weights[3], TN)
        x_out[:, low // group, 0] = part.astype(BF).reshape(group // BLOCK, BLOCK, width)


def sample_backward(
    counts,
    d_x,
    tokens,
    first,
    heads,
    mixed,
    logs,
    weights,
    norms,
    grad_out,
    keep_out,
    send_out,
    norm_out,
    d_rows,
    d_mix,
    d_heads,
    d_turned,
    total,
    norm_total,
):
    samples, width = tokens.shape[1:]
    head_size = width // HEADS
    score_scale = head_size ** (-0.5)
    group = d_x.shape[0] * BLOCK
    step = pl.program_id(0)

    @pl.when(step == 0)
    def _():
        total[...] = jnp.zeros_like(total)
        norm_total[...] = jnp.zeros_like(norm_total)

    feature_live = counts[2] + step < counts[1]

    @pl.when(jnp.logical_not(feature_live))
    def _():
        grad_out[...] = jnp.zeros_like(grad_out)

    @pl.when(feature_live)
    def _():
        for low in range(0, samples, group):
            d_rows[low : low + group] = d_x[:, low // group, 0].reshape(group, width)
        d_mix[...] = dot(weights[3], d_rows[...], NT).astype(BF)
        total[3 * width :] += dot(mixed[0], d_rows[...])
        live = row_index((samples, 1)) < counts[0]
        for pair in range(0, HEADS, 2):
            d_keys, d_values = [], []
            for head in (pair, pair + 1):
                lanes = slice(head * head_size, (head + 1) * head_size)
                keys = heads[0, 1, lanes]
                values = heads[0, 2, lanes]
                queries = heads[0, 0, lanes]
                grads = d_mix[lanes]
                shared = column_sum(grads.astype(F32) * mixed[0, lanes].astype(F32))
                scores = dot(keys, queries, TN)
                scores = jnp.where(live, scores, NEGATIVE)
                probs = jnp.exp(scores - logs[0, head : head + 1])
                d_probs = dot(values, grads, TN)
                d_scores = (probs * (d_probs - shared)).astype(BF)
                d_heads[lanes] = (dot(keys, d_scores) * score_scale).astype(BF)
                d_keys.append(dot(d_scores, queries, NT).astype(BF))
                d_values.append(dot(probs.astype(BF), grads, NT).astype(BF))
            lanes = slice(pair * head_size, (pair + 2) * head_size)
            d_turned[1, :, lanes] = jnp.concatenate(d_keys, axis=1)
            d_turned[2, :, lanes] = jnp.concatenate(d_values, axis=1)
        d_turned[0] = d_heads[...].T
        for which in range(3):
            total[which * width : (which + 1) * width] += dot(first[0], d_turned[which], TN)
        for low in range(0, samples, ROWS):
            rows = slice(low, low + ROWS)
            d_first = dot(d_turned[0, rows], weights[0], NT)
            d_first = d_first + dot(d_turned[1, rows], weights[1], NT)
            d_first = d_first + dot(d_turned[2, rows], weights[2], NT)
            normal, scale = normalize(tokens[0, rows].astype(F32))
            norm_total[0:1] += column_sum(d_first * normal)
            norm_total[1:2] += column_sum(d_first)
            back = normalize_back(normal, scale, d_first, norms[0:1])
            grad_out[0, rows] = (d_rows[rows].astype(F32) + back).astype(BF)

    @pl.when(step == pl.num_programs(0) - 1)
    def _():
        attention_parts(keep_out, total, counts[4], 0)
        attention_parts(send_out, total, 1 - counts[4], 0)
        norm_out[...] = norm_total[...]


def gelu_parts(pre):
    root = 0.7978845608028654
    square = pre * pre
    curve = jnp.tanh(root * pre * (1.0 + 0.044715 * square))
    half = 0.5 * (1.0 + curve)
    slope = half + (0.5 * root) * pre * (1.0 - curve * curve) * (1.0 + 3 * 0.044715 * square)
    return pre * half, slope


def part_of(total, chip, core, owners, rows):
    start = pl.multiple_of((chip * 2 + core) * (owners * rows), owners * rows)
    part = total[pl.ds(start, owners * rows)].astype(BF)
    return part.reshape(owners, rows, part.shape[-1])


def attention_parts(where, total, core, low):
    chips, owners = where.shape[:2]
    half = total.shape[0] // (2 * chips * owners)
    for pair in range(chips // 2):
        part = part_of(total, pair, core, owners, 2 * half)
        for piece in range(2):
            rows = part[:, piece * half : (piece + 1) * half]
            where[2 * pair + piece, :, low : low + half] = rows


def middle(
    counts,
    x_in,
    cot_in,
    weights,
    weight_in,
    weight_out,
    norms,
    y_out,
    d_out,
    keep_out,
    send_out,
    norm_out,
    turned,
    order,
    back_order,
    x_one,
    normal_one,
    scale_one,
    normal_two,
    scale_two,
    x_two,
    low_rows,
    heads,
    d_heads,
    d_turned,
    mixed,
    d_mix,
    probs,
    live_grad,
    third,
    grad_rows,
    total_attn,
    total_in,
    total_out,
    norm_total,
):
    devices, _, local, _, width = x_in.shape
    features = devices * local
    cells = features * BLOCK
    head_size = width // HEADS
    score_scale = head_size ** (-0.5)
    hidden_width = weight_in.shape[1]
    step = pl.program_id(0)
    first_sample = (step * devices + counts[3]) * BLOCK

    @pl.when(step == 0)
    def _():
        for which in range(3):
            turned[which] = weights[which].T
        here = row_index((cells, cells))
        there = lax.broadcasted_iota(jnp.int32, (cells, cells), 1)
        source = (here % features) * BLOCK + here // features
        order[...] = jnp.where(source == there, 1.0, 0.0).astype(BF)
        source = (here % BLOCK) * features + here // BLOCK
        back_order[...] = jnp.where(source == there, 1.0, 0.0).astype(BF)
        total_attn[...] = jnp.zeros_like(total_attn)
        total_in[...] = jnp.zeros_like(total_in)
        total_out[...] = jnp.zeros_like(total_out)
        norm_total[...] = jnp.zeros_like(norm_total)

    x_one[...] = dot(order[...], x_in[:, 0].reshape(cells, width))
    for low in range(0, cells, ROWS):
        rows = slice(low, low + ROWS)
        normal, scale = normalize(x_one[rows])
        normal_one[rows] = normal
        scale_one[rows] = scale
        low_rows[rows] = (normal * norms[2:3] + norms[3:4]).astype(BF)
    heads[0] = scaled(dot(turned[0], low_rows[...], NT), head_size)
    for which in range(1, 3):
        heads[which] = dot(turned[which], low_rows[...], NT).astype(BF)

    units = cells // UNIT
    key_row = row_index((UNIT, cells))
    query_row = lax.broadcasted_iota(jnp.int32, (UNIT, cells), 1) % UNIT
    mask = (key_row // features == query_row // features) & (key_row % features < counts[1])
    for head in range(HEADS):
        lanes = slice(head * head_size, (head + 1) * head_size)
        scores = by_unit(units, lambda cols: dot(heads[1, lanes, cols], heads[0, lanes, cols], TN))
        scores = jnp.where(mask, scores, NEGATIVE)
        top = jnp.max(scores, axis=0, keepdims=True)
        powers = jnp.exp(scores - top)
        total = jnp.sum(powers, axis=0, keepdims=True)
        prob = powers * (1.0 / total)
        probs[head] = prob
        prob = prob.astype(BF)
        mixed[lanes] = by_unit(units, lambda cols: dot(heads[2, lanes, cols], prob[:, cols])).astype(BF)
    for low in range(0, cells, ROWS):
        rows = slice(low, low + ROWS)
        part = x_one[rows] + dot(mixed[:, rows], weights[3], TN)
        x_two[rows] = part
        normal, scale = normalize(part)
        normal_two[rows] = normal
        scale_two[rows] = scale
        third[rows] = (normal * norms[4:5] + norms[5:6]).astype(BF)

    alive = first_sample < counts[0]

    @pl.when(jnp.logical_not(alive))
    def _():
        for low in range(0, hidden_width, width):
            cols = slice(low, low + width)
            hidden, _ = gelu_parts(dot(third[...], weight_in[:, cols]))
            x_two[...] += dot(hidden.astype(BF), weight_out[cols])
        d_out[...] = jnp.zeros_like(d_out)

    @pl.when(alive)
    def _():
        place = row_index((cells, 1))
        cell_live = (place % features < counts[1]) & (
            first_sample + place // features < counts[0]
        )
        grads = dot(order[...], cot_in[:, 0].reshape(cells, width))
        live_grad[...] = jnp.where(cell_live, grads, 0.0).astype(BF)
        for low in range(0, hidden_width, width):
            cols = slice(low, low + width)
            hidden, slope = gelu_parts(dot(third[...], weight_in[:, cols]))
            hidden = hidden.astype(BF)
            x_two[...] += dot(hidden, weight_out[cols])
            total_out[cols] += dot(hidden, live_grad[...], TN)
            d_pre = (dot(live_grad[...], weight_out[cols], NT) * slope).astype(BF)
            total_in[cols] += dot(d_pre, third[...], TN)
            d_third = dot(d_pre, weight_in[:, cols], NT)
            if low:
                grad_rows[...] += d_third
            else:
                grad_rows[...] = d_third
        for low in range(0, cells, ROWS):
            rows = slice(low, low + ROWS)
            normal = normal_two[rows]
            d_third = grad_rows[rows]
            norm_total[2:3] += column_sum(d_third * normal)
            norm_total[3:4] += column_sum(d_third)
            back = normalize_back(normal, scale_two[rows], d_third, norms[4:5])
            back = back + live_grad[rows].astype(F32)
            grad_rows[rows] = back
            live_grad[rows] = back.astype(BF)
        d_mix[...] = dot(weights[3], live_grad[...], NT).astype(BF)
        total_attn[3 * width :] += dot(mixed[...], live_grad[...])
        for head in range(HEADS):
            lanes = slice(head * head_size, (head + 1) * head_size)
            prob = probs[head]
            grads = d_mix[lanes]
            shared = column_sum(grads.astype(F32) * mixed[lanes].astype(F32))
            d_probs = by_unit(units, lambda cols: dot(heads[2, lanes, cols], grads[:, cols], TN))
            d_scores = (prob * (d_probs - shared)).astype(BF)
            low_prob = prob.astype(BF)
            d_query = by_unit(units, lambda cols: dot(heads[1, lanes, cols], d_scores[:, cols]))
            d_heads[0, lanes] = (d_query * score_scale).astype(BF)
            d_key = by_unit(units, lambda cols: dot(heads[0, lanes, cols], d_scores[:, cols], NT))
            d_heads[1, lanes] = d_key.astype(BF)
            d_value = by_unit(units, lambda cols: dot(grads[:, cols], low_prob[:, cols], NT))
            d_heads[2, lanes] = d_value.astype(BF)
        for which in range(3):
            d_turned[which] = d_heads[which].T
        for which in range(3):
            total_attn[which * width : (which + 1) * width] += dot(low_rows[...], d_turned[which], TN)
        for low in range(0, cells, ROWS):
            rows = slice(low, low + ROWS)
            d_second = dot(d_turned[0, rows], weights[0], NT)
            d_second = d_second + dot(d_turned[1, rows], weights[1], NT)
            d_second = d_second + dot(d_turned[2, rows], weights[2], NT)
            normal = normal_one[rows]
            norm_total[0:1] += column_sum(d_second * normal)
            norm_total[1:2] += column_sum(d_second)
            back = normalize_back(normal, scale_one[rows], d_second, norms[2:3])
            live_grad[rows] = (grad_rows[rows] + back).astype(BF)
        moved = dot(back_order[...], live_grad[...]).astype(BF)
        d_out[:, 0] = moved.reshape(devices, local, BLOCK, width)

    moved = dot(back_order[...], x_two[...].astype(BF)).astype(BF)
    y_out[:, 0] = moved.reshape(devices, local, BLOCK, width)

    @pl.when(step == pl.num_programs(0) - 1)
    def _():
        chips, owners, rows, _ = keep_out.shape
        own_ff = hidden_width // (2 * chips * owners)
        for where, core in ((keep_out, counts[4]), (send_out, 1 - counts[4])):
            for chip in range(chips):
                for which, total in ((0, total_in), (1, total_out)):
                    part = part_of(total, chip, core, owners, own_ff)
                    where[chip, :, which * own_ff : (which + 1) * own_ff] = part
            attention_parts(where, total_attn, core, 2 * own_ff)
        norm_out[...] = norm_total[...]


def whole(shape):
    zeros = (0,) * len(shape)
    return pl.BlockSpec(shape, lambda step: zeros, pipeline_mode=pl.Buffered(1))


def half(shape, which):
    return pl.BlockSpec(
        (shape[0] // 2,) + tuple(shape[1:]),
        lambda step: (which, 0, 0),
        pipeline_mode=pl.Buffered(1),
    )


def once(shape):
    zeros = (0,) * len(shape)
    return pl.BlockSpec(shape, lambda step: zeros)


def lead(shape):
    zeros = (0,) * (len(shape) - 1)
    return pl.BlockSpec((1,) + tuple(shape[1:]), lambda step: (step,) + zeros)


def call(body, grid, in_specs, outs, scratch, nanoseconds, name):
    return pl.pallas_call(
        body,
        grid=(grid,),
        in_specs=[pl.BlockSpec(memory_space=pltpu.SMEM)] + in_specs,
        out_specs=[spec for spec, _, _ in outs],
        out_shape=[jax.ShapeDtypeStruct(shape, kind) for _, shape, kind in outs],
        scratch_shapes=[pltpu.VMEM(shape, kind) for shape, kind in scratch],
        compiler_params=pltpu.CompilerParams(vmem_limit_bytes=VMEM_BYTES),
        cost_estimate=pl.CostEstimate(
            flops=nanoseconds * 1150000, bytes_accessed=1 << 24, transcendentals=0
        ),
        name=name,
    )


def run_sample_forward(counts, tokens, weights, norms, devices):
    local, samples, width = tokens.shape
    deals = samples // (devices * BLOCK)
    dealt = (devices, deals, local, BLOCK, width)
    square = (local, samples, width)
    three = (local, 3, width, samples)
    stats = (local, HEADS, samples)
    return call(
        sample_forward,
        local,
        [lead(square), half(weights.shape, 0), whole(norms.shape)],
        [
            (
                pl.BlockSpec(
                    (devices, deals, 1, BLOCK, width), lambda step: (0, 0, step, 0, 0)
                ),
                dealt,
                BF,
            ),
            (lead(square), square, BF),
            (lead(three), three, BF),
            (lead(square), (local, width, samples), BF),
            (lead(stats), stats, F32),
        ],
        [((3, width, width), BF)],
        36000,
        "sample_forward",
    )(counts, tokens, weights, norms)


def run_middle(counts, x_dealt, cot_dealt, weights, weight_in, weight_out, norms, chips):
    devices, deals, local, _, width = x_dealt.shape
    cells = devices * local * BLOCK
    hidden_width = weight_in.shape[1]
    parts = (chips, devices, (hidden_width + 2 * width) // (chips * devices), width)
    dealt = pl.BlockSpec(
        (devices, 1, local, BLOCK, width), lambda step: (0, step, 0, 0, 0)
    )
    square = (cells, width)
    turned = (width, cells)
    return call(
        middle,
        deals,
        [
            dealt,
            dealt,
            half(weights.shape, 1),
            whole(weight_in.shape),
            whole(weight_out.shape),
            whole(norms.shape),
        ],
        [
            (dealt, x_dealt.shape, BF),
            (dealt, x_dealt.shape, BF),
            (once(parts), parts, BF),
            (once(parts), parts, BF),
            (once((4, width)), (4, width), F32),
        ],
        [
            ((3, width, width), BF),
            ((cells, cells), BF),
            ((cells, cells), BF),
            (square, F32),
            (square, F32),
            ((cells, 1), F32),
            (square, F32),
            ((cells, 1), F32),
            (square, F32),
            (square, BF),
            ((3,) + turned, BF),
            ((3,) + turned, BF),
            ((3,) + square, BF),
            (turned, BF),
            (turned, BF),
            ((HEADS, UNIT, cells), F32),
            (square, BF),
            (square, BF),
            (square, F32),
            ((4 * width, width), F32),
            ((hidden_width, width), F32),
            ((hidden_width, width), F32),
            ((4, width), F32),
        ],
        90000,
        "middle",
    )(counts, x_dealt, cot_dealt, weights, weight_in, weight_out, norms)


def run_sample_backward(
    counts, d_dealt, tokens, first, heads, mixed, logs, weights, norms, chips
):
    devices, deals, local, _, width = d_dealt.shape
    samples = tokens.shape[1]
    square = (local, samples, width)
    three = (local, 3, width, samples)
    parts = (chips, devices, 4 * width // (2 * chips * devices), width)
    return call(
        sample_backward,
        local,
        [
            pl.BlockSpec((devices, deals, 1, BLOCK, width), lambda step: (0, 0, step, 0, 0)),
            lead(square),
            lead(square),
            lead(three),
            lead(mixed.shape),
            lead(logs.shape),
            half(weights.shape, 0),
            whole(norms.shape),
        ],
        [
            (lead(square), square, BF),
            (once(parts), parts, BF),
            (once(parts), parts, BF),
            (once((2, width)), (2, width), F32),
        ],
        [
            ((samples, width), BF),
            ((width, samples), BF),
            ((width, samples), BF),
            ((3, samples, width), BF),
            ((4 * width, width), F32),
            ((2, width), F32),
        ],
        49000,
        "sample_backward",
    )(counts, d_dealt, tokens, first, heads, mixed, logs, weights, norms)


def adam_step(weight, grad, first_m, second_m, rate):
    moment = BETA_ONE * first_m + (1.0 - BETA_ONE) * grad
    square = BETA_TWO * second_m + (1.0 - BETA_TWO) * grad * grad
    fix_one = 1.0 - BETA_ONE**STEP
    fix_two = 1.0 - BETA_TWO**STEP
    fresh = weight - rate * (
        moment / fix_one / (jnp.sqrt(square / fix_two) + ADAM_EPS) + DECAY * weight
    )
    return (fresh, moment, square)


def exchange(values, axis, groups=None):
    return lax.all_to_all(values, axis, 0, 0, axis_index_groups=groups, tiled=True)


def task_pairs(hop):
    return [(place, hop(place)) for place in range(lax.axis_size("task"))]


def reduce_core(keep, send):
    came = lax.ppermute(send, "task", task_pairs(lambda place: place ^ 1))
    return (keep.astype(F32) + came.astype(F32)).astype(BF)


def reduce_chips(values):
    chips = values.shape[0]
    chip = lax.axis_index("task") // 2
    if chips == 2:
        mine = lax.dynamic_index_in_dim(values, chip, 0, keepdims=False)
        other = lax.dynamic_index_in_dim(values, 1 - chip, 0, keepdims=False)
        came = lax.ppermute(other, "task", task_pairs(lambda place: place ^ 2))
        return (mine.astype(F32) + came.astype(F32)).astype(BF)
    groups = [[2 * place + core for place in range(chips)] for core in range(2)]
    return jnp.sum(exchange(values, "task", groups).astype(F32), axis=0).astype(BF)


def reduce_feat(values):
    return jnp.sum(exchange(values, "feat").astype(F32), axis=0)


def to_owners(one, two):
    chips = lax.axis_size("task") // 2
    chip = lax.axis_index("task") // 2
    even = chip % 2 == 0
    stay, leave = jnp.where(even, one, two), jnp.where(even, two, one)

    def target(chip, second):
        return chip // 2 + (chips // 2 if second else 0)

    def send(values, odd_second):
        pairs = task_pairs(
            lambda place: 2 * target(place // 2, (place // 2 % 2 == 1) == odd_second) + place % 2
        )
        return lax.ppermute(values, "task", pairs)

    if chips > 2:
        stay = send(stay, True)
    leave = send(leave, False)
    early = chip < chips // 2
    return jnp.concatenate(
        [jnp.where(early, stay, leave), jnp.where(early, leave, stay)], axis=0
    )


def total_of(values):
    count = lax.axis_size("task") * lax.axis_size("feat")
    copies = jnp.broadcast_to(values[None], (count,) + values.shape)
    return jnp.sum(exchange(copies, ("task", "feat")), axis=0)


def shards(
    tokens,
    cotangent,
    attn_weights,
    weight_in,
    weight_out,
    norm_params,
    master_attn,
    master_in,
    master_out,
    first_attn,
    first_in,
    first_out,
    first_norms,
    second_attn,
    second_in,
    second_out,
    second_norms,
    sample_count,
    feature_count,
):
    local, samples, width = tokens.shape[1:]
    devices = lax.axis_size("feat")
    tasks = lax.axis_size("task")
    chips = tasks // 2
    place = lax.axis_index("feat")
    deals = samples // (devices * BLOCK)
    counts = jnp.stack(
        [sample_count[0], feature_count[0], place * local, place, lax.axis_index("task") % 2]
    ).astype(jnp.int32)
    weights = attn_weights.reshape(8, width, width)

    dealt_cot = cotangent[0].reshape(local, deals, devices, BLOCK, width).transpose(2, 1, 0, 3, 4)
    came_cot = exchange(dealt_cot, "feat")
    dealt_x, first, heads, mixed, logs = run_sample_forward(
        counts, tokens[0], weights, norm_params, devices
    )
    came_x = exchange(dealt_x, "feat")
    dealt_y, dealt_d, keep_two, send_two, norms_two = run_middle(
        counts, came_x, came_cot, weights, weight_in, weight_out, norm_params, chips
    )
    came_d = exchange(dealt_d, "feat")
    part_two = reduce_chips(reduce_core(keep_two, send_two))
    part_two, came_d = lax.optimization_barrier((part_two, came_d))
    own_ff = weight_in.shape[1] // (tasks * devices)
    own_attn = attn_weights.shape[0] // (tasks * devices)
    share_two = reduce_feat(part_two)
    input_grad, keep_one, send_one, norms_one = run_sample_backward(
        counts, came_d, tokens[0], first, heads, mixed, logs, weights, norm_params, chips
    )
    share_two, send_one = lax.optimization_barrier((share_two, send_one))
    share_one = reduce_feat(reduce_chips(reduce_core(keep_one, send_one)))
    came_y = exchange(dealt_y, "feat")
    block_out = came_y.transpose(2, 1, 0, 3, 4).reshape(1, local, samples, width)

    share_in_turned = share_two[:own_ff]
    share_out = share_two[own_ff : 2 * own_ff]
    share_attn = to_owners(share_one, share_two[2 * own_ff :])
    local_squares = jnp.sum(share_one * share_one) + jnp.sum(share_two * share_two)
    small = jnp.concatenate(
        [norms_one, norms_two, jnp.full((2, width), local_squares, F32)], axis=0
    )
    small = total_of(small)
    total_norms = small[:6]
    squares = small[6, 0] + jnp.sum(total_norms * total_norms)
    grad_norm = jnp.sqrt(squares)
    factor = jnp.minimum(1.0, CLIP_AT / (grad_norm + 1e-06))
    new_attn, moment_attn, square_attn = adam_step(
        master_attn, factor * share_attn, first_attn, second_attn, RATE
    )
    new_in, moment_in, square_in = adam_step(
        master_in, factor * share_in_turned.T, first_in, second_in, RATE
    )
    new_out, moment_out, square_out = adam_step(
        master_out, factor * share_out, first_out, second_out, RATE
    )
    new_norms, moment_norms, square_norms = adam_step(
        norm_params, factor * total_norms, first_norms, second_norms, NORM_RATE
    )
    own = jnp.concatenate(
        [new_attn.astype(BF), new_in.astype(BF).T, new_out.astype(BF)], axis=0
    )
    copies = lax.all_gather(own, ("task", "feat"), axis=0, tiled=False)
    copy_attn = copies[:, :own_attn].reshape(-1, width)
    copy_in = copies[:, own_attn : own_attn + own_ff].reshape(-1, width).T
    copy_out = copies[:, own_attn + own_ff :].reshape(-1, width)
    return (
        block_out,
        input_grad[None],
        grad_norm.reshape(1),
        new_attn,
        new_in,
        new_out,
        new_norms,
        moment_attn,
        moment_in,
        moment_out,
        moment_norms,
        square_attn,
        square_in,
        square_out,
        square_norms,
        copy_attn,
        copy_in,
        copy_out,
    )


def solution(mesh):
    cells = P("task", "feat", None, None)
    rows = P(("task", "feat"), None)
    columns = P(None, ("task", "feat"))
    return jax.shard_map(
        shards,
        mesh=mesh,
        in_specs=(cells, cells, P(), P(), P(), P())
        + (rows, columns, rows)
        + (rows, columns, rows, P())
        + (rows, columns, rows, P())
        + (P("task"), P("task")),
        out_specs=(cells, cells, P())
        + (rows, columns, rows, P())
        + (rows, columns, rows, P())
        + (rows, columns, rows, P())
        + (P(), P(), P()),
        check_vma=False,
    )
```

```python
import functools

import jax
import jax.numpy as jnp
from jax import lax
from jax.experimental import pallas as pl
from jax.experimental.pallas import tpu as pltpu
from jax.sharding import PartitionSpec as P

HEADS = 8
STEP = 5
NEGATIVE = -1e30
LN_EPS = 1e-05
CLIP_AT = 1.0
BETA_ONE = 0.9
BETA_TWO = 0.999
RATE = 0.02
NORM_RATE = 0.25
DECAY = 0.1
ADAM_EPS = 1e-08

BLOCK = 16
UNIT = 128
ROWS = 128
QUERIES = 512
UNROLL = 2
VMEM_BYTES = 60 * 1024 * 1024

BF = jnp.bfloat16
F32 = jnp.float32
NN = ((1,), (0,))
NT = ((1,), (1,))
TN = ((0,), (0,))


def dot(left, right, dims=NN):
    return lax.dot_general(left, right, (dims, ((), ())), preferred_element_type=F32)


def normalize(values):
    center = jnp.mean(values, axis=-1, keepdims=True)
    centred = values - center
    spread = jnp.mean(centred * centred, axis=-1, keepdims=True)
    scale = lax.rsqrt(spread + LN_EPS)
    return centred * scale, scale


def normalize_back(normal, scale, grad, gain):
    d_normal = grad * gain
    mean_one = jnp.mean(d_normal, axis=-1, keepdims=True)
    mean_two = jnp.mean(d_normal * normal, axis=-1, keepdims=True)
    return scale * (d_normal - mean_one - normal * mean_two)


def column_sum(values):
    return jnp.sum(values, axis=0, keepdims=True)


def by_unit(units, one):
    parts = [one(slice(place * UNIT, (place + 1) * UNIT)) for place in range(units)]
    return jnp.concatenate(parts, axis=1)


def scaled(values, head_size):
    return (values.astype(BF).astype(F32) * head_size ** (-0.5)).astype(BF)


def block_of(place, size):
    return pl.ds(pl.multiple_of(place * size, size), size)


def row_index(shape):
    return lax.broadcasted_iota(jnp.int32, shape, 0)


def sample_forward(late, counts, tokens, cotangent, weights, norms, x_out, *rest):
    if late:
        late_out, *rest = rest
    first_out, heads_out, mixed_out, log_out, turned = rest
    samples, width = tokens.shape[1:]
    head_size = width // HEADS
    early = x_out.shape[1]
    dealt = (x_out.shape[0], BLOCK, width)
    group = dealt[0] * BLOCK

    @pl.when(pl.program_id(0) == 0)
    def _():
        for which in range(3):
            turned[which] = weights[which].T

    for low in range(0, samples, ROWS):
        rows = slice(low, low + ROWS)
        normal, _ = normalize(tokens[0, rows].astype(F32))
        first_out[0, rows] = (normal * norms[0:1] + norms[1:2]).astype(BF)
    first = first_out[0]
    heads_out[0, 0] = scaled(dot(turned[0], first, NT), head_size)
    for which in range(1, 3):
        heads_out[0, which] = dot(turned[which], first, NT).astype(BF)
    live = row_index((samples, 1)) < counts[0]
    for head in range(HEADS):
        lanes = slice(head * head_size, (head + 1) * head_size)
        keys = heads_out[0, 1, lanes]
        values = heads_out[0, 2, lanes]
        for low in range(0, samples, QUERIES):
            cols = slice(low, low + QUERIES)
            scores = dot(keys, heads_out[0, 0, lanes, cols], TN)
            scores = jnp.where(live, scores, NEGATIVE)
            top = jnp.max(scores, axis=0, keepdims=True)
            powers = jnp.exp(scores - top)
            total = jnp.sum(powers, axis=0, keepdims=True)
            mixed = dot(values, powers.astype(BF)) * (1.0 / total)
            mixed_out[0, lanes, cols] = mixed.astype(BF)
            log_out[0, head : head + 1, cols] = top + jnp.log(total)
    for low in range(0, samples, group):
        rows = slice(low, low + group)
        part = tokens[0, rows].astype(F32) + dot(mixed_out[0, :, rows], weights[3], TN)
        part = part.astype(BF).reshape(dealt)
        if low // group < early:
            x_out[:, low // group, 0] = part
        else:
            late_out[:, 0, low // group - early, 0] = part
            late_out[:, 1, low // group - early, 0] = cotangent[0, rows].reshape(dealt)


def sample_backward(offset, early, opening, closing, counts, *refs):
    if early:
        d_early, *refs = refs
    d_late, tokens, first, heads, mixed, logs, weights, norms, *refs = refs
    if not opening:
        _, total_in, norm_total_in, *refs = refs
    grad_out, *refs = refs
    if closing:
        keep_out, send_out, norm_out, *refs = refs
    else:
        total_out, norm_out, *refs = refs
    d_rows, d_mix, d_heads, d_turned, total, norm_total = refs
    samples, width = tokens.shape[1:]
    head_size = width // HEADS
    score_scale = head_size ** (-0.5)
    group = d_late.shape[0] * BLOCK
    step = pl.program_id(0)

    @pl.when(step == 0)
    def _():
        if opening:
            total[...] = jnp.zeros_like(total)
            norm_total[...] = jnp.zeros_like(norm_total)
        else:
            total[...] = total_in[...]
            norm_total[...] = norm_total_in[...]

    feature_live = counts[2] + offset + step < counts[1]

    @pl.when(jnp.logical_not(feature_live))
    def _():
        grad_out[...] = jnp.zeros_like(grad_out)

    @pl.when(feature_live)
    def _():
        for low in range(0, samples, group):
            deal = low // group
            part = d_early[:, deal, 0] if deal < early else d_late[:, deal - early, 0]
            d_rows[low : low + group] = part.reshape(group, width)
        d_mix[...] = dot(weights[3], d_rows[...], NT).astype(BF)
        total[3 * width :] += dot(mixed[0], d_rows[...])
        live = row_index((samples, 1)) < counts[0]
        for pair in range(0, HEADS, 2):
            d_keys, d_values = [], []
            for head in (pair, pair + 1):
                lanes = slice(head * head_size, (head + 1) * head_size)
                keys = heads[0, 1, lanes]
                values = heads[0, 2, lanes]
                queries = heads[0, 0, lanes]
                grads = d_mix[lanes]
                shared = column_sum(grads.astype(F32) * mixed[0, lanes].astype(F32))
                scores = dot(keys, queries, TN)
                scores = jnp.where(live, scores, NEGATIVE)
                probs = jnp.exp(scores - logs[0, head : head + 1])
                d_probs = dot(values, grads, TN)
                d_scores = (probs * (d_probs - shared)).astype(BF)
                d_heads[lanes] = (dot(keys, d_scores) * score_scale).astype(BF)
                d_keys.append(dot(d_scores, queries, NT).astype(BF))
                d_values.append(dot(probs.astype(BF), grads, NT).astype(BF))
            lanes = slice(pair * head_size, (pair + 2) * head_size)
            d_turned[1, :, lanes] = jnp.concatenate(d_keys, axis=1)
            d_turned[2, :, lanes] = jnp.concatenate(d_values, axis=1)
        d_turned[0] = d_heads[...].T
        for which in range(3):
            total[which * width : (which + 1) * width] += dot(first[0], d_turned[which], TN)
        for low in range(0, samples, ROWS):
            rows = slice(low, low + ROWS)
            d_first = dot(d_turned[0, rows], weights[0], NT)
            d_first = d_first + dot(d_turned[1, rows], weights[1], NT)
            d_first = d_first + dot(d_turned[2, rows], weights[2], NT)
            normal, scale = normalize(tokens[0, rows].astype(F32))
            norm_total[0:1] += column_sum(d_first * normal)
            norm_total[1:2] += column_sum(d_first)
            back = normalize_back(normal, scale, d_first, norms[0:1])
            grad_out[0, rows] = (d_rows[rows].astype(F32) + back).astype(BF)

    @pl.when(step == pl.num_programs(0) - 1)
    def _():
        if closing:
            attention_parts(keep_out, total, counts[4], 0)
            attention_parts(send_out, total, 1 - counts[4], 0)
        else:
            total_out[...] = total[...]
        norm_out[...] = norm_total[...]


def gelu_parts(pre):
    root = 0.7978845608028654
    square = pre * pre
    curve = jnp.tanh(root * pre * (1.0 + 0.044715 * square))
    half = 0.5 * (1.0 + curve)
    slope = half + (0.5 * root) * pre * (1.0 - curve * curve) * (1.0 + 3 * 0.044715 * square)
    return pre * half, slope


def part_of(total, chip, core, owners, rows):
    start = pl.multiple_of((chip * 2 + core) * (owners * rows), owners * rows)
    part = total[pl.ds(start, owners * rows)].astype(BF)
    return part.reshape(owners, rows, part.shape[-1])


def attention_parts(where, total, core, low):
    chips, owners = where.shape[:2]
    half = total.shape[0] // (2 * chips * owners)
    for pair in range(chips // 2):
        part = part_of(total, pair, core, owners, 2 * half)
        for piece in range(2):
            rows = part[:, piece * half : (piece + 1) * half]
            where[2 * pair + piece, :, low : low + half] = rows


def middle(offset, opening, closing, groups, counts, *refs):
    refs = list(refs)

    def take(count):
        return [refs.pop(0) for _ in range(count)]

    x_in, cot_in, weights, weight_in, weight_out, norms = take(6)
    if not opening:
        held = take(3)
        (norm_held,) = take(1)
    if closing:
        d_outs = take(groups)
        y_out, keep_out, send_out, norm_out = take(4)
    else:
        (both_out,) = take(1)
        given = take(3)
        (norm_out,) = take(1)
    turned, order, back_order, x_one, normal_one, scale_one, normal_two, scale_two = take(8)
    x_two, low_rows, heads, d_heads, d_turned, mixed, d_mix, probs, live_grad = take(9)
    third, grad_rows, *totals, norm_total, copied = take(7)
    total_attn, total_in, total_out = totals
    if not opening:
        loads = [
            pltpu.make_async_copy(source, target, copied.at[place])
            for place, (source, target) in enumerate(zip(held, totals))
        ]
    devices, _, local, _, width = x_in.shape
    features = devices * local
    cells = features * BLOCK
    head_size = width // HEADS
    score_scale = head_size ** (-0.5)
    hidden_width = weight_in.shape[1]
    step = pl.program_id(0)
    first_sample = ((offset + step) * devices + counts[3]) * BLOCK

    @pl.when(step == 0)
    def _():
        if not opening:
            for load in loads:
                load.start()
        for which in range(3):
            turned[which] = weights[which].T
        here = row_index((cells, cells))
        there = lax.broadcasted_iota(jnp.int32, (cells, cells), 1)
        source = (here % features) * BLOCK + here // features
        order[...] = jnp.where(source == there, 1.0, 0.0).astype(BF)
        source = (here % BLOCK) * features + here // BLOCK
        back_order[...] = jnp.where(source == there, 1.0, 0.0).astype(BF)
        if opening:
            for total in totals:
                total[...] = jnp.zeros_like(total)
            norm_total[...] = jnp.zeros_like(norm_total)
        else:
            norm_total[...] = norm_held[...]

    x_one[...] = dot(order[...], x_in[:, 0].reshape(cells, width))
    for low in range(0, cells, ROWS):
        rows = slice(low, low + ROWS)
        normal, scale = normalize(x_one[rows])
        normal_one[rows] = normal
        scale_one[rows] = scale
        low_rows[rows] = (normal * norms[2:3] + norms[3:4]).astype(BF)
    heads[0] = scaled(dot(turned[0], low_rows[...], NT), head_size)
    for which in range(1, 3):
        heads[which] = dot(turned[which], low_rows[...], NT).astype(BF)

    units = cells // UNIT
    key_row = row_index((UNIT, cells))
    query_row = lax.broadcasted_iota(jnp.int32, (UNIT, cells), 1) % UNIT
    mask = (key_row // features == query_row // features) & (key_row % features < counts[1])
    for head in range(HEADS):
        lanes = slice(head * head_size, (head + 1) * head_size)
        scores = by_unit(units, lambda cols: dot(heads[1, lanes, cols], heads[0, lanes, cols], TN))
        scores = jnp.where(mask, scores, NEGATIVE)
        top = jnp.max(scores, axis=0, keepdims=True)
        powers = jnp.exp(scores - top)
        total = jnp.sum(powers, axis=0, keepdims=True)
        prob = powers * (1.0 / total)
        probs[head] = prob
        prob = prob.astype(BF)
        mixed[lanes] = by_unit(units, lambda cols: dot(heads[2, lanes, cols], prob[:, cols])).astype(BF)
    for low in range(0, cells, ROWS):
        rows = slice(low, low + ROWS)
        part = x_one[rows] + dot(mixed[:, rows], weights[3], TN)
        x_two[rows] = part
        normal, scale = normalize(part)
        normal_two[rows] = normal
        scale_two[rows] = scale
        third[rows] = (normal * norms[4:5] + norms[5:6]).astype(BF)

    if not opening:

        @pl.when(step == 0)
        def _():
            for load in loads:
                load.wait()

    def write_d(values):
        if not closing:
            both_out[:, 0, 0] = values
            return
        count = local // groups
        for place, d_out in enumerate(d_outs):
            d_out[:, 0] = values[:, place * count : (place + 1) * count]

    alive = first_sample < counts[0]

    @pl.when(jnp.logical_not(alive))
    def _():

        @pl.loop(0, hidden_width // width)
        def _(block):
            cols = block_of(block, width)
            hidden, _ = gelu_parts(dot(third[...], weight_in[:, cols]))
            x_two[...] += dot(hidden.astype(BF), weight_out[cols])

        write_d(jnp.zeros((devices, local, BLOCK, width), BF))

    @pl.when(alive)
    def _():
        place = row_index((cells, 1))
        cell_live = (place % features < counts[1]) & (
            first_sample + place // features < counts[0]
        )
        grads = dot(order[...], cot_in[:, 0].reshape(cells, width))
        live_grad[...] = jnp.where(cell_live, grads, 0.0).astype(BF)
        grad_rows[...] = jnp.zeros_like(grad_rows)

        @pl.loop(0, hidden_width // width)
        def _(block):
            cols = block_of(block, width)
            hidden, slope = gelu_parts(dot(third[...], weight_in[:, cols]))
            hidden = hidden.astype(BF)
            x_two[...] += dot(hidden, weight_out[cols])
            total_out[cols] += dot(hidden, live_grad[...], TN)
            d_pre = (dot(live_grad[...], weight_out[cols], NT) * slope).astype(BF)
            total_in[cols] += dot(d_pre, third[...], TN)
            grad_rows[...] += dot(d_pre, weight_in[:, cols], NT)


        for low in range(0, cells, ROWS):
            rows = slice(low, low + ROWS)
            normal = normal_two[rows]
            d_third = grad_rows[rows]
            norm_total[2:3] += column_sum(d_third * normal)
            norm_total[3:4] += column_sum(d_third)
            back = normalize_back(normal, scale_two[rows], d_third, norms[4:5])
            back = back + live_grad[rows].astype(F32)
            grad_rows[rows] = back
            live_grad[rows] = back.astype(BF)
        d_mix[...] = dot(weights[3], live_grad[...], NT).astype(BF)
        total_attn[3 * width :] += dot(mixed[...], live_grad[...])
        for head in range(HEADS):
            lanes = slice(head * head_size, (head + 1) * head_size)
            prob = probs[head]
            grads = d_mix[lanes]
            shared = column_sum(grads.astype(F32) * mixed[lanes].astype(F32))
            d_probs = by_unit(units, lambda cols: dot(heads[2, lanes, cols], grads[:, cols], TN))
            d_scores = (prob * (d_probs - shared)).astype(BF)
            low_prob = prob.astype(BF)
            d_query = by_unit(units, lambda cols: dot(heads[1, lanes, cols], d_scores[:, cols]))
            d_heads[0, lanes] = (d_query * score_scale).astype(BF)
            d_key = by_unit(units, lambda cols: dot(heads[0, lanes, cols], d_scores[:, cols], NT))
            d_heads[1, lanes] = d_key.astype(BF)
            d_value = by_unit(units, lambda cols: dot(grads[:, cols], low_prob[:, cols], NT))
            d_heads[2, lanes] = d_value.astype(BF)
        for which in range(3):
            d_turned[which] = d_heads[which].T
        for which in range(3):
            total_attn[which * width : (which + 1) * width] += dot(low_rows[...], d_turned[which], TN)
        for low in range(0, cells, ROWS):
            rows = slice(low, low + ROWS)
            d_second = dot(d_turned[0, rows], weights[0], NT)
            d_second = d_second + dot(d_turned[1, rows], weights[1], NT)
            d_second = d_second + dot(d_turned[2, rows], weights[2], NT)
            normal = normal_one[rows]
            norm_total[0:1] += column_sum(d_second * normal)
            norm_total[1:2] += column_sum(d_second)
            back = normalize_back(normal, scale_one[rows], d_second, norms[2:3])
            live_grad[rows] = (grad_rows[rows] + back).astype(BF)
        moved = dot(back_order[...], live_grad[...]).astype(BF)
        write_d(moved.reshape(devices, local, BLOCK, width))

    moved = dot(back_order[...], x_two[...].astype(BF)).astype(BF)
    moved = moved.reshape(devices, local, BLOCK, width)
    if closing:
        y_out[:, 0] = moved
    else:
        both_out[:, 1, 0] = moved

    @pl.when(step == pl.num_programs(0) - 1)
    def _():
        if closing:
            chips, owners, rows, _ = keep_out.shape
            own_ff = hidden_width // (2 * chips * owners)
            for where, core in ((keep_out, counts[4]), (send_out, 1 - counts[4])):
                for chip in range(chips):
                    for which, total in ((0, total_in), (1, total_out)):
                        part = part_of(total, chip, core, owners, own_ff)
                        where[chip, :, which * own_ff : (which + 1) * own_ff] = part
                attention_parts(where, total_attn, core, 2 * own_ff)
        else:
            stores = [
                pltpu.make_async_copy(source, target, copied.at[place])
                for place, (source, target) in enumerate(zip(totals, given))
            ]
            for store in stores:
                store.start()
            for store in stores:
                store.wait()
        norm_out[...] = norm_total[...]


def whole(shape):
    zeros = (0,) * len(shape)
    return pl.BlockSpec(shape, lambda step: zeros, pipeline_mode=pl.Buffered(1))


def half(shape, which):
    return pl.BlockSpec(
        (shape[0] // 2,) + tuple(shape[1:]),
        lambda step: (which, 0, 0),
        pipeline_mode=pl.Buffered(1),
    )


def once(shape):
    zeros = (0,) * len(shape)
    return pl.BlockSpec(shape, lambda step: zeros)


def lead(shape):
    zeros = (0,) * (len(shape) - 1)
    return pl.BlockSpec((1,) + tuple(shape[1:]), lambda step: (step,) + zeros)


def call(body, grid, ins, outs, scratch, nanoseconds, name, aliases=None):
    return pl.pallas_call(
        body,
        grid=(grid,),
        in_specs=[pl.BlockSpec(memory_space=pltpu.SMEM)] + [spec for spec, _ in ins[1:]],
        out_specs=[spec for spec, _, _ in outs],
        out_shape=[jax.ShapeDtypeStruct(shape, kind) for _, shape, kind in outs],
        scratch_shapes=[
            pltpu.SemaphoreType.DMA((3,)) if kind is None else pltpu.VMEM(shape, kind)
            for shape, kind in scratch
        ],
        input_output_aliases=aliases or {},
        compiler_params=pltpu.CompilerParams(vmem_limit_bytes=VMEM_BYTES),
        cost_estimate=pl.CostEstimate(
            flops=nanoseconds * 1150000, bytes_accessed=1 << 24, transcendentals=0
        ),
        name=name,
    )(ins[0][1], *[value for _, value in ins[1:]])


ANYWHERE = pl.BlockSpec(memory_space=pl.ANY)


def run_sample_forward(counts, tokens, cotangent, weights, norms, devices, early):
    local, samples, width = tokens.shape
    late = samples // (devices * BLOCK) - early
    square = (local, samples, width)
    three = (local, 3, width, samples)
    stats = (local, HEADS, samples)
    outs = [
        (
            pl.BlockSpec((devices, early, 1, BLOCK, width), lambda step: (0, 0, step, 0, 0)),
            (devices, early, local, BLOCK, width),
            BF,
        )
    ]
    if late:
        outs.append(
            (
                pl.BlockSpec(
                    (devices, 2, late, 1, BLOCK, width), lambda step: (0, 0, 0, step, 0, 0)
                ),
                (devices, 2, late, local, BLOCK, width),
                BF,
            )
        )
    outs = outs + [
        (lead(square), square, BF),
        (lead(three), three, BF),
        (lead(square), (local, width, samples), BF),
        (lead(stats), stats, F32),
    ]
    return call(
        functools.partial(sample_forward, late),
        local,
        [
            (None, counts),
            (lead(square), tokens),
            (lead(square), cotangent),
            (half(weights.shape, 0), weights),
            (whole(norms.shape), norms),
        ],
        outs,
        [((3, width, width), BF)],
        25000,
        "sample_forward",
    )


def run_middle(counts, x_dealt, cot_dealt, weights, weight_in, weight_out, norms, chips, offset, held, groups):
    array, which = x_dealt
    devices = array.shape[0]
    deals, local, _, width = array.shape[-4:]
    cells = devices * local * BLOCK
    hidden_width = weight_in.shape[1]
    parts = (chips, devices, (hidden_width + 2 * width) // (chips * devices), width)

    def dealt(which):
        if which is None:
            return pl.BlockSpec(
                (devices, 1, local, BLOCK, width), lambda step: (0, step, 0, 0, 0)
            )
        return pl.BlockSpec(
            (devices, None, 1, local, BLOCK, width),
            lambda step: (0, which, step, 0, 0, 0),
        )

    ins = [
        (None, counts),
        (dealt(x_dealt[1]), x_dealt[0]),
        (dealt(cot_dealt[1]), cot_dealt[0]),
        (half(weights.shape, 1), weights),
        (whole(weight_in.shape), weight_in),
        (whole(weight_out.shape), weight_out),
        (whole(norms.shape), norms),
    ]
    sums = [(4 * width, width), (hidden_width, width), (hidden_width, width)]
    norm_sums = (4, width)
    if held is not None:
        ins = ins + [(ANYWHERE, value) for value in held[:3]] + [(whole(norm_sums), held[3])]
    if groups:
        few = (devices, deals, local // groups, BLOCK, width)
        piece = pl.BlockSpec((devices, 1) + few[2:], lambda step: (0, step, 0, 0, 0))
        outs = [(piece, few, BF)] * groups + [
            (dealt(None), (devices, deals, local, BLOCK, width), BF),
            (once(parts), parts, BF),
            (once(parts), parts, BF),
        ]
    else:
        outs = [
            (
                pl.BlockSpec(
                    (devices, 2, 1, local, BLOCK, width), lambda step: (0, 0, step, 0, 0, 0)
                ),
                (devices, 2, deals, local, BLOCK, width),
                BF,
            )
        ] + [(ANYWHERE, shape, F32) for shape in sums]
    outs.append((once(norm_sums), norm_sums, F32))
    square = (cells, width)
    turned = (width, cells)
    return call(
        functools.partial(middle, offset, held is None, bool(groups), groups),
        deals,
        ins,
        outs,
        [
            ((3, width, width), BF),
            ((cells, cells), BF),
            ((cells, cells), BF),
            (square, F32),
            (square, F32),
            ((cells, 1), F32),
            (square, F32),
            ((cells, 1), F32),
            (square, F32),
            (square, BF),
            ((3,) + turned, BF),
            ((3,) + turned, BF),
            ((3,) + square, BF),
            (turned, BF),
            (turned, BF),
            ((HEADS, UNIT, cells), F32),
            (square, BF),
            (square, BF),
            (square, F32),
        ]
        + [(shape, F32) for shape in sums]
        + [(norm_sums, F32), ((3,), None)],
        deals * 23000,
        "middle",
    )


def run_sample_backward(counts, d_early, d_late, saved, weights, norms, chips, offset, held, closing):
    devices, late, count, _, width = d_late.shape
    tokens = saved[0]
    local, samples, _ = tokens.shape
    early = 0 if d_early is None else d_early.shape[2]
    parts = (chips, devices, 4 * width // (2 * chips * devices), width)

    def moved(shape):
        zeros = (0,) * (len(shape) - 1)
        return pl.BlockSpec((1,) + tuple(shape[1:]), lambda step: (step + offset,) + zeros)

    ins = [(None, counts)]
    if early:
        ins.append(
            (
                pl.BlockSpec(
                    (devices, None, early, 1, BLOCK, width),
                    lambda step: (0, 0, 0, step + offset, 0, 0),
                ),
                d_early,
            )
        )
    ins.append(
        (
            pl.BlockSpec((devices, late, 1, BLOCK, width), lambda step: (0, 0, step, 0, 0)),
            d_late,
        )
    )
    ins = ins + [(moved(value.shape), value) for value in saved]
    ins = ins + [(half(weights.shape, 0), weights), (whole(norms.shape), norms)]
    sums, norm_sums = (4 * width, width), (2, width)
    aliases = {}
    if held is not None:
        aliases = {len(ins): 0}
        ins = ins + [(ANYWHERE, held[0]), (whole(sums), held[1]), (whole(norm_sums), held[2])]
    outs = [(moved(tokens.shape), tokens.shape, BF)]
    if closing:
        outs = outs + [(once(parts), parts, BF), (once(parts), parts, BF)]
    else:
        outs = outs + [(once(sums), sums, F32)]
    outs.append((once(norm_sums), norm_sums, F32))
    return call(
        functools.partial(sample_backward, offset, early, held is None, closing),
        count,
        ins,
        outs,
        [
            ((samples, width), BF),
            ((width, samples), BF),
            ((width, samples), BF),
            ((3, samples, width), BF),
            (sums, F32),
            (norm_sums, F32),
        ],
        count * 11000,
        "sample_backward",
        aliases,
    )


def adam_step(weight, grad, first_m, second_m, rate):
    moment = BETA_ONE * first_m + (1.0 - BETA_ONE) * grad
    square = BETA_TWO * second_m + (1.0 - BETA_TWO) * grad * grad
    fix_one = 1.0 - BETA_ONE**STEP
    fix_two = 1.0 - BETA_TWO**STEP
    fresh = weight - rate * (
        moment / fix_one / (jnp.sqrt(square / fix_two) + ADAM_EPS) + DECAY * weight
    )
    return (fresh, moment, square)


def exchange(values, axis, groups=None):
    return lax.all_to_all(values, axis, 0, 0, axis_index_groups=groups, tiled=True)


def task_pairs(hop):
    return [(place, hop(place)) for place in range(lax.axis_size("task"))]


def reduce_core(keep, send):
    came = lax.ppermute(send, "task", task_pairs(lambda place: place ^ 1))
    return (keep.astype(F32) + came.astype(F32)).astype(BF)


def reduce_chips(values):
    chips = values.shape[0]
    chip = lax.axis_index("task") // 2
    if chips == 2:
        mine = lax.dynamic_index_in_dim(values, chip, 0, keepdims=False)
        other = lax.dynamic_index_in_dim(values, 1 - chip, 0, keepdims=False)
        came = lax.ppermute(other, "task", task_pairs(lambda place: place ^ 2))
        return (mine.astype(F32) + came.astype(F32)).astype(BF)
    groups = [[2 * place + core for place in range(chips)] for core in range(2)]
    return jnp.sum(exchange(values, "task", groups).astype(F32), axis=0).astype(BF)


def reduce_feat(values):
    return jnp.sum(exchange(values, "feat").astype(F32), axis=0)


def to_owners(one, two):
    chips = lax.axis_size("task") // 2
    chip = lax.axis_index("task") // 2
    even = chip % 2 == 0
    stay, leave = jnp.where(even, one, two), jnp.where(even, two, one)

    def target(chip, second):
        return chip // 2 + (chips // 2 if second else 0)

    def send(values, odd_second):
        pairs = task_pairs(
            lambda place: 2 * target(place // 2, (place // 2 % 2 == 1) == odd_second) + place % 2
        )
        return lax.ppermute(values, "task", pairs)

    if chips > 2:
        stay = send(stay, True)
    leave = send(leave, False)
    early = chip < chips // 2
    return jnp.concatenate(
        [jnp.where(early, stay, leave), jnp.where(early, leave, stay)], axis=0
    )


def total_of(values):
    count = lax.axis_size("task") * lax.axis_size("feat")
    copies = jnp.broadcast_to(values[None], (count,) + values.shape)
    return jnp.sum(exchange(copies, ("task", "feat")), axis=0)


def shards(
    tokens,
    cotangent,
    attn_weights,
    weight_in,
    weight_out,
    norm_params,
    master_attn,
    master_in,
    master_out,
    first_attn,
    first_in,
    first_out,
    first_norms,
    second_attn,
    second_in,
    second_out,
    second_norms,
    sample_count,
    feature_count,
):
    local, samples, width = tokens.shape[1:]
    devices = lax.axis_size("feat")
    tasks = lax.axis_size("task")
    chips = tasks // 2
    place = lax.axis_index("feat")
    deals = samples // (devices * BLOCK)
    counts = jnp.stack(
        [sample_count[0], feature_count[0], place * local, place, lax.axis_index("task") % 2]
    ).astype(jnp.int32)
    weights = attn_weights.reshape(8, width, width)

    early = max(deals // 2, 1)
    late = deals - early
    groups = 2 if late and local % 2 == 0 else 1
    own_ff = weight_in.shape[1] // (tasks * devices)
    own_attn = attn_weights.shape[0] // (tasks * devices)

    def dealt(values):
        count = values.shape[1] // (devices * BLOCK)
        values = values.reshape(local, count, devices, BLOCK, width)
        return values.transpose(2, 1, 0, 3, 4)

    came_cot = exchange(dealt(cotangent[0, :, : early * devices * BLOCK]), "feat")
    dealt_x, *rest = run_sample_forward(
        counts, tokens[0], cotangent[0], weights, norm_params, devices, early
    )
    came_cot, dealt_x, *rest = lax.optimization_barrier((came_cot, dealt_x, *rest))
    saved = [tokens[0]] + rest[-4:]
    came_x = exchange(dealt_x, "feat")
    shared = (weights, weight_in, weight_out, norm_params, chips)
    came_both = None
    if late:
        dealt_late, came_x = lax.optimization_barrier((rest[0], came_x))
        came_late = exchange(dealt_late, "feat")
        dealt_both, *held = run_middle(
            counts, (came_x, None), (came_cot, None), *shared, 0, None, 0
        )
        *dealt_d, dealt_y, keep_two, send_two, norms_two = run_middle(
            counts, (came_late, 0), (came_late, 1), *shared, early, held, groups
        )
        came_both = exchange(dealt_both, "feat")
        came_both, dealt_d, dealt_y, keep_two, send_two, norms_two = lax.optimization_barrier(
            (came_both, dealt_d, dealt_y, keep_two, send_two, norms_two)
        )
    else:
        *dealt_d, dealt_y, keep_two, send_two, norms_two = run_middle(
            counts, (came_x, None), (came_cot, None), *shared, 0, None, groups
        )
    part_two = reduce_chips(reduce_core(keep_two, send_two))
    came_d = exchange(dealt_d[0], "feat")
    if groups == 2:
        dealt_d[1], came_d = lax.optimization_barrier((dealt_d[1], came_d))
        came_last = exchange(dealt_d[1], "feat")
        held = run_sample_backward(
            counts, came_both, came_d, saved, weights, norm_params, chips, 0, None, False
        )
        came_d, held = lax.optimization_barrier((came_last, held))
    else:
        held = None
    part_two, came_d = lax.optimization_barrier((part_two, came_d))
    share_two = reduce_feat(part_two)
    input_grad, keep_one, send_one, norms_one = run_sample_backward(
        counts,
        came_both,
        came_d,
        saved,
        weights,
        norm_params,
        chips,
        0 if held is None else local // 2,
        held,
        True,
    )
    share_two, input_grad, keep_one, send_one, norms_one = lax.optimization_barrier(
        (share_two, input_grad, keep_one, send_one, norms_one)
    )
    share_one = reduce_feat(reduce_chips(reduce_core(keep_one, send_one)))
    came_y = exchange(dealt_y, "feat")
    if late:
        came_y = jnp.concatenate([came_both[:, 1], came_y], axis=1)
    block_out = came_y.transpose(2, 1, 0, 3, 4).reshape(1, local, samples, width)

    share_in_turned = share_two[:own_ff]
    share_out = share_two[own_ff : 2 * own_ff]
    share_attn = to_owners(share_one, share_two[2 * own_ff :])
    local_squares = jnp.sum(share_one * share_one) + jnp.sum(share_two * share_two)
    small = jnp.concatenate(
        [norms_one, norms_two, jnp.full((2, width), local_squares, F32)], axis=0
    )
    small = total_of(small)
    total_norms = small[:6]
    squares = small[6, 0] + jnp.sum(total_norms * total_norms)
    grad_norm = jnp.sqrt(squares)
    factor = jnp.minimum(1.0, CLIP_AT / (grad_norm + 1e-06))
    new_attn, moment_attn, square_attn = adam_step(
        master_attn, factor * share_attn, first_attn, second_attn, RATE
    )
    new_in, moment_in, square_in = adam_step(
        master_in, factor * share_in_turned.T, first_in, second_in, RATE
    )
    new_out, moment_out, square_out = adam_step(
        master_out, factor * share_out, first_out, second_out, RATE
    )
    new_norms, moment_norms, square_norms = adam_step(
        norm_params, factor * total_norms, first_norms, second_norms, NORM_RATE
    )
    own = jnp.concatenate(
        [new_attn.astype(BF), new_in.astype(BF).T, new_out.astype(BF)], axis=0
    )
    copies = lax.all_gather(own, ("task", "feat"), axis=0, tiled=False)
    copy_attn = copies[:, :own_attn].reshape(-1, width)
    copy_in = copies[:, own_attn : own_attn + own_ff].reshape(-1, width).T
    copy_out = copies[:, own_attn + own_ff :].reshape(-1, width)
    return (
        block_out,
        input_grad[None],
        grad_norm.reshape(1),
        new_attn,
        new_in,
        new_out,
        new_norms,
        moment_attn,
        moment_in,
        moment_out,
        moment_norms,
        square_attn,
        square_in,
        square_out,
        square_norms,
        copy_attn,
        copy_in,
        copy_out,
    )


def solution(mesh):
    cells = P("task", "feat", None, None)
    rows = P(("task", "feat"), None)
    columns = P(None, ("task", "feat"))
    return jax.shard_map(
        shards,
        mesh=mesh,
        in_specs=(cells, cells, P(), P(), P(), P())
        + (rows, columns, rows)
        + (rows, columns, rows, P())
        + (rows, columns, rows, P())
        + (P("task"), P("task")),
        out_specs=(cells, cells, P())
        + (rows, columns, rows, P())
        + (rows, columns, rows, P())
        + (rows, columns, rows, P())
        + (P(), P(), P()),
        check_vma=False,
    )
```

```python
import functools

import jax
import jax.numpy as jnp
from jax import lax
from jax.experimental import pallas as pl
from jax.experimental.pallas import tpu as pltpu
from jax.sharding import PartitionSpec as P

HEADS = 8
STEP = 5
NEGATIVE = -1e30
LN_EPS = 1e-05
CLIP_AT = 1.0
BETA_ONE = 0.9
BETA_TWO = 0.999
RATE = 0.02
NORM_RATE = 0.25
DECAY = 0.1
ADAM_EPS = 1e-08

BLOCK = 16
UNIT = 128
ROWS = 128
QUERIES = 512
UNROLL = 2
VMEM_BYTES = 60 * 1024 * 1024

BF = jnp.bfloat16
F32 = jnp.float32
NN = ((1,), (0,))
NT = ((1,), (1,))
TN = ((0,), (0,))


def dot(left, right, dims=NN):
    return lax.dot_general(left, right, (dims, ((), ())), preferred_element_type=F32)


def normalize(values):
    center = jnp.mean(values, axis=-1, keepdims=True)
    centred = values - center
    spread = jnp.mean(centred * centred, axis=-1, keepdims=True)
    scale = lax.rsqrt(spread + LN_EPS)
    return centred * scale, scale


def normalize_back(normal, scale, grad, gain):
    d_normal = grad * gain
    mean_one = jnp.mean(d_normal, axis=-1, keepdims=True)
    mean_two = jnp.mean(d_normal * normal, axis=-1, keepdims=True)
    return scale * (d_normal - mean_one - normal * mean_two)


def column_sum(values):
    return jnp.sum(values, axis=0, keepdims=True)


def by_unit(units, one):
    parts = [one(slice(place * UNIT, (place + 1) * UNIT)) for place in range(units)]
    return jnp.concatenate(parts, axis=1)


def scaled(values, head_size):
    return (values.astype(BF).astype(F32) * head_size ** (-0.5)).astype(BF)


def block_of(place, size):
    return pl.ds(pl.multiple_of(place * size, size), size)


def row_index(shape):
    return lax.broadcasted_iota(jnp.int32, shape, 0)


def sample_forward(late, counts, tokens, cotangent, weights, norms, x_out, *rest):
    if late:
        late_out, *rest = rest
    first_out, heads_out, mixed_out, log_out, turned = rest
    samples, width = tokens.shape[1:]
    head_size = width // HEADS
    early = x_out.shape[1]
    dealt = (x_out.shape[0], BLOCK, width)
    group = dealt[0] * BLOCK

    @pl.when(pl.program_id(0) == 0)
    def _():
        for which in range(3):
            turned[which] = weights[which].T

    for low in range(0, samples, ROWS):
        rows = slice(low, low + ROWS)
        normal, _ = normalize(tokens[0, rows].astype(F32))
        first_out[0, rows] = (normal * norms[0:1] + norms[1:2]).astype(BF)
    first = first_out[0]
    heads_out[0, 0] = scaled(dot(turned[0], first, NT), head_size)
    for which in range(1, 3):
        heads_out[0, which] = dot(turned[which], first, NT).astype(BF)
    live = row_index((samples, 1)) < counts[0]
    for head in range(HEADS):
        lanes = slice(head * head_size, (head + 1) * head_size)
        keys = heads_out[0, 1, lanes]
        values = heads_out[0, 2, lanes]
        for low in range(0, samples, QUERIES):
            cols = slice(low, low + QUERIES)
            scores = dot(keys, heads_out[0, 0, lanes, cols], TN)
            scores = jnp.where(live, scores, NEGATIVE)
            top = jnp.max(scores, axis=0, keepdims=True)
            powers = jnp.exp(scores - top)
            total = jnp.sum(powers, axis=0, keepdims=True)
            mixed = dot(values, powers.astype(BF)) * (1.0 / total)
            mixed_out[0, lanes, cols] = mixed.astype(BF)
            log_out[0, head : head + 1, cols] = top + jnp.log(total)
    for low in range(0, samples, group):
        rows = slice(low, low + group)
        part = tokens[0, rows].astype(F32) + dot(mixed_out[0, :, rows], weights[3], TN)
        part = part.astype(BF).reshape(dealt)
        if low // group < early:
            x_out[:, low // group, 0] = part
        else:
            late_out[:, 0, low // group - early, 0] = part
            late_out[:, 1, low // group - early, 0] = cotangent[0, rows].reshape(dealt)


def sample_backward(offset, early, opening, closing, counts, *refs):
    if early:
        d_early, *refs = refs
    d_late, tokens, first, heads, mixed, logs, weights, norms, *refs = refs
    if not opening:
        _, total_in, norm_total_in, *refs = refs
    grad_out, *refs = refs
    if closing:
        keep_out, send_out, norm_out, *refs = refs
    else:
        total_out, norm_out, *refs = refs
    d_rows, d_mix, d_heads, d_turned, total, norm_total = refs
    samples, width = tokens.shape[1:]
    head_size = width // HEADS
    score_scale = head_size ** (-0.5)
    group = d_late.shape[0] * BLOCK
    step = pl.program_id(0)

    @pl.when(step == 0)
    def _():
        if opening:
            total[...] = jnp.zeros_like(total)
            norm_total[...] = jnp.zeros_like(norm_total)
        else:
            total[...] = total_in[...]
            norm_total[...] = norm_total_in[...]

    feature_live = counts[2] + offset + step < counts[1]

    @pl.when(jnp.logical_not(feature_live))
    def _():
        grad_out[...] = jnp.zeros_like(grad_out)

    @pl.when(feature_live)
    def _():
        for low in range(0, samples, group):
            deal = low // group
            part = d_early[:, deal, 0] if deal < early else d_late[:, deal - early, 0]
            d_rows[low : low + group] = part.reshape(group, width)
        d_mix[...] = dot(weights[3], d_rows[...], NT).astype(BF)
        total[3 * width :] += dot(mixed[0], d_rows[...])
        live = row_index((samples, 1)) < counts[0]
        for pair in range(0, HEADS, 2):
            d_keys, d_values = [], []
            for head in (pair, pair + 1):
                lanes = slice(head * head_size, (head + 1) * head_size)
                keys = heads[0, 1, lanes]
                values = heads[0, 2, lanes]
                queries = heads[0, 0, lanes]
                grads = d_mix[lanes]
                shared = column_sum(grads.astype(F32) * mixed[0, lanes].astype(F32))
                scores = dot(keys, queries, TN)
                scores = jnp.where(live, scores, NEGATIVE)
                probs = jnp.exp(scores - logs[0, head : head + 1])
                d_probs = dot(values, grads, TN)
                d_scores = (probs * (d_probs - shared)).astype(BF)
                d_heads[lanes] = (dot(keys, d_scores) * score_scale).astype(BF)
                d_keys.append(dot(d_scores, queries, NT).astype(BF))
                d_values.append(dot(probs.astype(BF), grads, NT).astype(BF))
            lanes = slice(pair * head_size, (pair + 2) * head_size)
            d_turned[1, :, lanes] = jnp.concatenate(d_keys, axis=1)
            d_turned[2, :, lanes] = jnp.concatenate(d_values, axis=1)
        d_turned[0] = d_heads[...].T
        for which in range(3):
            total[which * width : (which + 1) * width] += dot(first[0], d_turned[which], TN)
        for low in range(0, samples, ROWS):
            rows = slice(low, low + ROWS)
            d_first = dot(d_turned[0, rows], weights[0], NT)
            d_first = d_first + dot(d_turned[1, rows], weights[1], NT)
            d_first = d_first + dot(d_turned[2, rows], weights[2], NT)
            normal, scale = normalize(tokens[0, rows].astype(F32))
            norm_total[0:1] += column_sum(d_first * normal)
            norm_total[1:2] += column_sum(d_first)
            back = normalize_back(normal, scale, d_first, norms[0:1])
            grad_out[0, rows] = (d_rows[rows].astype(F32) + back).astype(BF)

    @pl.when(step == pl.num_programs(0) - 1)
    def _():
        if closing:
            attention_parts(keep_out, total, counts[4], 0)
            attention_parts(send_out, total, 1 - counts[4], 0)
        else:
            total_out[...] = total[...]
        norm_out[...] = norm_total[...]


def gelu_parts(pre):
    root = 0.7978845608028654
    square = pre * pre
    curve = jnp.tanh(root * pre * (1.0 + 0.044715 * square))
    half = 0.5 * (1.0 + curve)
    slope = half + (0.5 * root) * pre * (1.0 - curve * curve) * (1.0 + 3 * 0.044715 * square)
    return pre * half, slope


def part_of(total, chip, core, owners, rows):
    start = pl.multiple_of((chip * 2 + core) * (owners * rows), owners * rows)
    part = total[pl.ds(start, owners * rows)].astype(BF)
    return part.reshape(owners, rows, part.shape[-1])


def attention_parts(where, total, core, low):
    chips, owners = where.shape[:2]
    half = total.shape[0] // (2 * chips * owners)
    for pair in range(chips // 2):
        part = part_of(total, pair, core, owners, 2 * half)
        for piece in range(2):
            rows = part[:, piece * half : (piece + 1) * half]
            where[2 * pair + piece, :, low : low + half] = rows


def middle(offset, opening, closing, groups, counts, *refs):
    refs = list(refs)

    def take(count):
        return [refs.pop(0) for _ in range(count)]

    x_in, cot_in, weights, weight_in, weight_out, norms = take(6)
    if not opening:
        held = take(3)
        (norm_held,) = take(1)
    if closing:
        d_outs = take(groups)
        y_out, keep_out, send_out, norm_out = take(4)
    else:
        (both_out,) = take(1)
        given = take(3)
        (norm_out,) = take(1)
    turned, order, back_order, x_one, normal_one, scale_one, normal_two, scale_two = take(8)
    x_two, low_rows, heads, d_heads, d_turned, mixed, d_mix, probs, live_grad = take(9)
    third, grad_rows, *totals, norm_total, copied = take(7)
    total_attn, total_in, total_out = totals
    if not opening:
        loads = [
            pltpu.make_async_copy(source, target, copied.at[place])
            for place, (source, target) in enumerate(zip(held, totals))
        ]
    devices, _, local, _, width = x_in.shape
    features = devices * local
    cells = features * BLOCK
    head_size = width // HEADS
    score_scale = head_size ** (-0.5)
    hidden_width = weight_in.shape[1]
    step = pl.program_id(0)
    first_sample = ((offset + step) * devices + counts[3]) * BLOCK

    @pl.when(step == 0)
    def _():
        if not opening:
            for load in loads:
                load.start()
        for which in range(3):
            turned[which] = weights[which].T
        here = row_index((cells, cells))
        there = lax.broadcasted_iota(jnp.int32, (cells, cells), 1)
        source = (here % features) * BLOCK + here // features
        order[...] = jnp.where(source == there, 1.0, 0.0).astype(BF)
        source = (here % BLOCK) * features + here // BLOCK
        back_order[...] = jnp.where(source == there, 1.0, 0.0).astype(BF)
        if opening:
            for total in totals:
                total[...] = jnp.zeros_like(total)
            norm_total[...] = jnp.zeros_like(norm_total)
        else:
            norm_total[...] = norm_held[...]

    x_one[...] = dot(order[...], x_in[:, 0].reshape(cells, width))
    for low in range(0, cells, ROWS):
        rows = slice(low, low + ROWS)
        normal, scale = normalize(x_one[rows])
        normal_one[rows] = normal
        scale_one[rows] = scale
        low_rows[rows] = (normal * norms[2:3] + norms[3:4]).astype(BF)
    heads[0] = scaled(dot(turned[0], low_rows[...], NT), head_size)
    for which in range(1, 3):
        heads[which] = dot(turned[which], low_rows[...], NT).astype(BF)

    units = cells // UNIT
    key_row = row_index((UNIT, cells))
    query_row = lax.broadcasted_iota(jnp.int32, (UNIT, cells), 1) % UNIT
    mask = (key_row // features == query_row // features) & (key_row % features < counts[1])
    for head in range(HEADS):
        lanes = slice(head * head_size, (head + 1) * head_size)
        scores = by_unit(units, lambda cols: dot(heads[1, lanes, cols], heads[0, lanes, cols], TN))
        scores = jnp.where(mask, scores, NEGATIVE)
        top = jnp.max(scores, axis=0, keepdims=True)
        powers = jnp.exp(scores - top)
        total = jnp.sum(powers, axis=0, keepdims=True)
        prob = powers * (1.0 / total)
        probs[head] = prob
        prob = prob.astype(BF)
        mixed[lanes] = by_unit(units, lambda cols: dot(heads[2, lanes, cols], prob[:, cols])).astype(BF)
    for low in range(0, cells, ROWS):
        rows = slice(low, low + ROWS)
        part = x_one[rows] + dot(mixed[:, rows], weights[3], TN)
        x_two[rows] = part
        normal, scale = normalize(part)
        normal_two[rows] = normal
        scale_two[rows] = scale
        third[rows] = (normal * norms[4:5] + norms[5:6]).astype(BF)

    if not opening:

        @pl.when(step == 0)
        def _():
            for load in loads:
                load.wait()

    def write_d(values):
        if not closing:
            both_out[:, 0, 0] = values
            return
        count = local // groups
        for place, d_out in enumerate(d_outs):
            d_out[:, 0] = values[:, place * count : (place + 1) * count]

    alive = first_sample < counts[0]

    @pl.when(jnp.logical_not(alive))
    def _():

        @pl.loop(0, hidden_width // width)
        def _(block):
            cols = block_of(block, width)
            hidden, _ = gelu_parts(dot(third[...], weight_in[:, cols]))
            x_two[...] += dot(hidden.astype(BF), weight_out[cols])

        write_d(jnp.zeros((devices, local, BLOCK, width), BF))

    @pl.when(alive)
    def _():
        place = row_index((cells, 1))
        cell_live = (place % features < counts[1]) & (
            first_sample + place // features < counts[0]
        )
        grads = dot(order[...], cot_in[:, 0].reshape(cells, width))
        live_grad[...] = jnp.where(cell_live, grads, 0.0).astype(BF)
        grad_rows[...] = jnp.zeros_like(grad_rows)

        @pl.loop(0, hidden_width // width)
        def _(block):
            cols = block_of(block, width)
            hidden, slope = gelu_parts(dot(third[...], weight_in[:, cols]))
            hidden = hidden.astype(BF)
            x_two[...] += dot(hidden, weight_out[cols])
            total_out[cols] += dot(hidden, live_grad[...], TN)
            d_pre = (dot(live_grad[...], weight_out[cols], NT) * slope).astype(BF)
            total_in[cols] += dot(d_pre, third[...], TN)
            grad_rows[...] += dot(d_pre, weight_in[:, cols], NT)


        for low in range(0, cells, ROWS):
            rows = slice(low, low + ROWS)
            normal = normal_two[rows]
            d_third = grad_rows[rows]
            norm_total[2:3] += column_sum(d_third * normal)
            norm_total[3:4] += column_sum(d_third)
            back = normalize_back(normal, scale_two[rows], d_third, norms[4:5])
            back = back + live_grad[rows].astype(F32)
            grad_rows[rows] = back
            live_grad[rows] = back.astype(BF)
        d_mix[...] = dot(weights[3], live_grad[...], NT).astype(BF)
        total_attn[3 * width :] += dot(mixed[...], live_grad[...])
        for head in range(HEADS):
            lanes = slice(head * head_size, (head + 1) * head_size)
            prob = probs[head]
            grads = d_mix[lanes]
            shared = column_sum(grads.astype(F32) * mixed[lanes].astype(F32))
            d_probs = by_unit(units, lambda cols: dot(heads[2, lanes, cols], grads[:, cols], TN))
            d_scores = (prob * (d_probs - shared)).astype(BF)
            low_prob = prob.astype(BF)
            d_query = by_unit(units, lambda cols: dot(heads[1, lanes, cols], d_scores[:, cols]))
            d_heads[0, lanes] = (d_query * score_scale).astype(BF)
            d_key = by_unit(units, lambda cols: dot(heads[0, lanes, cols], d_scores[:, cols], NT))
            d_heads[1, lanes] = d_key.astype(BF)
            d_value = by_unit(units, lambda cols: dot(grads[:, cols], low_prob[:, cols], NT))
            d_heads[2, lanes] = d_value.astype(BF)
        for which in range(3):
            d_turned[which] = d_heads[which].T
        for which in range(3):
            total_attn[which * width : (which + 1) * width] += dot(low_rows[...], d_turned[which], TN)
        for low in range(0, cells, ROWS):
            rows = slice(low, low + ROWS)
            d_second = dot(d_turned[0, rows], weights[0], NT)
            d_second = d_second + dot(d_turned[1, rows], weights[1], NT)
            d_second = d_second + dot(d_turned[2, rows], weights[2], NT)
            normal = normal_one[rows]
            norm_total[0:1] += column_sum(d_second * normal)
            norm_total[1:2] += column_sum(d_second)
            back = normalize_back(normal, scale_one[rows], d_second, norms[2:3])
            live_grad[rows] = (grad_rows[rows] + back).astype(BF)
        moved = dot(back_order[...], live_grad[...]).astype(BF)
        write_d(moved.reshape(devices, local, BLOCK, width))

    moved = dot(back_order[...], x_two[...].astype(BF)).astype(BF)
    moved = moved.reshape(devices, local, BLOCK, width)
    if closing:
        y_out[:, 0] = moved
    else:
        both_out[:, 1, 0] = moved

    @pl.when(step == pl.num_programs(0) - 1)
    def _():
        if closing:
            chips, owners, rows, _ = keep_out.shape
            own_ff = hidden_width // (2 * chips * owners)
            for where, core in ((keep_out, counts[4]), (send_out, 1 - counts[4])):
                for chip in range(chips):
                    for which, total in ((0, total_in), (1, total_out)):
                        part = part_of(total, chip, core, owners, own_ff)
                        where[chip, :, which * own_ff : (which + 1) * own_ff] = part
                attention_parts(where, total_attn, core, 2 * own_ff)
        else:
            stores = [
                pltpu.make_async_copy(source, target, copied.at[place])
                for place, (source, target) in enumerate(zip(totals, given))
            ]
            for store in stores:
                store.start()
            for store in stores:
                store.wait()
        norm_out[...] = norm_total[...]


def whole(shape):
    zeros = (0,) * len(shape)
    return pl.BlockSpec(shape, lambda step: zeros, pipeline_mode=pl.Buffered(1))


def half(shape, which):
    return pl.BlockSpec(
        (shape[0] // 2,) + tuple(shape[1:]),
        lambda step: (which, 0, 0),
        pipeline_mode=pl.Buffered(1),
    )


def once(shape):
    zeros = (0,) * len(shape)
    return pl.BlockSpec(shape, lambda step: zeros)


def lead(shape):
    zeros = (0,) * (len(shape) - 1)
    return pl.BlockSpec((1,) + tuple(shape[1:]), lambda step: (step,) + zeros)


def call(body, grid, ins, outs, scratch, nanoseconds, name, aliases=None):
    return pl.pallas_call(
        body,
        grid=(grid,),
        in_specs=[pl.BlockSpec(memory_space=pltpu.SMEM)] + [spec for spec, _ in ins[1:]],
        out_specs=[spec for spec, _, _ in outs],
        out_shape=[jax.ShapeDtypeStruct(shape, kind) for _, shape, kind in outs],
        scratch_shapes=[
            pltpu.SemaphoreType.DMA((3,)) if kind is None else pltpu.VMEM(shape, kind)
            for shape, kind in scratch
        ],
        input_output_aliases=aliases or {},
        compiler_params=pltpu.CompilerParams(vmem_limit_bytes=VMEM_BYTES),
        cost_estimate=pl.CostEstimate(
            flops=nanoseconds * 1150000, bytes_accessed=1 << 24, transcendentals=0
        ),
        name=name,
    )(ins[0][1], *[value for _, value in ins[1:]])


ANYWHERE = pl.BlockSpec(memory_space=pl.ANY)


def run_sample_forward(counts, tokens, cotangent, weights, norms, devices, early):
    local, samples, width = tokens.shape
    late = samples // (devices * BLOCK) - early
    square = (local, samples, width)
    three = (local, 3, width, samples)
    stats = (local, HEADS, samples)
    outs = [
        (
            pl.BlockSpec((devices, early, 1, BLOCK, width), lambda step: (0, 0, step, 0, 0)),
            (devices, early, local, BLOCK, width),
            BF,
        )
    ]
    if late:
        outs.append(
            (
                pl.BlockSpec(
                    (devices, 2, late, 1, BLOCK, width), lambda step: (0, 0, 0, step, 0, 0)
                ),
                (devices, 2, late, local, BLOCK, width),
                BF,
            )
        )
    outs = outs + [
        (lead(square), square, BF),
        (lead(three), three, BF),
        (lead(square), (local, width, samples), BF),
        (lead(stats), stats, F32),
    ]
    return call(
        functools.partial(sample_forward, late),
        local,
        [
            (None, counts),
            (lead(square), tokens),
            (lead(square), cotangent),
            (half(weights.shape, 0), weights),
            (whole(norms.shape), norms),
        ],
        outs,
        [((3, width, width), BF)],
        25000,
        "sample_forward",
    )


def run_middle(counts, x_dealt, cot_dealt, weights, weight_in, weight_out, norms, chips, offset, held, groups):
    array, which = x_dealt
    devices = array.shape[0]
    deals, local, _, width = array.shape[-4:]
    cells = devices * local * BLOCK
    hidden_width = weight_in.shape[1]
    parts = (chips, devices, (hidden_width + 2 * width) // (chips * devices), width)

    def dealt(which):
        if which is None:
            return pl.BlockSpec(
                (devices, 1, local, BLOCK, width), lambda step: (0, step, 0, 0, 0)
            )
        return pl.BlockSpec(
            (devices, None, 1, local, BLOCK, width),
            lambda step: (0, which, step, 0, 0, 0),
        )

    ins = [
        (None, counts),
        (dealt(x_dealt[1]), x_dealt[0]),
        (dealt(cot_dealt[1]), cot_dealt[0]),
        (half(weights.shape, 1), weights),
        (whole(weight_in.shape), weight_in),
        (whole(weight_out.shape), weight_out),
        (whole(norms.shape), norms),
    ]
    sums = [(4 * width, width), (hidden_width, width), (hidden_width, width)]
    norm_sums = (4, width)
    if held is not None:
        ins = ins + [(ANYWHERE, value) for value in held[:3]] + [(whole(norm_sums), held[3])]
    if groups:
        few = (devices, deals, local // groups, BLOCK, width)
        piece = pl.BlockSpec((devices, 1) + few[2:], lambda step: (0, step, 0, 0, 0))
        outs = [(piece, few, BF)] * groups + [
            (dealt(None), (devices, deals, local, BLOCK, width), BF),
            (once(parts), parts, BF),
            (once(parts), parts, BF),
        ]
    else:
        outs = [
            (
                pl.BlockSpec(
                    (devices, 2, 1, local, BLOCK, width), lambda step: (0, 0, step, 0, 0, 0)
                ),
                (devices, 2, deals, local, BLOCK, width),
                BF,
            )
        ] + [(ANYWHERE, shape, F32) for shape in sums]
    outs.append((once(norm_sums), norm_sums, F32))
    square = (cells, width)
    turned = (width, cells)
    return call(
        functools.partial(middle, offset, held is None, bool(groups), groups),
        deals,
        ins,
        outs,
        [
            ((3, width, width), BF),
            ((cells, cells), BF),
            ((cells, cells), BF),
            (square, F32),
            (square, F32),
            ((cells, 1), F32),
            (square, F32),
            ((cells, 1), F32),
            (square, F32),
            (square, BF),
            ((3,) + turned, BF),
            ((3,) + turned, BF),
            ((3,) + square, BF),
            (turned, BF),
            (turned, BF),
            ((HEADS, UNIT, cells), F32),
            (square, BF),
            (square, BF),
            (square, F32),
        ]
        + [(shape, F32) for shape in sums]
        + [(norm_sums, F32), ((3,), None)],
        deals * 23000,
        "middle",
    )


def run_sample_backward(counts, d_early, d_late, saved, weights, norms, chips, offset, held, closing):
    devices, late, count, _, width = d_late.shape
    tokens = saved[0]
    local, samples, _ = tokens.shape
    early = 0 if d_early is None else d_early.shape[2]
    parts = (chips, devices, 4 * width // (2 * chips * devices), width)

    def moved(shape):
        zeros = (0,) * (len(shape) - 1)
        return pl.BlockSpec((1,) + tuple(shape[1:]), lambda step: (step + offset,) + zeros)

    ins = [(None, counts)]
    if early:
        ins.append(
            (
                pl.BlockSpec(
                    (devices, None, early, 1, BLOCK, width),
                    lambda step: (0, 0, 0, step + offset, 0, 0),
                ),
                d_early,
            )
        )
    ins.append(
        (
            pl.BlockSpec((devices, late, 1, BLOCK, width), lambda step: (0, 0, step, 0, 0)),
            d_late,
        )
    )
    ins = ins + [(moved(value.shape), value) for value in saved]
    ins = ins + [(half(weights.shape, 0), weights), (whole(norms.shape), norms)]
    sums, norm_sums = (4 * width, width), (2, width)
    aliases = {}
    if held is not None:
        aliases = {len(ins): 0}
        ins = ins + [(ANYWHERE, held[0]), (whole(sums), held[1]), (whole(norm_sums), held[2])]
    outs = [(moved(tokens.shape), tokens.shape, BF)]
    if closing:
        outs = outs + [(once(parts), parts, BF), (once(parts), parts, BF)]
    else:
        outs = outs + [(once(sums), sums, F32)]
    outs.append((once(norm_sums), norm_sums, F32))
    return call(
        functools.partial(sample_backward, offset, early, held is None, closing),
        count,
        ins,
        outs,
        [
            ((samples, width), BF),
            ((width, samples), BF),
            ((width, samples), BF),
            ((3, samples, width), BF),
            (sums, F32),
            (norm_sums, F32),
        ],
        count * 11000,
        "sample_backward",
        aliases,
    )


def adam_step(weight, grad, first_m, second_m, rate):
    moment = BETA_ONE * first_m + (1.0 - BETA_ONE) * grad
    square = BETA_TWO * second_m + (1.0 - BETA_TWO) * grad * grad
    fix_one = 1.0 - BETA_ONE**STEP
    fix_two = 1.0 - BETA_TWO**STEP
    fresh = weight - rate * (
        moment / fix_one / (jnp.sqrt(square / fix_two) + ADAM_EPS) + DECAY * weight
    )
    return (fresh, moment, square)


def exchange(values, axis, groups=None):
    return lax.all_to_all(values, axis, 0, 0, axis_index_groups=groups, tiled=True)


def moved_by(values, axis, hop):
    pairs = [(place, hop(place)) for place in range(lax.axis_size(axis))]
    return lax.ppermute(values, axis, pairs)


def other_core(values):
    return moved_by(values, "task", lambda place: place ^ 1)


def along_y(values, shift):
    tasks = lax.axis_size("task")
    return moved_by(values, "task", lambda place: (place + 2 * shift) % tasks)


def along_x(values):
    return moved_by(values, "feat", lambda place: place ^ 1)


def along_z(values, shift):
    devices = lax.axis_size("feat")
    return moved_by(values, "feat", lambda place: (place + 2 * shift) % devices)


def reduce_core(keep, send):
    came = other_core(send)
    return (keep.astype(F32) + came.astype(F32)).astype(BF)


def chip_parts(values):
    if values.shape[0] != 2:
        return (values,)
    chip = lax.axis_index("task") // 2
    return tuple(
        lax.dynamic_index_in_dim(values, place, 0, keepdims=False) for place in (chip, 1 - chip)
    )


def reduce_chips(parts):
    if len(parts) == 2:
        return (parts[0].astype(F32) + along_y(parts[1], 1).astype(F32)).astype(BF)
    (values,) = parts
    chips = values.shape[0]
    groups = [[2 * place + core for place in range(chips)] for core in range(2)]
    return jnp.sum(exchange(values, "task", groups).astype(F32), axis=0).astype(BF)


def reduce_feat(values):
    return jnp.sum(exchange(values, "feat").astype(F32), axis=0)


def to_owners(one, two):
    chips = lax.axis_size("task") // 2
    chip = lax.axis_index("task") // 2
    even = chip % 2 == 0
    stay, leave = jnp.where(even, one, two), jnp.where(even, two, one)

    def target(chip, second):
        return chip // 2 + (chips // 2 if second else 0)

    def send(values, odd_second):
        return moved_by(
            values,
            "task",
            lambda place: 2 * target(place // 2, (place // 2 % 2 == 1) == odd_second) + place % 2,
        )

    if chips > 2:
        stay = send(stay, True)
    leave = send(leave, False)
    early = chip < chips // 2
    return jnp.concatenate(
        [jnp.where(early, stay, leave), jnp.where(early, leave, stay)], axis=0
    )


def place_copies(chips, layers, table, *refs):
    count = 2 * chips
    near, far = refs[:count], refs[count : count + 4]
    *halves, attn_out, in_out, out_out, block_out, pair, copied = refs[count + 4 :]
    step = pl.program_id(0)
    moves = []
    for half in halves:
        for deal in range(half.shape[-4]):
            for feature in range(half.shape[-3]):
                index = (slice(None),) + (1,) * (len(half.shape) - 5) + (deal, feature)
                place = len(moves)
                target = block_out.at[feature, place // half.shape[-3]]
                moves.append(pltpu.make_async_copy(half.at[index], target, copied.at[place]))

    @pl.when(step == 0)
    def _():
        for move in moves:
            move.start()
    side, layer = table[count], table[count + 1]
    rows = near[0].shape[2]
    half = far[0].shape[1] // 2

    def owner(other, behind):
        return ((layer + layers - behind) % layers) * 2 + (side ^ other)

    for place in range(count):

        @pl.when(step == place)
        def _():
            core, chip = place // chips, place % chips
            for other in range(2):
                for behind in range(layers):
                    at = owner(other, behind)
                    attn_out[block_of(at, rows)] = near[place][other, behind]
                    part = far[core * 2 + other]
                    pair[block_of(at, half)] = part[chip * layers + behind, :half]
                    out_out[block_of(at, half)] = part[chip * layers + behind, half:]

    in_out[...] = pair[...].T

    @pl.when(step == count - 1)
    def _():
        for move in moves:
            move.wait()


def gather_layers(own_attn, own_ff):
    layers = lax.axis_size("feat") // 2
    nears = [own_attn] + [along_z(own_attn, shift) for shift in range(1, layers)]
    fars = [own_ff] + [along_z(own_ff, shift) for shift in range(1, layers)]
    return jnp.stack(nears), jnp.stack(fars)


def gather_rest(nears, fars, came_halves):
    layers, rows_near, width = nears.shape
    rows_far = fars.shape[1]
    chips = lax.axis_size("task") // 2
    task, place = lax.axis_index("task"), lax.axis_index("feat")
    near = jnp.stack([nears, along_x(nears)])
    far = jnp.concatenate([fars] + [along_y(fars, shift) for shift in range(1, chips)])
    nears = [near] + [along_y(near, shift) for shift in range(1, chips)]
    fars = [far, along_x(far)]
    nears = nears + [other_core(value) for value in nears]
    fars = fars + [other_core(value) for value in fars]
    steps = jnp.arange(2 * chips, dtype=jnp.int32)
    chip = (task // 2 - steps) % chips
    core = (task % 2) ^ (steps // chips)
    table = jnp.concatenate([chip * 2 + core, jnp.stack([place % 2, place // 2])])
    total = 2 * chips
    owned = 2 * layers
    devices, _, local, _, _ = came_halves[-1].shape
    deals = sum(value.shape[-4] for value in came_halves)

    def held(value):
        zeros = (0,) * value.ndim
        return pl.BlockSpec(
            value.shape, lambda step, table: zeros, pipeline_mode=pl.Buffered(1)
        )

    return pl.pallas_call(
        functools.partial(place_copies, chips, layers),
        grid_spec=pltpu.PrefetchScalarGridSpec(
            num_scalar_prefetch=1,
            grid=(total,),
            in_specs=[held(value) for value in nears + fars] + [ANYWHERE] * len(came_halves),
            out_specs=[
                pl.BlockSpec((owned * rows_near, width), lambda step, table: (table[step], 0)),
                pl.BlockSpec(
                    (width, owned * rows_far // 2), lambda step, table: (0, table[step])
                ),
                pl.BlockSpec(
                    (owned * rows_far // 2, width), lambda step, table: (table[step], 0)
                ),
                ANYWHERE,
            ],
            scratch_shapes=[
                pltpu.VMEM((owned * rows_far // 2, width), BF),
                pltpu.SemaphoreType.DMA((deals * local,)),
            ],
        ),
        out_shape=[
            jax.ShapeDtypeStruct((total * owned * rows_near, width), BF),
            jax.ShapeDtypeStruct((width, total * owned * rows_far // 2), BF),
            jax.ShapeDtypeStruct((total * owned * rows_far // 2, width), BF),
            jax.ShapeDtypeStruct((local, deals, devices, BLOCK, width), BF),
        ],
        compiler_params=pltpu.CompilerParams(vmem_limit_bytes=40 * 1024 * 1024),
        name="place_copies",
    )(table.astype(jnp.int32), *nears, *fars, *came_halves)


def total_of(values):
    values = values + other_core(values)
    chips = lax.axis_size("task") // 2
    values = sum([along_y(values, shift) for shift in range(1, chips)], values)
    bit = 1
    while bit < lax.axis_size("feat"):
        values = values + moved_by(values, "feat", lambda place: place ^ bit)
        bit *= 2
    return values


def shards(
    tokens,
    cotangent,
    attn_weights,
    weight_in,
    weight_out,
    norm_params,
    master_attn,
    master_in,
    master_out,
    first_attn,
    first_in,
    first_out,
    first_norms,
    second_attn,
    second_in,
    second_out,
    second_norms,
    sample_count,
    feature_count,
):
    local, samples, width = tokens.shape[1:]
    devices = lax.axis_size("feat")
    tasks = lax.axis_size("task")
    chips = tasks // 2
    place = lax.axis_index("feat")
    deals = samples // (devices * BLOCK)
    counts = jnp.stack(
        [sample_count[0], feature_count[0], place * local, place, lax.axis_index("task") % 2]
    ).astype(jnp.int32)
    weights = attn_weights.reshape(8, width, width)

    early = max(deals // 2, 1)
    late = deals - early
    groups = 2 if late and local % 2 == 0 else 1
    own_ff = weight_in.shape[1] // (tasks * devices)
    own_attn = attn_weights.shape[0] // (tasks * devices)

    def dealt(values):
        count = values.shape[1] // (devices * BLOCK)
        values = values.reshape(local, count, devices, BLOCK, width)
        return values.transpose(2, 1, 0, 3, 4)

    came_cot = exchange(dealt(cotangent[0, :, : early * devices * BLOCK]), "feat")
    dealt_x, *rest = run_sample_forward(
        counts, tokens[0], cotangent[0], weights, norm_params, devices, early
    )
    came_cot, dealt_x, *rest = lax.optimization_barrier((came_cot, dealt_x, *rest))
    saved = [tokens[0]] + rest[-4:]
    came_x = exchange(dealt_x, "feat")
    shared = (weights, weight_in, weight_out, norm_params, chips)
    came_both = None
    if late:
        dealt_late, came_x = lax.optimization_barrier((rest[0], came_x))
        came_late = exchange(dealt_late, "feat")
        dealt_both, *held = run_middle(
            counts, (came_x, None), (came_cot, None), *shared, 0, None, 0
        )
        *dealt_d, dealt_y, keep_two, send_two, norms_two = run_middle(
            counts, (came_late, 0), (came_late, 1), *shared, early, held, groups
        )
        came_both = exchange(dealt_both, "feat")
        came_both, dealt_d, dealt_y, keep_two, send_two, norms_two = lax.optimization_barrier(
            (came_both, dealt_d, dealt_y, keep_two, send_two, norms_two)
        )
    else:
        *dealt_d, dealt_y, keep_two, send_two, norms_two = run_middle(
            counts, (came_x, None), (came_cot, None), *shared, 0, None, groups
        )
    came_d = exchange(dealt_d[0], "feat")
    parts_two = chip_parts(reduce_core(keep_two, send_two))
    came_d, _ = lax.optimization_barrier((came_d, parts_two))
    if groups == 2:
        dealt_d[1], came_d = lax.optimization_barrier((dealt_d[1], came_d))
        came_last = exchange(dealt_d[1], "feat")
        held = run_sample_backward(
            counts, came_both, came_d, saved, weights, norm_params, chips, 0, None, False
        )
        kept, *parts_two = parts_two
        came_d, held, kept = lax.optimization_barrier((came_last, held, kept))
        parts_two = (kept, *parts_two)
    else:
        held = None
    part_two, came_d = lax.optimization_barrier((reduce_chips(parts_two), came_d))
    share_two = reduce_feat(part_two)
    input_grad, keep_one, send_one, norms_one = run_sample_backward(
        counts,
        came_both,
        came_d,
        saved,
        weights,
        norm_params,
        chips,
        0 if held is None else local // 2,
        held,
        True,
    )
    share_two, input_grad, keep_one, send_one, norms_one = lax.optimization_barrier(
        (share_two, input_grad, keep_one, send_one, norms_one)
    )
    share_one = reduce_feat(reduce_chips(chip_parts(reduce_core(keep_one, send_one))))
    share_in_turned = share_two[:own_ff]
    share_out = share_two[own_ff : 2 * own_ff]
    share_one, dealt_y = lax.optimization_barrier((share_one, dealt_y))
    came_y = exchange(dealt_y, "feat")
    local_squares = jnp.sum(share_one * share_one) + jnp.sum(share_two * share_two)
    small = jnp.concatenate(
        [norms_one, norms_two, jnp.full((2, width), local_squares, F32)], axis=0
    )
    small, part_one, part_two = lax.optimization_barrier(
        (small, share_one, share_two[2 * own_ff :])
    )
    share_attn = to_owners(part_one, part_two)
    small, share_attn, came_y = lax.optimization_barrier((total_of(small), share_attn, came_y))
    total_norms = small[:6]
    squares = small[6, 0] + jnp.sum(total_norms * total_norms)
    grad_norm = jnp.sqrt(squares)
    factor = jnp.minimum(1.0, CLIP_AT / (grad_norm + 1e-06))
    new_attn, moment_attn, square_attn = adam_step(
        master_attn, factor * share_attn, first_attn, second_attn, RATE
    )
    new_in, moment_in, square_in = adam_step(
        master_in, factor * share_in_turned.T, first_in, second_in, RATE
    )
    new_out, moment_out, square_out = adam_step(
        master_out, factor * share_out, first_out, second_out, RATE
    )
    new_norms, moment_norms, square_norms = adam_step(
        norm_params, factor * total_norms, first_norms, second_norms, NORM_RATE
    )
    own_both = jnp.concatenate([new_in.astype(BF).T, new_out.astype(BF)], axis=0)
    nears, fars = gather_layers(new_attn.astype(BF), own_both)
    came_halves = [came_y] if came_both is None else [came_both, came_y]
    copy_attn, copy_in, copy_out, block_out = gather_rest(nears, fars, came_halves)
    block_out = block_out.reshape(1, local, samples, width)
    return (
        block_out,
        input_grad[None],
        grad_norm.reshape(1),
        new_attn,
        new_in,
        new_out,
        new_norms,
        moment_attn,
        moment_in,
        moment_out,
        moment_norms,
        square_attn,
        square_in,
        square_out,
        square_norms,
        copy_attn,
        copy_in,
        copy_out,
    )


def solution(mesh):
    cells = P("task", "feat", None, None)
    rows = P(("task", "feat"), None)
    columns = P(None, ("task", "feat"))
    return jax.shard_map(
        shards,
        mesh=mesh,
        in_specs=(cells, cells, P(), P(), P(), P())
        + (rows, columns, rows)
        + (rows, columns, rows, P())
        + (rows, columns, rows, P())
        + (P("task"), P("task")),
        out_specs=(cells, cells, P())
        + (rows, columns, rows, P())
        + (rows, columns, rows, P())
        + (rows, columns, rows, P())
        + (P(), P(), P()),
        check_vma=False,
    )
```

```python
import functools

import jax
import jax.numpy as jnp
from jax import lax
from jax.experimental import pallas as pl
from jax.experimental.pallas import tpu as pltpu
from jax.sharding import PartitionSpec as P

HEADS = 8
STEP = 5
NEGATIVE = -1e30
LN_EPS = 1e-05
CLIP_AT = 1.0
BETA_ONE = 0.9
BETA_TWO = 0.999
RATE = 0.02
NORM_RATE = 0.25
DECAY = 0.1
ADAM_EPS = 1e-08

BLOCK = 16
UNIT = 128
ROWS = 128
QUERIES = 512
UNROLL = 2
VMEM_BYTES = 60 * 1024 * 1024

BF = jnp.bfloat16
F32 = jnp.float32
NN = ((1,), (0,))
NT = ((1,), (1,))
TN = ((0,), (0,))


def dot(left, right, dims=NN):
    return lax.dot_general(left, right, (dims, ((), ())), preferred_element_type=F32)


def normalize(values):
    center = jnp.mean(values, axis=-1, keepdims=True)
    centred = values - center
    spread = jnp.mean(centred * centred, axis=-1, keepdims=True)
    scale = lax.rsqrt(spread + LN_EPS)
    return centred * scale, scale


def normalize_back(normal, scale, grad, gain):
    d_normal = grad * gain
    mean_one = jnp.mean(d_normal, axis=-1, keepdims=True)
    mean_two = jnp.mean(d_normal * normal, axis=-1, keepdims=True)
    return scale * (d_normal - mean_one - normal * mean_two)


def column_sum(values):
    return jnp.sum(values, axis=0, keepdims=True)


def by_unit(units, one):
    parts = [one(slice(place * UNIT, (place + 1) * UNIT)) for place in range(units)]
    return jnp.concatenate(parts, axis=1)


def scaled(values, head_size):
    return (values.astype(BF).astype(F32) * head_size ** (-0.5)).astype(BF)


def block_of(place, size):
    return pl.ds(pl.multiple_of(place * size, size), size)


def row_index(shape):
    return lax.broadcasted_iota(jnp.int32, shape, 0)


def sample_forward(late, counts, tokens, cotangent, weights, norms, x_out, *rest):
    if late:
        late_out, *rest = rest
    first_out, heads_out, mixed_out, log_out, turned = rest
    samples, width = tokens.shape[1:]
    head_size = width // HEADS
    early = x_out.shape[1]
    dealt = (x_out.shape[0], BLOCK, width)
    group = dealt[0] * BLOCK

    @pl.when(pl.program_id(0) == 0)
    def _():
        for which in range(3):
            turned[which] = weights[which].T

    for low in range(0, samples, ROWS):
        rows = slice(low, low + ROWS)
        normal, _ = normalize(tokens[0, rows].astype(F32))
        first_out[0, rows] = (normal * norms[0:1] + norms[1:2]).astype(BF)
    first = first_out[0]
    heads_out[0, 0] = scaled(dot(turned[0], first, NT), head_size)
    for which in range(1, 3):
        heads_out[0, which] = dot(turned[which], first, NT).astype(BF)
    live = row_index((samples, 1)) < counts[0]
    for head in range(HEADS):
        lanes = slice(head * head_size, (head + 1) * head_size)
        keys = heads_out[0, 1, lanes]
        values = heads_out[0, 2, lanes]
        for low in range(0, samples, QUERIES):
            cols = slice(low, low + QUERIES)
            scores = dot(keys, heads_out[0, 0, lanes, cols], TN)
            scores = jnp.where(live, scores, NEGATIVE)
            top = jnp.max(scores, axis=0, keepdims=True)
            powers = jnp.exp(scores - top)
            total = jnp.sum(powers, axis=0, keepdims=True)
            mixed = dot(values, powers.astype(BF)) * (1.0 / total)
            mixed_out[0, lanes, cols] = mixed.astype(BF)
            log_out[0, head : head + 1, cols] = top + jnp.log(total)
    for low in range(0, samples, group):
        rows = slice(low, low + group)
        part = tokens[0, rows].astype(F32) + dot(mixed_out[0, :, rows], weights[3], TN)
        part = part.astype(BF).reshape(dealt)
        if low // group < early:
            x_out[:, low // group, 0] = part
        else:
            late_out[:, 0, low // group - early, 0] = part
            late_out[:, 1, low // group - early, 0] = cotangent[0, rows].reshape(dealt)


def sample_backward(offset, early, opening, closing, counts, *refs):
    if early:
        d_early, *refs = refs
    d_late, tokens, first, heads, mixed, logs, weights, norms, *refs = refs
    if not opening:
        _, total_in, norm_total_in, *refs = refs
    grad_out, *refs = refs
    if closing:
        keep_out, send_out, norm_out, *refs = refs
    else:
        total_out, norm_out, *refs = refs
    d_rows, d_mix, d_heads, d_turned, total, norm_total = refs
    samples, width = tokens.shape[1:]
    head_size = width // HEADS
    score_scale = head_size ** (-0.5)
    group = d_late.shape[0] * BLOCK
    step = pl.program_id(0)

    @pl.when(step == 0)
    def _():
        if opening:
            total[...] = jnp.zeros_like(total)
            norm_total[...] = jnp.zeros_like(norm_total)
        else:
            total[...] = total_in[...]
            norm_total[...] = norm_total_in[...]

    feature_live = counts[2] + offset + step < counts[1]

    @pl.when(jnp.logical_not(feature_live))
    def _():
        grad_out[...] = jnp.zeros_like(grad_out)

    @pl.when(feature_live)
    def _():
        for low in range(0, samples, group):
            deal = low // group
            part = d_early[:, deal, 0] if deal < early else d_late[:, deal - early, 0]
            d_rows[low : low + group] = part.reshape(group, width)
        d_mix[...] = dot(weights[3], d_rows[...], NT).astype(BF)
        total[3 * width :] += dot(mixed[0], d_rows[...])
        live = row_index((samples, 1)) < counts[0]
        for pair in range(0, HEADS, 2):
            d_keys, d_values = [], []
            for head in (pair, pair + 1):
                lanes = slice(head * head_size, (head + 1) * head_size)
                keys = heads[0, 1, lanes]
                values = heads[0, 2, lanes]
                queries = heads[0, 0, lanes]
                grads = d_mix[lanes]
                shared = column_sum(grads.astype(F32) * mixed[0, lanes].astype(F32))
                scores = dot(keys, queries, TN)
                scores = jnp.where(live, scores, NEGATIVE)
                probs = jnp.exp(scores - logs[0, head : head + 1])
                d_probs = dot(values, grads, TN)
                d_scores = (probs * (d_probs - shared)).astype(BF)
                d_heads[lanes] = (dot(keys, d_scores) * score_scale).astype(BF)
                d_keys.append(dot(d_scores, queries, NT).astype(BF))
                d_values.append(dot(probs.astype(BF), grads, NT).astype(BF))
            lanes = slice(pair * head_size, (pair + 2) * head_size)
            d_turned[1, :, lanes] = jnp.concatenate(d_keys, axis=1)
            d_turned[2, :, lanes] = jnp.concatenate(d_values, axis=1)
        d_turned[0] = d_heads[...].T
        for which in range(3):
            total[which * width : (which + 1) * width] += dot(first[0], d_turned[which], TN)
        for low in range(0, samples, ROWS):
            rows = slice(low, low + ROWS)
            d_first = dot(d_turned[0, rows], weights[0], NT)
            d_first = d_first + dot(d_turned[1, rows], weights[1], NT)
            d_first = d_first + dot(d_turned[2, rows], weights[2], NT)
            normal, scale = normalize(tokens[0, rows].astype(F32))
            norm_total[0:1] += column_sum(d_first * normal)
            norm_total[1:2] += column_sum(d_first)
            back = normalize_back(normal, scale, d_first, norms[0:1])
            grad_out[0, rows] = (d_rows[rows].astype(F32) + back).astype(BF)

    @pl.when(step == pl.num_programs(0) - 1)
    def _():
        if closing:
            attention_parts(keep_out, total, counts[4], 0)
            attention_parts(send_out, total, 1 - counts[4], 0)
        else:
            total_out[...] = total[...]
        norm_out[...] = norm_total[...]


def gelu_parts(pre):
    root = 0.7978845608028654
    square = pre * pre
    curve = jnp.tanh(root * pre * (1.0 + 0.044715 * square))
    half = 0.5 * (1.0 + curve)
    slope = half + (0.5 * root) * pre * (1.0 - curve * curve) * (1.0 + 3 * 0.044715 * square)
    return pre * half, slope


def part_of(total, chip, core, owners, rows):
    start = pl.multiple_of((chip * 2 + core) * (owners * rows), owners * rows)
    part = total[pl.ds(start, owners * rows)].astype(BF)
    return part.reshape(owners, rows, part.shape[-1])


def attention_parts(where, total, core, low):
    chips, owners = where.shape[:2]
    half = total.shape[0] // (2 * chips * owners)
    for pair in range(chips // 2):
        part = part_of(total, pair, core, owners, 2 * half)
        for piece in range(2):
            rows = part[:, piece * half : (piece + 1) * half]
            where[2 * pair + piece, :, low : low + half] = rows


def middle(offset, opening, closing, groups, counts, *refs):
    refs = list(refs)

    def take(count):
        return [refs.pop(0) for _ in range(count)]

    x_in, cot_in, weights, weight_in, weight_out, norms = take(6)
    if not opening:
        held = take(3)
        (norm_held,) = take(1)
    if closing:
        d_outs = take(groups)
        y_out, keep_out, send_out, norm_out = take(4)
    else:
        (both_out,) = take(1)
        given = take(3)
        (norm_out,) = take(1)
    turned, order, back_order, x_one, normal_one, scale_one, normal_two, scale_two = take(8)
    x_two, low_rows, heads, d_heads, d_turned, mixed, d_mix, probs, live_grad = take(9)
    third, grad_rows, *totals, norm_total, copied = take(7)
    total_attn, total_in, total_out = totals
    if not opening:
        loads = [
            pltpu.make_async_copy(source, target, copied.at[place])
            for place, (source, target) in enumerate(zip(held, totals))
        ]
    devices, _, local, _, width = x_in.shape
    features = devices * local
    cells = features * BLOCK
    head_size = width // HEADS
    score_scale = head_size ** (-0.5)
    hidden_width = weight_in.shape[1]
    step = pl.program_id(0)
    first_sample = ((offset + step) * devices + counts[3]) * BLOCK

    @pl.when(step == 0)
    def _():
        if not opening:
            for load in loads:
                load.start()
        for which in range(3):
            turned[which] = weights[which].T
        here = row_index((cells, cells))
        there = lax.broadcasted_iota(jnp.int32, (cells, cells), 1)
        source = (here % features) * BLOCK + here // features
        order[...] = jnp.where(source == there, 1.0, 0.0).astype(BF)
        source = (here % BLOCK) * features + here // BLOCK
        back_order[...] = jnp.where(source == there, 1.0, 0.0).astype(BF)
        if opening:
            for total in totals:
                total[...] = jnp.zeros_like(total)
            norm_total[...] = jnp.zeros_like(norm_total)
        else:
            norm_total[...] = norm_held[...]

    x_one[...] = dot(order[...], x_in[:, 0].reshape(cells, width))
    for low in range(0, cells, ROWS):
        rows = slice(low, low + ROWS)
        normal, scale = normalize(x_one[rows])
        normal_one[rows] = normal
        scale_one[rows] = scale
        low_rows[rows] = (normal * norms[2:3] + norms[3:4]).astype(BF)
    heads[0] = scaled(dot(turned[0], low_rows[...], NT), head_size)
    for which in range(1, 3):
        heads[which] = dot(turned[which], low_rows[...], NT).astype(BF)

    units = cells // UNIT
    key_row = row_index((UNIT, cells))
    query_row = lax.broadcasted_iota(jnp.int32, (UNIT, cells), 1) % UNIT
    mask = (key_row // features == query_row // features) & (key_row % features < counts[1])
    for head in range(HEADS):
        lanes = slice(head * head_size, (head + 1) * head_size)
        scores = by_unit(units, lambda cols: dot(heads[1, lanes, cols], heads[0, lanes, cols], TN))
        scores = jnp.where(mask, scores, NEGATIVE)
        top = jnp.max(scores, axis=0, keepdims=True)
        powers = jnp.exp(scores - top)
        total = jnp.sum(powers, axis=0, keepdims=True)
        prob = powers * (1.0 / total)
        probs[head] = prob
        prob = prob.astype(BF)
        mixed[lanes] = by_unit(units, lambda cols: dot(heads[2, lanes, cols], prob[:, cols])).astype(BF)
    for low in range(0, cells, ROWS):
        rows = slice(low, low + ROWS)
        part = x_one[rows] + dot(mixed[:, rows], weights[3], TN)
        x_two[rows] = part
        normal, scale = normalize(part)
        normal_two[rows] = normal
        scale_two[rows] = scale
        third[rows] = (normal * norms[4:5] + norms[5:6]).astype(BF)

    if not opening:

        @pl.when(step == 0)
        def _():
            for load in loads:
                load.wait()

    def write_d(values):
        if not closing:
            both_out[:, 0, 0] = values
            return
        count = local // groups
        for place, d_out in enumerate(d_outs):
            d_out[:, 0] = values[:, place * count : (place + 1) * count]

    alive = first_sample < counts[0]

    @pl.when(jnp.logical_not(alive))
    def _():

        @pl.loop(0, hidden_width // width)
        def _(block):
            cols = block_of(block, width)
            hidden, _ = gelu_parts(dot(third[...], weight_in[:, cols]))
            x_two[...] += dot(hidden.astype(BF), weight_out[cols])

        write_d(jnp.zeros((devices, local, BLOCK, width), BF))

    @pl.when(alive)
    def _():
        place = row_index((cells, 1))
        cell_live = (place % features < counts[1]) & (
            first_sample + place // features < counts[0]
        )
        grads = dot(order[...], cot_in[:, 0].reshape(cells, width))
        live_grad[...] = jnp.where(cell_live, grads, 0.0).astype(BF)
        grad_rows[...] = jnp.zeros_like(grad_rows)

        @pl.loop(0, hidden_width // width)
        def _(block):
            cols = block_of(block, width)
            hidden, slope = gelu_parts(dot(third[...], weight_in[:, cols]))
            hidden = hidden.astype(BF)
            x_two[...] += dot(hidden, weight_out[cols])
            total_out[cols] += dot(hidden, live_grad[...], TN)
            d_pre = (dot(live_grad[...], weight_out[cols], NT) * slope).astype(BF)
            total_in[cols] += dot(d_pre, third[...], TN)
            grad_rows[...] += dot(d_pre, weight_in[:, cols], NT)


        for low in range(0, cells, ROWS):
            rows = slice(low, low + ROWS)
            normal = normal_two[rows]
            d_third = grad_rows[rows]
            norm_total[2:3] += column_sum(d_third * normal)
            norm_total[3:4] += column_sum(d_third)
            back = normalize_back(normal, scale_two[rows], d_third, norms[4:5])
            back = back + live_grad[rows].astype(F32)
            grad_rows[rows] = back
            live_grad[rows] = back.astype(BF)
        d_mix[...] = dot(weights[3], live_grad[...], NT).astype(BF)
        total_attn[3 * width :] += dot(mixed[...], live_grad[...])
        for head in range(HEADS):
            lanes = slice(head * head_size, (head + 1) * head_size)
            prob = probs[head]
            grads = d_mix[lanes]
            shared = column_sum(grads.astype(F32) * mixed[lanes].astype(F32))
            d_probs = by_unit(units, lambda cols: dot(heads[2, lanes, cols], grads[:, cols], TN))
            d_scores = (prob * (d_probs - shared)).astype(BF)
            low_prob = prob.astype(BF)
            d_query = by_unit(units, lambda cols: dot(heads[1, lanes, cols], d_scores[:, cols]))
            d_heads[0, lanes] = (d_query * score_scale).astype(BF)
            d_key = by_unit(units, lambda cols: dot(heads[0, lanes, cols], d_scores[:, cols], NT))
            d_heads[1, lanes] = d_key.astype(BF)
            d_value = by_unit(units, lambda cols: dot(grads[:, cols], low_prob[:, cols], NT))
            d_heads[2, lanes] = d_value.astype(BF)
        for which in range(3):
            d_turned[which] = d_heads[which].T
        for which in range(3):
            total_attn[which * width : (which + 1) * width] += dot(low_rows[...], d_turned[which], TN)
        for low in range(0, cells, ROWS):
            rows = slice(low, low + ROWS)
            d_second = dot(d_turned[0, rows], weights[0], NT)
            d_second = d_second + dot(d_turned[1, rows], weights[1], NT)
            d_second = d_second + dot(d_turned[2, rows], weights[2], NT)
            normal = normal_one[rows]
            norm_total[0:1] += column_sum(d_second * normal)
            norm_total[1:2] += column_sum(d_second)
            back = normalize_back(normal, scale_one[rows], d_second, norms[2:3])
            live_grad[rows] = (grad_rows[rows] + back).astype(BF)
        moved = dot(back_order[...], live_grad[...]).astype(BF)
        write_d(moved.reshape(devices, local, BLOCK, width))

    moved = dot(back_order[...], x_two[...].astype(BF)).astype(BF)
    moved = moved.reshape(devices, local, BLOCK, width)
    if closing:
        y_out[:, 0] = moved
    else:
        both_out[:, 1, 0] = moved

    @pl.when(step == pl.num_programs(0) - 1)
    def _():
        if closing:
            chips, owners, rows, _ = keep_out.shape
            own_ff = hidden_width // (2 * chips * owners)
            for where, core in ((keep_out, counts[4]), (send_out, 1 - counts[4])):
                for chip in range(chips):
                    for which, total in ((0, total_in), (1, total_out)):
                        part = part_of(total, chip, core, owners, own_ff)
                        where[chip, :, which * own_ff : (which + 1) * own_ff] = part
                attention_parts(where, total_attn, core, 2 * own_ff)
        else:
            stores = [
                pltpu.make_async_copy(source, target, copied.at[place])
                for place, (source, target) in enumerate(zip(totals, given))
            ]
            for store in stores:
                store.start()
            for store in stores:
                store.wait()
        norm_out[...] = norm_total[...]


def whole(shape):
    zeros = (0,) * len(shape)
    return pl.BlockSpec(shape, lambda step: zeros, pipeline_mode=pl.Buffered(1))


def half(shape, which):
    return pl.BlockSpec(
        (shape[0] // 2,) + tuple(shape[1:]),
        lambda step: (which, 0, 0),
        pipeline_mode=pl.Buffered(1),
    )


def once(shape):
    zeros = (0,) * len(shape)
    return pl.BlockSpec(shape, lambda step: zeros)


def lead(shape):
    zeros = (0,) * (len(shape) - 1)
    return pl.BlockSpec((1,) + tuple(shape[1:]), lambda step: (step,) + zeros)


def call(body, grid, ins, outs, scratch, nanoseconds, name, aliases=None):
    return pl.pallas_call(
        body,
        grid=(grid,),
        in_specs=[pl.BlockSpec(memory_space=pltpu.SMEM)] + [spec for spec, _ in ins[1:]],
        out_specs=[spec for spec, _, _ in outs],
        out_shape=[jax.ShapeDtypeStruct(shape, kind) for _, shape, kind in outs],
        scratch_shapes=[
            pltpu.SemaphoreType.DMA((3,)) if kind is None else pltpu.VMEM(shape, kind)
            for shape, kind in scratch
        ],
        input_output_aliases=aliases or {},
        compiler_params=pltpu.CompilerParams(vmem_limit_bytes=VMEM_BYTES),
        cost_estimate=pl.CostEstimate(
            flops=nanoseconds * 1150000, bytes_accessed=1 << 24, transcendentals=0
        ),
        name=name,
    )(ins[0][1], *[value for _, value in ins[1:]])


ANYWHERE = pl.BlockSpec(memory_space=pl.ANY)


def run_sample_forward(counts, tokens, cotangent, weights, norms, devices, early):
    local, samples, width = tokens.shape
    late = samples // (devices * BLOCK) - early
    square = (local, samples, width)
    three = (local, 3, width, samples)
    stats = (local, HEADS, samples)
    outs = [
        (
            pl.BlockSpec((devices, early, 1, BLOCK, width), lambda step: (0, 0, step, 0, 0)),
            (devices, early, local, BLOCK, width),
            BF,
        )
    ]
    if late:
        outs.append(
            (
                pl.BlockSpec(
                    (devices, 2, late, 1, BLOCK, width), lambda step: (0, 0, 0, step, 0, 0)
                ),
                (devices, 2, late, local, BLOCK, width),
                BF,
            )
        )
    outs = outs + [
        (lead(square), square, BF),
        (lead(three), three, BF),
        (lead(square), (local, width, samples), BF),
        (lead(stats), stats, F32),
    ]
    return call(
        functools.partial(sample_forward, late),
        local,
        [
            (None, counts),
            (lead(square), tokens),
            (lead(square), cotangent),
            (half(weights.shape, 0), weights),
            (whole(norms.shape), norms),
        ],
        outs,
        [((3, width, width), BF)],
        25000,
        "sample_forward",
    )


def run_middle(counts, x_dealt, cot_dealt, weights, weight_in, weight_out, norms, chips, offset, held, groups):
    array, which = x_dealt
    devices = array.shape[0]
    deals, local, _, width = array.shape[-4:]
    cells = devices * local * BLOCK
    hidden_width = weight_in.shape[1]
    parts = (chips, devices, (hidden_width + 2 * width) // (chips * devices), width)

    def dealt(which):
        if which is None:
            return pl.BlockSpec(
                (devices, 1, local, BLOCK, width), lambda step: (0, step, 0, 0, 0)
            )
        return pl.BlockSpec(
            (devices, None, 1, local, BLOCK, width),
            lambda step: (0, which, step, 0, 0, 0),
        )

    ins = [
        (None, counts),
        (dealt(x_dealt[1]), x_dealt[0]),
        (dealt(cot_dealt[1]), cot_dealt[0]),
        (half(weights.shape, 1), weights),
        (whole(weight_in.shape), weight_in),
        (whole(weight_out.shape), weight_out),
        (whole(norms.shape), norms),
    ]
    sums = [(4 * width, width), (hidden_width, width), (hidden_width, width)]
    norm_sums = (4, width)
    if held is not None:
        ins = ins + [(ANYWHERE, value) for value in held[:3]] + [(whole(norm_sums), held[3])]
    if groups:
        few = (devices, deals, local // groups, BLOCK, width)
        piece = pl.BlockSpec((devices, 1) + few[2:], lambda step: (0, step, 0, 0, 0))
        outs = [(piece, few, BF)] * groups + [
            (dealt(None), (devices, deals, local, BLOCK, width), BF),
            (once(parts), parts, BF),
            (once(parts), parts, BF),
        ]
    else:
        outs = [
            (
                pl.BlockSpec(
                    (devices, 2, 1, local, BLOCK, width), lambda step: (0, 0, step, 0, 0, 0)
                ),
                (devices, 2, deals, local, BLOCK, width),
                BF,
            )
        ] + [(ANYWHERE, shape, F32) for shape in sums]
    outs.append((once(norm_sums), norm_sums, F32))
    square = (cells, width)
    turned = (width, cells)
    return call(
        functools.partial(middle, offset, held is None, bool(groups), groups),
        deals,
        ins,
        outs,
        [
            ((3, width, width), BF),
            ((cells, cells), BF),
            ((cells, cells), BF),
            (square, F32),
            (square, F32),
            ((cells, 1), F32),
            (square, F32),
            ((cells, 1), F32),
            (square, F32),
            (square, BF),
            ((3,) + turned, BF),
            ((3,) + turned, BF),
            ((3,) + square, BF),
            (turned, BF),
            (turned, BF),
            ((HEADS, UNIT, cells), F32),
            (square, BF),
            (square, BF),
            (square, F32),
        ]
        + [(shape, F32) for shape in sums]
        + [(norm_sums, F32), ((3,), None)],
        deals * 23000,
        "middle",
    )


def run_sample_backward(counts, d_early, d_late, saved, weights, norms, chips, offset, held, closing):
    devices, late, count, _, width = d_late.shape
    tokens = saved[0]
    local, samples, _ = tokens.shape
    early = 0 if d_early is None else d_early.shape[2]
    parts = (chips, devices, 4 * width // (2 * chips * devices), width)

    def moved(shape):
        zeros = (0,) * (len(shape) - 1)
        return pl.BlockSpec((1,) + tuple(shape[1:]), lambda step: (step + offset,) + zeros)

    ins = [(None, counts)]
    if early:
        ins.append(
            (
                pl.BlockSpec(
                    (devices, None, early, 1, BLOCK, width),
                    lambda step: (0, 0, 0, step + offset, 0, 0),
                ),
                d_early,
            )
        )
    ins.append(
        (
            pl.BlockSpec((devices, late, 1, BLOCK, width), lambda step: (0, 0, step, 0, 0)),
            d_late,
        )
    )
    ins = ins + [(moved(value.shape), value) for value in saved]
    ins = ins + [(half(weights.shape, 0), weights), (whole(norms.shape), norms)]
    sums, norm_sums = (4 * width, width), (2, width)
    aliases = {}
    if held is not None:
        aliases = {len(ins): 0}
        ins = ins + [(ANYWHERE, held[0]), (whole(sums), held[1]), (whole(norm_sums), held[2])]
    outs = [(moved(tokens.shape), tokens.shape, BF)]
    if closing:
        outs = outs + [(once(parts), parts, BF), (once(parts), parts, BF)]
    else:
        outs = outs + [(once(sums), sums, F32)]
    outs.append((once(norm_sums), norm_sums, F32))
    return call(
        functools.partial(sample_backward, offset, early, held is None, closing),
        count,
        ins,
        outs,
        [
            ((samples, width), BF),
            ((width, samples), BF),
            ((width, samples), BF),
            ((3, samples, width), BF),
            (sums, F32),
            (norm_sums, F32),
        ],
        count * 11000,
        "sample_backward",
        aliases,
    )


def adam_step(weight, grad, first_m, second_m, rate):
    moment = BETA_ONE * first_m + (1.0 - BETA_ONE) * grad
    square = BETA_TWO * second_m + (1.0 - BETA_TWO) * grad * grad
    fix_one = 1.0 - BETA_ONE**STEP
    fix_two = 1.0 - BETA_TWO**STEP
    fresh = weight - rate * (
        moment / fix_one / (jnp.sqrt(square / fix_two) + ADAM_EPS) + DECAY * weight
    )
    return (fresh, moment, square)


def exchange(values, axis, groups=None):
    return lax.all_to_all(values, axis, 0, 0, axis_index_groups=groups, tiled=True)


def moved_by(values, axis, hop):
    pairs = [(place, hop(place)) for place in range(lax.axis_size(axis))]
    return lax.ppermute(values, axis, pairs)


def other_core(values):
    return moved_by(values, "task", lambda place: place ^ 1)


def along_y(values, shift):
    tasks = lax.axis_size("task")
    return moved_by(values, "task", lambda place: (place + 2 * shift) % tasks)


def along_x(values):
    return moved_by(values, "feat", lambda place: place ^ 1)


def along_z(values, shift):
    devices = lax.axis_size("feat")
    return moved_by(values, "feat", lambda place: (place + 2 * shift) % devices)


def reduce_core(keep, send):
    came = other_core(send)
    return (keep.astype(F32) + came.astype(F32)).astype(BF)


def in_plane(values, up, across):
    tasks, devices = lax.axis_size("task"), lax.axis_size("feat")
    pairs = [
        (task * devices + place, (task + 2 * up) % tasks * devices + (place ^ across))
        for task in range(tasks)
        for place in range(devices)
    ]
    return lax.ppermute(values, ("task", "feat"), pairs)


def plane_parts(values):
    chips, devices = values.shape[:2]
    values = values.reshape((chips, devices // 2, 2) + values.shape[2:])
    chip, side = lax.axis_index("task") // 2, lax.axis_index("feat") % 2
    parts = []
    for up in range(chips):
        part = lax.dynamic_index_in_dim(values, (chip + up) % chips, 0, keepdims=False)
        for across in range(2):
            parts.append(lax.dynamic_index_in_dim(part, side ^ across, 1, keepdims=False))
    return parts


def reduce_plane(parts):
    total = parts[0].astype(F32)
    for place, part in enumerate(parts[1:], 1):
        total = total + in_plane(part, place // 2, place % 2).astype(F32)
    return total.astype(BF)


def layer_parts(values):
    layers = values.shape[0]
    layer = lax.axis_index("feat") // 2
    return [
        lax.dynamic_index_in_dim(values, (layer + shift) % layers, 0, keepdims=False)
        for shift in range(layers)
    ]


def reduce_layers(parts):
    total = parts[0].astype(F32)
    for shift, part in enumerate(parts[1:], 1):
        total = total + along_z(part, shift).astype(F32)
    return total


def to_owners(one, two):
    chips = lax.axis_size("task") // 2
    chip = lax.axis_index("task") // 2
    even = chip % 2 == 0
    stay, leave = jnp.where(even, one, two), jnp.where(even, two, one)

    def target(chip, second):
        return chip // 2 + (chips // 2 if second else 0)

    def send(values, odd_second):
        return moved_by(
            values,
            "task",
            lambda place: 2 * target(place // 2, (place // 2 % 2 == 1) == odd_second) + place % 2,
        )

    if chips > 2:
        stay = send(stay, True)
    leave = send(leave, False)
    early = chip < chips // 2
    return jnp.concatenate(
        [jnp.where(early, stay, leave), jnp.where(early, leave, stay)], axis=0
    )


def place_copies(chips, layers, table, *refs):
    count = 2 * chips
    near, far = refs[:count], refs[count : count + 4]
    *halves, attn_out, in_out, out_out, block_out, pair, copied = refs[count + 4 :]
    step = pl.program_id(0)
    moves = []
    for half in halves:
        for deal in range(half.shape[-4]):
            for feature in range(half.shape[-3]):
                index = (slice(None),) + (1,) * (len(half.shape) - 5) + (deal, feature)
                place = len(moves)
                target = block_out.at[feature, place // half.shape[-3]]
                moves.append(pltpu.make_async_copy(half.at[index], target, copied.at[place]))

    @pl.when(step == 0)
    def _():
        for move in moves:
            move.start()
    side, layer = table[count], table[count + 1]
    rows = near[0].shape[2]
    half = far[0].shape[1] // 2

    def owner(other, behind):
        return ((layer + layers - behind) % layers) * 2 + (side ^ other)

    for place in range(count):

        @pl.when(step == place)
        def _():
            core, chip = place // chips, place % chips
            for other in range(2):
                for behind in range(layers):
                    at = owner(other, behind)
                    attn_out[block_of(at, rows)] = near[place][other, behind]
                    part = far[core * 2 + other]
                    pair[block_of(at, half)] = part[chip * layers + behind, :half]
                    out_out[block_of(at, half)] = part[chip * layers + behind, half:]

    in_out[...] = pair[...].T

    @pl.when(step == count - 1)
    def _():
        for move in moves:
            move.wait()


def gather_layers(own_attn, own_ff):
    layers = lax.axis_size("feat") // 2
    nears = [own_attn] + [along_z(own_attn, shift) for shift in range(1, layers)]
    fars = [own_ff] + [along_z(own_ff, shift) for shift in range(1, layers)]
    return jnp.stack(nears), jnp.stack(fars)


def gather_rest(nears, fars, came_halves):
    layers, rows_near, width = nears.shape
    rows_far = fars.shape[1]
    chips = lax.axis_size("task") // 2
    task, place = lax.axis_index("task"), lax.axis_index("feat")
    near = jnp.stack([nears, along_x(nears)])
    far = jnp.concatenate([fars] + [along_y(fars, shift) for shift in range(1, chips)])
    nears = [near] + [along_y(near, shift) for shift in range(1, chips)]
    fars = [far, along_x(far)]
    nears = nears + [other_core(value) for value in nears]
    fars = fars + [other_core(value) for value in fars]
    steps = jnp.arange(2 * chips, dtype=jnp.int32)
    chip = (task // 2 - steps) % chips
    core = (task % 2) ^ (steps // chips)
    table = jnp.concatenate([chip * 2 + core, jnp.stack([place % 2, place // 2])])
    total = 2 * chips
    owned = 2 * layers
    devices, _, local, _, _ = came_halves[-1].shape
    deals = sum(value.shape[-4] for value in came_halves)

    def held(value):
        zeros = (0,) * value.ndim
        return pl.BlockSpec(
            value.shape, lambda step, table: zeros, pipeline_mode=pl.Buffered(1)
        )

    return pl.pallas_call(
        functools.partial(place_copies, chips, layers),
        grid_spec=pltpu.PrefetchScalarGridSpec(
            num_scalar_prefetch=1,
            grid=(total,),
            in_specs=[held(value) for value in nears + fars] + [ANYWHERE] * len(came_halves),
            out_specs=[
                pl.BlockSpec((owned * rows_near, width), lambda step, table: (table[step], 0)),
                pl.BlockSpec(
                    (width, owned * rows_far // 2), lambda step, table: (0, table[step])
                ),
                pl.BlockSpec(
                    (owned * rows_far // 2, width), lambda step, table: (table[step], 0)
                ),
                ANYWHERE,
            ],
            scratch_shapes=[
                pltpu.VMEM((owned * rows_far // 2, width), BF),
                pltpu.SemaphoreType.DMA((deals * local,)),
            ],
        ),
        out_shape=[
            jax.ShapeDtypeStruct((total * owned * rows_near, width), BF),
            jax.ShapeDtypeStruct((width, total * owned * rows_far // 2), BF),
            jax.ShapeDtypeStruct((total * owned * rows_far // 2, width), BF),
            jax.ShapeDtypeStruct((local, deals, devices, BLOCK, width), BF),
        ],
        compiler_params=pltpu.CompilerParams(vmem_limit_bytes=40 * 1024 * 1024),
        name="place_copies",
    )(table.astype(jnp.int32), *nears, *fars, *came_halves)


def total_of(values):
    values = values + other_core(values)
    chips = lax.axis_size("task") // 2
    values = sum([along_y(values, shift) for shift in range(1, chips)], values)
    bit = 1
    while bit < lax.axis_size("feat"):
        values = values + moved_by(values, "feat", lambda place: place ^ bit)
        bit *= 2
    return values


def shards(
    tokens,
    cotangent,
    attn_weights,
    weight_in,
    weight_out,
    norm_params,
    master_attn,
    master_in,
    master_out,
    first_attn,
    first_in,
    first_out,
    first_norms,
    second_attn,
    second_in,
    second_out,
    second_norms,
    sample_count,
    feature_count,
):
    local, samples, width = tokens.shape[1:]
    devices = lax.axis_size("feat")
    tasks = lax.axis_size("task")
    chips = tasks // 2
    place = lax.axis_index("feat")
    deals = samples // (devices * BLOCK)
    counts = jnp.stack(
        [sample_count[0], feature_count[0], place * local, place, lax.axis_index("task") % 2]
    ).astype(jnp.int32)
    weights = attn_weights.reshape(8, width, width)

    early = max(deals // 2, 1)
    late = deals - early
    groups = 2 if late and local % 2 == 0 else 1
    own_ff = weight_in.shape[1] // (tasks * devices)
    own_attn = attn_weights.shape[0] // (tasks * devices)

    def dealt(values):
        count = values.shape[1] // (devices * BLOCK)
        values = values.reshape(local, count, devices, BLOCK, width)
        return values.transpose(2, 1, 0, 3, 4)

    came_cot = exchange(dealt(cotangent[0, :, : early * devices * BLOCK]), "feat")
    dealt_x, *rest = run_sample_forward(
        counts, tokens[0], cotangent[0], weights, norm_params, devices, early
    )
    came_cot, dealt_x, *rest = lax.optimization_barrier((came_cot, dealt_x, *rest))
    saved = [tokens[0]] + rest[-4:]
    came_x = exchange(dealt_x, "feat")
    shared = (weights, weight_in, weight_out, norm_params, chips)
    came_both = None
    if late:
        dealt_late, came_x = lax.optimization_barrier((rest[0], came_x))
        came_late = exchange(dealt_late, "feat")
        dealt_both, *held = run_middle(
            counts, (came_x, None), (came_cot, None), *shared, 0, None, 0
        )
        *dealt_d, dealt_y, keep_two, send_two, norms_two = run_middle(
            counts, (came_late, 0), (came_late, 1), *shared, early, held, groups
        )
        came_both = exchange(dealt_both, "feat")
        came_both, dealt_d, dealt_y, keep_two, send_two, norms_two = lax.optimization_barrier(
            (came_both, dealt_d, dealt_y, keep_two, send_two, norms_two)
        )
    else:
        *dealt_d, dealt_y, keep_two, send_two, norms_two = run_middle(
            counts, (came_x, None), (came_cot, None), *shared, 0, None, groups
        )
    came_d = exchange(dealt_d[0], "feat")
    parts_two = plane_parts(reduce_core(keep_two, send_two))
    came_d, _ = lax.optimization_barrier((came_d, parts_two))
    if groups == 2:
        dealt_d[1], came_d = lax.optimization_barrier((dealt_d[1], came_d))
        came_last = exchange(dealt_d[1], "feat")
        held = run_sample_backward(
            counts, came_both, came_d, saved, weights, norm_params, chips, 0, None, False
        )
        came_d, held, parts_two[0] = lax.optimization_barrier((came_last, held, parts_two[0]))
    else:
        held = None
    part_two, came_d = lax.optimization_barrier((reduce_plane(parts_two), came_d))
    came_two = exchange(part_two, "feat", [list(range(side, devices, 2)) for side in range(2)])
    input_grad, keep_one, send_one, norms_one = run_sample_backward(
        counts,
        came_both,
        came_d,
        saved,
        weights,
        norm_params,
        chips,
        0 if held is None else local // 2,
        held,
        True,
    )
    came_two, input_grad, keep_one, send_one, norms_one = lax.optimization_barrier(
        (came_two, input_grad, keep_one, send_one, norms_one)
    )
    share_two = jnp.sum(came_two.astype(F32), axis=0)
    share_one = reduce_layers(layer_parts(reduce_plane(plane_parts(reduce_core(keep_one, send_one)))))
    share_in_turned = share_two[:own_ff]
    share_out = share_two[own_ff : 2 * own_ff]
    share_one, dealt_y = lax.optimization_barrier((share_one, dealt_y))
    came_y = exchange(dealt_y, "feat")
    local_squares = jnp.sum(share_one * share_one) + jnp.sum(share_two * share_two)
    small = jnp.concatenate(
        [norms_one, norms_two, jnp.full((2, width), local_squares, F32)], axis=0
    )
    small, part_one, part_two = lax.optimization_barrier(
        (small, share_one, share_two[2 * own_ff :])
    )
    share_attn = to_owners(part_one, part_two)
    small, share_attn, came_y = lax.optimization_barrier((total_of(small), share_attn, came_y))
    total_norms = small[:6]
    squares = small[6, 0] + jnp.sum(total_norms * total_norms)
    grad_norm = jnp.sqrt(squares)
    factor = jnp.minimum(1.0, CLIP_AT / (grad_norm + 1e-06))
    new_attn, moment_attn, square_attn = adam_step(
        master_attn, factor * share_attn, first_attn, second_attn, RATE
    )
    new_in, moment_in, square_in = adam_step(
        master_in, factor * share_in_turned.T, first_in, second_in, RATE
    )
    new_out, moment_out, square_out = adam_step(
        master_out, factor * share_out, first_out, second_out, RATE
    )
    new_norms, moment_norms, square_norms = adam_step(
        norm_params, factor * total_norms, first_norms, second_norms, NORM_RATE
    )
    own_both = jnp.concatenate([new_in.astype(BF).T, new_out.astype(BF)], axis=0)
    nears, fars = gather_layers(new_attn.astype(BF), own_both)
    came_halves = [came_y] if came_both is None else [came_both, came_y]
    copy_attn, copy_in, copy_out, block_out = gather_rest(nears, fars, came_halves)
    block_out = block_out.reshape(1, local, samples, width)
    return (
        block_out,
        input_grad[None],
        grad_norm.reshape(1),
        new_attn,
        new_in,
        new_out,
        new_norms,
        moment_attn,
        moment_in,
        moment_out,
        moment_norms,
        square_attn,
        square_in,
        square_out,
        square_norms,
        copy_attn,
        copy_in,
        copy_out,
    )


def solution(mesh):
    cells = P("task", "feat", None, None)
    rows = P(("task", "feat"), None)
    columns = P(None, ("task", "feat"))
    return jax.shard_map(
        shards,
        mesh=mesh,
        in_specs=(cells, cells, P(), P(), P(), P())
        + (rows, columns, rows)
        + (rows, columns, rows, P())
        + (rows, columns, rows, P())
        + (P("task"), P("task")),
        out_specs=(cells, cells, P())
        + (rows, columns, rows, P())
        + (rows, columns, rows, P())
        + (rows, columns, rows, P())
        + (P(), P(), P()),
        check_vma=False,
    )
```

```python
import functools

import jax
import jax.numpy as jnp
from jax import lax
from jax.experimental import pallas as pl
from jax.experimental.pallas import tpu as pltpu
from jax.sharding import PartitionSpec as P

HEADS = 8
STEP = 5
NEGATIVE = -1e30
LN_EPS = 1e-05
CLIP_AT = 1.0
BETA_ONE = 0.9
BETA_TWO = 0.999
RATE = 0.02
NORM_RATE = 0.25
DECAY = 0.1
ADAM_EPS = 1e-08

BLOCK = 16
UNIT = 128
ROWS = 128
QUERIES = 512
UNROLL = 2
VMEM_BYTES = 60 * 1024 * 1024

BF = jnp.bfloat16
F32 = jnp.float32
NN = ((1,), (0,))
NT = ((1,), (1,))
TN = ((0,), (0,))


def dot(left, right, dims=NN):
    return lax.dot_general(left, right, (dims, ((), ())), preferred_element_type=F32)


def normalize(values):
    center = jnp.mean(values, axis=-1, keepdims=True)
    centred = values - center
    spread = jnp.mean(centred * centred, axis=-1, keepdims=True)
    scale = lax.rsqrt(spread + LN_EPS)
    return centred * scale, scale


def normalize_back(normal, scale, grad, gain):
    d_normal = grad * gain
    mean_one = jnp.mean(d_normal, axis=-1, keepdims=True)
    mean_two = jnp.mean(d_normal * normal, axis=-1, keepdims=True)
    return scale * (d_normal - mean_one - normal * mean_two)


def column_sum(values):
    return jnp.sum(values, axis=0, keepdims=True)


def by_unit(units, one):
    parts = [one(slice(place * UNIT, (place + 1) * UNIT)) for place in range(units)]
    return jnp.concatenate(parts, axis=1)


def scaled(values, head_size):
    return (values.astype(BF).astype(F32) * head_size ** (-0.5)).astype(BF)


def block_of(place, size):
    return pl.ds(pl.multiple_of(place * size, size), size)


def row_index(shape):
    return lax.broadcasted_iota(jnp.int32, shape, 0)


def sample_forward(late, counts, tokens, cotangent, weights, norms, x_out, *rest):
    if late:
        late_out, *rest = rest
    first_out, heads_out, mixed_out, log_out, turned = rest
    samples, width = tokens.shape[1:]
    head_size = width // HEADS
    early = x_out.shape[1]
    dealt = (x_out.shape[0], BLOCK, width)
    group = dealt[0] * BLOCK

    @pl.when(pl.program_id(0) == 0)
    def _():
        for which in range(3):
            turned[which] = weights[which].T

    for low in range(0, samples, ROWS):
        rows = slice(low, low + ROWS)
        normal, _ = normalize(tokens[0, rows].astype(F32))
        first_out[0, rows] = (normal * norms[0:1] + norms[1:2]).astype(BF)
    first = first_out[0]
    heads_out[0, 0] = scaled(dot(turned[0], first, NT), head_size)
    for which in range(1, 3):
        heads_out[0, which] = dot(turned[which], first, NT).astype(BF)
    live = row_index((samples, 1)) < counts[0]
    for head in range(HEADS):
        lanes = slice(head * head_size, (head + 1) * head_size)
        keys = heads_out[0, 1, lanes]
        values = heads_out[0, 2, lanes]
        for low in range(0, samples, QUERIES):
            cols = slice(low, low + QUERIES)
            scores = dot(keys, heads_out[0, 0, lanes, cols], TN)
            scores = jnp.where(live, scores, NEGATIVE)
            top = jnp.max(scores, axis=0, keepdims=True)
            powers = jnp.exp(scores - top)
            total = jnp.sum(powers, axis=0, keepdims=True)
            mixed = dot(values, powers.astype(BF)) * (1.0 / total)
            mixed_out[0, lanes, cols] = mixed.astype(BF)
            log_out[0, head : head + 1, cols] = top + jnp.log(total)
    for low in range(0, samples, group):
        rows = slice(low, low + group)
        part = tokens[0, rows].astype(F32) + dot(mixed_out[0, :, rows], weights[3], TN)
        part = part.astype(BF).reshape(dealt)
        if low // group < early:
            x_out[:, low // group, 0] = part
        else:
            late_out[:, 0, low // group - early, 0] = part
            late_out[:, 1, low // group - early, 0] = cotangent[0, rows].reshape(dealt)


def sample_backward(offset, early, opening, closing, counts, *refs):
    if early:
        d_early, *refs = refs
    d_late, tokens, first, heads, mixed, logs, weights, norms, *refs = refs
    if not opening:
        _, total_in, norm_total_in, *refs = refs
    grad_out, *refs = refs
    if closing:
        keep_out, send_out, norm_out, *refs = refs
    else:
        total_out, norm_out, *refs = refs
    d_rows, d_mix, d_heads, d_turned, total, norm_total = refs
    samples, width = tokens.shape[1:]
    head_size = width // HEADS
    score_scale = head_size ** (-0.5)
    group = d_late.shape[0] * BLOCK
    step = pl.program_id(0)

    @pl.when(step == 0)
    def _():
        if opening:
            total[...] = jnp.zeros_like(total)
            norm_total[...] = jnp.zeros_like(norm_total)
        else:
            total[...] = total_in[...]
            norm_total[...] = norm_total_in[...]

    feature_live = counts[2] + offset + step < counts[1]

    @pl.when(jnp.logical_not(feature_live))
    def _():
        grad_out[...] = jnp.zeros_like(grad_out)

    @pl.when(feature_live)
    def _():
        for low in range(0, samples, group):
            deal = low // group
            part = d_early[:, deal, 0] if deal < early else d_late[:, deal - early, 0]
            d_rows[low : low + group] = part.reshape(group, width)
        d_mix[...] = dot(weights[3], d_rows[...], NT).astype(BF)
        total[3 * width :] += dot(mixed[0], d_rows[...])
        live = row_index((samples, 1)) < counts[0]
        for pair in range(0, HEADS, 2):
            d_keys, d_values = [], []
            for head in (pair, pair + 1):
                lanes = slice(head * head_size, (head + 1) * head_size)
                keys = heads[0, 1, lanes]
                values = heads[0, 2, lanes]
                queries = heads[0, 0, lanes]
                grads = d_mix[lanes]
                shared = column_sum(grads.astype(F32) * mixed[0, lanes].astype(F32))
                scores = dot(keys, queries, TN)
                scores = jnp.where(live, scores, NEGATIVE)
                probs = jnp.exp(scores - logs[0, head : head + 1])
                d_probs = dot(values, grads, TN)
                d_scores = (probs * (d_probs - shared)).astype(BF)
                d_heads[lanes] = (dot(keys, d_scores) * score_scale).astype(BF)
                d_keys.append(dot(d_scores, queries, NT).astype(BF))
                d_values.append(dot(probs.astype(BF), grads, NT).astype(BF))
            lanes = slice(pair * head_size, (pair + 2) * head_size)
            d_turned[1, :, lanes] = jnp.concatenate(d_keys, axis=1)
            d_turned[2, :, lanes] = jnp.concatenate(d_values, axis=1)
        d_turned[0] = d_heads[...].T
        for which in range(3):
            total[which * width : (which + 1) * width] += dot(first[0], d_turned[which], TN)
        for low in range(0, samples, ROWS):
            rows = slice(low, low + ROWS)
            d_first = dot(d_turned[0, rows], weights[0], NT)
            d_first = d_first + dot(d_turned[1, rows], weights[1], NT)
            d_first = d_first + dot(d_turned[2, rows], weights[2], NT)
            normal, scale = normalize(tokens[0, rows].astype(F32))
            norm_total[0:1] += column_sum(d_first * normal)
            norm_total[1:2] += column_sum(d_first)
            back = normalize_back(normal, scale, d_first, norms[0:1])
            grad_out[0, rows] = (d_rows[rows].astype(F32) + back).astype(BF)

    @pl.when(step == pl.num_programs(0) - 1)
    def _():
        if closing:
            attention_parts(keep_out, total, counts[4], 0)
            attention_parts(send_out, total, 1 - counts[4], 0)
        else:
            total_out[...] = total[...]
        norm_out[...] = norm_total[...]


def gelu_parts(pre):
    root = 0.7978845608028654
    square = pre * pre
    curve = jnp.tanh(root * pre * (1.0 + 0.044715 * square))
    half = 0.5 * (1.0 + curve)
    slope = half + (0.5 * root) * pre * (1.0 - curve * curve) * (1.0 + 3 * 0.044715 * square)
    return pre * half, slope


def part_of(total, chip, core, owners, rows):
    start = pl.multiple_of((chip * 2 + core) * (owners * rows), owners * rows)
    part = total[pl.ds(start, owners * rows)].astype(BF)
    return part.reshape(owners, rows, part.shape[-1])


def attention_parts(where, total, core, low):
    chips, owners = where.shape[:2]
    half = total.shape[0] // (2 * chips * owners)
    for pair in range(chips // 2):
        part = part_of(total, pair, core, owners, 2 * half)
        for piece in range(2):
            rows = part[:, piece * half : (piece + 1) * half]
            where[2 * pair + piece, :, low : low + half] = rows


def middle(offset, opening, closing, groups, counts, *refs):
    refs = list(refs)

    def take(count):
        return [refs.pop(0) for _ in range(count)]

    x_in, cot_in, weights, weight_in, weight_out, norms = take(6)
    if not opening:
        held = take(3)
        (norm_held,) = take(1)
    if closing:
        d_outs = take(groups)
        y_out, keep_out, send_out, norm_out = take(4)
    else:
        (both_out,) = take(1)
        given = take(3)
        (norm_out,) = take(1)
    turned, order, back_order, x_one, normal_one, scale_one, normal_two, scale_two = take(8)
    x_two, low_rows, heads, d_heads, d_turned, mixed, d_mix, probs, live_grad = take(9)
    third, grad_rows, *totals, norm_total, copied = take(7)
    total_attn, total_in, total_out = totals
    if not opening:
        loads = [
            pltpu.make_async_copy(source, target, copied.at[place])
            for place, (source, target) in enumerate(zip(held, totals))
        ]
    devices, _, local, _, width = x_in.shape
    features = devices * local
    cells = features * BLOCK
    head_size = width // HEADS
    score_scale = head_size ** (-0.5)
    hidden_width = weight_in.shape[1]
    step = pl.program_id(0)
    first_sample = ((offset + step) * devices + counts[3]) * BLOCK

    @pl.when(step == 0)
    def _():
        if not opening:
            for load in loads:
                load.start()
        for which in range(3):
            turned[which] = weights[which].T
        here = row_index((cells, cells))
        there = lax.broadcasted_iota(jnp.int32, (cells, cells), 1)
        source = (here % features) * BLOCK + here // features
        order[...] = jnp.where(source == there, 1.0, 0.0).astype(BF)
        source = (here % BLOCK) * features + here // BLOCK
        back_order[...] = jnp.where(source == there, 1.0, 0.0).astype(BF)
        if opening:
            for total in totals:
                total[...] = jnp.zeros_like(total)
            norm_total[...] = jnp.zeros_like(norm_total)
        else:
            norm_total[...] = norm_held[...]

    x_one[...] = dot(order[...], x_in[:, 0].reshape(cells, width))
    for low in range(0, cells, ROWS):
        rows = slice(low, low + ROWS)
        normal, scale = normalize(x_one[rows])
        normal_one[rows] = normal
        scale_one[rows] = scale
        low_rows[rows] = (normal * norms[2:3] + norms[3:4]).astype(BF)
    heads[0] = scaled(dot(turned[0], low_rows[...], NT), head_size)
    for which in range(1, 3):
        heads[which] = dot(turned[which], low_rows[...], NT).astype(BF)

    units = cells // UNIT
    key_row = row_index((UNIT, cells))
    query_row = lax.broadcasted_iota(jnp.int32, (UNIT, cells), 1) % UNIT
    mask = (key_row // features == query_row // features) & (key_row % features < counts[1])
    for head in range(HEADS):
        lanes = slice(head * head_size, (head + 1) * head_size)
        scores = by_unit(units, lambda cols: dot(heads[1, lanes, cols], heads[0, lanes, cols], TN))
        scores = jnp.where(mask, scores, NEGATIVE)
        top = jnp.max(scores, axis=0, keepdims=True)
        powers = jnp.exp(scores - top)
        total = jnp.sum(powers, axis=0, keepdims=True)
        prob = powers * (1.0 / total)
        probs[head] = prob
        prob = prob.astype(BF)
        mixed[lanes] = by_unit(units, lambda cols: dot(heads[2, lanes, cols], prob[:, cols])).astype(BF)
    for low in range(0, cells, ROWS):
        rows = slice(low, low + ROWS)
        part = x_one[rows] + dot(mixed[:, rows], weights[3], TN)
        x_two[rows] = part
        normal, scale = normalize(part)
        normal_two[rows] = normal
        scale_two[rows] = scale
        third[rows] = (normal * norms[4:5] + norms[5:6]).astype(BF)

    if not opening:

        @pl.when(step == 0)
        def _():
            for load in loads:
                load.wait()

    def write_d(values):
        if not closing:
            both_out[:, 0, 0] = values
            return
        count = local // groups
        for place, d_out in enumerate(d_outs):
            d_out[:, 0] = values[:, place * count : (place + 1) * count]

    alive = first_sample < counts[0]

    @pl.when(jnp.logical_not(alive))
    def _():

        @pl.loop(0, hidden_width // width)
        def _(block):
            cols = block_of(block, width)
            hidden, _ = gelu_parts(dot(third[...], weight_in[:, cols]))
            x_two[...] += dot(hidden.astype(BF), weight_out[cols])

        write_d(jnp.zeros((devices, local, BLOCK, width), BF))

    @pl.when(alive)
    def _():
        place = row_index((cells, 1))
        cell_live = (place % features < counts[1]) & (
            first_sample + place // features < counts[0]
        )
        grads = dot(order[...], cot_in[:, 0].reshape(cells, width))
        live_grad[...] = jnp.where(cell_live, grads, 0.0).astype(BF)
        grad_rows[...] = jnp.zeros_like(grad_rows)

        @pl.loop(0, hidden_width // width)
        def _(block):
            cols = block_of(block, width)
            hidden, slope = gelu_parts(dot(third[...], weight_in[:, cols]))
            hidden = hidden.astype(BF)
            x_two[...] += dot(hidden, weight_out[cols])
            total_out[cols] += dot(hidden, live_grad[...], TN)
            d_pre = (dot(live_grad[...], weight_out[cols], NT) * slope).astype(BF)
            total_in[cols] += dot(d_pre, third[...], TN)
            grad_rows[...] += dot(d_pre, weight_in[:, cols], NT)


        for low in range(0, cells, ROWS):
            rows = slice(low, low + ROWS)
            normal = normal_two[rows]
            d_third = grad_rows[rows]
            norm_total[2:3] += column_sum(d_third * normal)
            norm_total[3:4] += column_sum(d_third)
            back = normalize_back(normal, scale_two[rows], d_third, norms[4:5])
            back = back + live_grad[rows].astype(F32)
            grad_rows[rows] = back
            live_grad[rows] = back.astype(BF)
        d_mix[...] = dot(weights[3], live_grad[...], NT).astype(BF)
        total_attn[3 * width :] += dot(mixed[...], live_grad[...])
        for head in range(HEADS):
            lanes = slice(head * head_size, (head + 1) * head_size)
            prob = probs[head]
            grads = d_mix[lanes]
            shared = column_sum(grads.astype(F32) * mixed[lanes].astype(F32))
            d_probs = by_unit(units, lambda cols: dot(heads[2, lanes, cols], grads[:, cols], TN))
            d_scores = (prob * (d_probs - shared)).astype(BF)
            low_prob = prob.astype(BF)
            d_query = by_unit(units, lambda cols: dot(heads[1, lanes, cols], d_scores[:, cols]))
            d_heads[0, lanes] = (d_query * score_scale).astype(BF)
            d_key = by_unit(units, lambda cols: dot(heads[0, lanes, cols], d_scores[:, cols], NT))
            d_heads[1, lanes] = d_key.astype(BF)
            d_value = by_unit(units, lambda cols: dot(grads[:, cols], low_prob[:, cols], NT))
            d_heads[2, lanes] = d_value.astype(BF)
        for which in range(3):
            d_turned[which] = d_heads[which].T
        for which in range(3):
            total_attn[which * width : (which + 1) * width] += dot(low_rows[...], d_turned[which], TN)
        for low in range(0, cells, ROWS):
            rows = slice(low, low + ROWS)
            d_second = dot(d_turned[0, rows], weights[0], NT)
            d_second = d_second + dot(d_turned[1, rows], weights[1], NT)
            d_second = d_second + dot(d_turned[2, rows], weights[2], NT)
            normal = normal_one[rows]
            norm_total[0:1] += column_sum(d_second * normal)
            norm_total[1:2] += column_sum(d_second)
            back = normalize_back(normal, scale_one[rows], d_second, norms[2:3])
            live_grad[rows] = (grad_rows[rows] + back).astype(BF)
        moved = dot(back_order[...], live_grad[...]).astype(BF)
        write_d(moved.reshape(devices, local, BLOCK, width))

    moved = dot(back_order[...], x_two[...].astype(BF)).astype(BF)
    moved = moved.reshape(devices, local, BLOCK, width)
    if closing:
        y_out[:, 0] = moved
    else:
        both_out[:, 1, 0] = moved

    @pl.when(step == pl.num_programs(0) - 1)
    def _():
        if closing:
            chips, owners, rows, _ = keep_out.shape
            own_ff = hidden_width // (2 * chips * owners)
            for where, core in ((keep_out, counts[4]), (send_out, 1 - counts[4])):
                for chip in range(chips):
                    for which, total in ((0, total_in), (1, total_out)):
                        part = part_of(total, chip, core, owners, own_ff)
                        where[chip, :, which * own_ff : (which + 1) * own_ff] = part
                attention_parts(where, total_attn, core, 2 * own_ff)
        else:
            stores = [
                pltpu.make_async_copy(source, target, copied.at[place])
                for place, (source, target) in enumerate(zip(totals, given))
            ]
            for store in stores:
                store.start()
            for store in stores:
                store.wait()
        norm_out[...] = norm_total[...]


def whole(shape):
    zeros = (0,) * len(shape)
    return pl.BlockSpec(shape, lambda step: zeros, pipeline_mode=pl.Buffered(1))


def half(shape, which):
    return pl.BlockSpec(
        (shape[0] // 2,) + tuple(shape[1:]),
        lambda step: (which, 0, 0),
        pipeline_mode=pl.Buffered(1),
    )


def once(shape):
    zeros = (0,) * len(shape)
    return pl.BlockSpec(shape, lambda step: zeros)


def lead(shape):
    zeros = (0,) * (len(shape) - 1)
    return pl.BlockSpec((1,) + tuple(shape[1:]), lambda step: (step,) + zeros)


def call(body, grid, ins, outs, scratch, nanoseconds, name, aliases=None):
    return pl.pallas_call(
        body,
        grid=(grid,),
        in_specs=[pl.BlockSpec(memory_space=pltpu.SMEM)] + [spec for spec, _ in ins[1:]],
        out_specs=[spec for spec, _, _ in outs],
        out_shape=[jax.ShapeDtypeStruct(shape, kind) for _, shape, kind in outs],
        scratch_shapes=[
            pltpu.SemaphoreType.DMA((3,)) if kind is None else pltpu.VMEM(shape, kind)
            for shape, kind in scratch
        ],
        input_output_aliases=aliases or {},
        compiler_params=pltpu.CompilerParams(vmem_limit_bytes=VMEM_BYTES),
        cost_estimate=pl.CostEstimate(
            flops=nanoseconds * 1150000, bytes_accessed=1 << 24, transcendentals=0
        ),
        name=name,
    )(ins[0][1], *[value for _, value in ins[1:]])


ANYWHERE = pl.BlockSpec(memory_space=pl.ANY)


def run_sample_forward(counts, tokens, cotangent, weights, norms, devices, early):
    local, samples, width = tokens.shape
    late = samples // (devices * BLOCK) - early
    square = (local, samples, width)
    three = (local, 3, width, samples)
    stats = (local, HEADS, samples)
    outs = [
        (
            pl.BlockSpec((devices, early, 1, BLOCK, width), lambda step: (0, 0, step, 0, 0)),
            (devices, early, local, BLOCK, width),
            BF,
        )
    ]
    if late:
        outs.append(
            (
                pl.BlockSpec(
                    (devices, 2, late, 1, BLOCK, width), lambda step: (0, 0, 0, step, 0, 0)
                ),
                (devices, 2, late, local, BLOCK, width),
                BF,
            )
        )
    outs = outs + [
        (lead(square), square, BF),
        (lead(three), three, BF),
        (lead(square), (local, width, samples), BF),
        (lead(stats), stats, F32),
    ]
    return call(
        functools.partial(sample_forward, late),
        local,
        [
            (None, counts),
            (lead(square), tokens),
            (lead(square), cotangent),
            (half(weights.shape, 0), weights),
            (whole(norms.shape), norms),
        ],
        outs,
        [((3, width, width), BF)],
        25000,
        "sample_forward",
    )


def run_middle(counts, x_dealt, cot_dealt, weights, weight_in, weight_out, norms, chips, offset, held, groups):
    array, which = x_dealt
    devices = array.shape[0]
    deals, local, _, width = array.shape[-4:]
    cells = devices * local * BLOCK
    hidden_width = weight_in.shape[1]
    parts = (chips, devices, (hidden_width + 2 * width) // (chips * devices), width)

    def dealt(which):
        if which is None:
            return pl.BlockSpec(
                (devices, 1, local, BLOCK, width), lambda step: (0, step, 0, 0, 0)
            )
        return pl.BlockSpec(
            (devices, None, 1, local, BLOCK, width),
            lambda step: (0, which, step, 0, 0, 0),
        )

    ins = [
        (None, counts),
        (dealt(x_dealt[1]), x_dealt[0]),
        (dealt(cot_dealt[1]), cot_dealt[0]),
        (half(weights.shape, 1), weights),
        (whole(weight_in.shape), weight_in),
        (whole(weight_out.shape), weight_out),
        (whole(norms.shape), norms),
    ]
    sums = [(4 * width, width), (hidden_width, width), (hidden_width, width)]
    norm_sums = (4, width)
    if held is not None:
        ins = ins + [(ANYWHERE, value) for value in held[:3]] + [(whole(norm_sums), held[3])]
    if groups:
        few = (devices, deals, local // groups, BLOCK, width)
        piece = pl.BlockSpec((devices, 1) + few[2:], lambda step: (0, step, 0, 0, 0))
        outs = [(piece, few, BF)] * groups + [
            (dealt(None), (devices, deals, local, BLOCK, width), BF),
            (once(parts), parts, BF),
            (once(parts), parts, BF),
        ]
    else:
        outs = [
            (
                pl.BlockSpec(
                    (devices, 2, 1, local, BLOCK, width), lambda step: (0, 0, step, 0, 0, 0)
                ),
                (devices, 2, deals, local, BLOCK, width),
                BF,
            )
        ] + [(ANYWHERE, shape, F32) for shape in sums]
    outs.append((once(norm_sums), norm_sums, F32))
    square = (cells, width)
    turned = (width, cells)
    return call(
        functools.partial(middle, offset, held is None, bool(groups), groups),
        deals,
        ins,
        outs,
        [
            ((3, width, width), BF),
            ((cells, cells), BF),
            ((cells, cells), BF),
            (square, F32),
            (square, F32),
            ((cells, 1), F32),
            (square, F32),
            ((cells, 1), F32),
            (square, F32),
            (square, BF),
            ((3,) + turned, BF),
            ((3,) + turned, BF),
            ((3,) + square, BF),
            (turned, BF),
            (turned, BF),
            ((HEADS, UNIT, cells), F32),
            (square, BF),
            (square, BF),
            (square, F32),
        ]
        + [(shape, F32) for shape in sums]
        + [(norm_sums, F32), ((3,), None)],
        deals * 23000,
        "middle",
    )


def run_sample_backward(counts, d_early, d_late, saved, weights, norms, chips, offset, held, closing):
    devices, late, count, _, width = d_late.shape
    tokens = saved[0]
    local, samples, _ = tokens.shape
    early = 0 if d_early is None else d_early.shape[2]
    parts = (chips, devices, 4 * width // (2 * chips * devices), width)

    def moved(shape):
        zeros = (0,) * (len(shape) - 1)
        return pl.BlockSpec((1,) + tuple(shape[1:]), lambda step: (step + offset,) + zeros)

    ins = [(None, counts)]
    if early:
        ins.append(
            (
                pl.BlockSpec(
                    (devices, None, early, 1, BLOCK, width),
                    lambda step: (0, 0, 0, step + offset, 0, 0),
                ),
                d_early,
            )
        )
    ins.append(
        (
            pl.BlockSpec((devices, late, 1, BLOCK, width), lambda step: (0, 0, step, 0, 0)),
            d_late,
        )
    )
    ins = ins + [(moved(value.shape), value) for value in saved]
    ins = ins + [(half(weights.shape, 0), weights), (whole(norms.shape), norms)]
    sums, norm_sums = (4 * width, width), (2, width)
    aliases = {}
    if held is not None:
        aliases = {len(ins): 0}
        ins = ins + [(ANYWHERE, held[0]), (whole(sums), held[1]), (whole(norm_sums), held[2])]
    outs = [(moved(tokens.shape), tokens.shape, BF)]
    if closing:
        outs = outs + [(once(parts), parts, BF), (once(parts), parts, BF)]
    else:
        outs = outs + [(once(sums), sums, F32)]
    outs.append((once(norm_sums), norm_sums, F32))
    return call(
        functools.partial(sample_backward, offset, early, held is None, closing),
        count,
        ins,
        outs,
        [
            ((samples, width), BF),
            ((width, samples), BF),
            ((width, samples), BF),
            ((3, samples, width), BF),
            (sums, F32),
            (norm_sums, F32),
        ],
        count * 11000,
        "sample_backward",
        aliases,
    )


def adam_step(weight, grad, first_m, second_m, rate):
    moment = BETA_ONE * first_m + (1.0 - BETA_ONE) * grad
    square = BETA_TWO * second_m + (1.0 - BETA_TWO) * grad * grad
    fix_one = 1.0 - BETA_ONE**STEP
    fix_two = 1.0 - BETA_TWO**STEP
    fresh = weight - rate * (
        moment / fix_one / (jnp.sqrt(square / fix_two) + ADAM_EPS) + DECAY * weight
    )
    return (fresh, moment, square)


def exchange(values, axis, groups=None):
    return lax.all_to_all(values, axis, 0, 0, axis_index_groups=groups, tiled=True)


def moved_by(values, axis, hop):
    pairs = [(place, hop(place)) for place in range(lax.axis_size(axis))]
    return lax.ppermute(values, axis, pairs)


def other_core(values):
    return moved_by(values, "task", lambda place: place ^ 1)


def along_y(values, shift):
    tasks = lax.axis_size("task")
    return moved_by(values, "task", lambda place: (place + 2 * shift) % tasks)


def along_x(values):
    return moved_by(values, "feat", lambda place: place ^ 1)


def along_z(values, shift):
    devices = lax.axis_size("feat")
    return moved_by(values, "feat", lambda place: (place + 2 * shift) % devices)


def reduce_core(keep, send):
    came = other_core(send)
    return (keep.astype(F32) + came.astype(F32)).astype(BF)


def in_plane(values, up, across):
    tasks, devices = lax.axis_size("task"), lax.axis_size("feat")
    pairs = [
        (task * devices + place, (task + 2 * up) % tasks * devices + (place ^ across))
        for task in range(tasks)
        for place in range(devices)
    ]
    return lax.ppermute(values, ("task", "feat"), pairs)


def plane_parts(values):
    chips, devices = values.shape[:2]
    values = values.reshape((chips, devices // 2, 2) + values.shape[2:])
    chip, side = lax.axis_index("task") // 2, lax.axis_index("feat") % 2
    parts = []
    for up in range(chips):
        part = lax.dynamic_index_in_dim(values, (chip + up) % chips, 0, keepdims=False)
        for across in range(2):
            parts.append(lax.dynamic_index_in_dim(part, side ^ across, 1, keepdims=False))
    return parts


def reduce_plane(parts):
    total = parts[0].astype(F32)
    for place, part in enumerate(parts[1:], 1):
        total = total + in_plane(part, place // 2, place % 2).astype(F32)
    return total.astype(BF)


def layer_parts(values):
    layers = values.shape[0]
    layer = lax.axis_index("feat") // 2
    return [
        lax.dynamic_index_in_dim(values, (layer + shift) % layers, 0, keepdims=False)
        for shift in range(layers)
    ]


def reduce_layers(parts):
    total = parts[0].astype(F32)
    for shift, part in enumerate(parts[1:], 1):
        total = total + along_z(part, shift).astype(F32)
    return total


def to_owners(one, two):
    chips = lax.axis_size("task") // 2
    chip = lax.axis_index("task") // 2
    even = chip % 2 == 0
    stay, leave = jnp.where(even, one, two), jnp.where(even, two, one)

    def target(chip, second):
        return chip // 2 + (chips // 2 if second else 0)

    def send(values, odd_second):
        return moved_by(
            values,
            "task",
            lambda place: 2 * target(place // 2, (place // 2 % 2 == 1) == odd_second) + place % 2,
        )

    if chips > 2:
        stay = send(stay, True)
    leave = send(leave, False)
    early = chip < chips // 2
    return jnp.concatenate(
        [jnp.where(early, stay, leave), jnp.where(early, leave, stay)], axis=0
    )


def place_copies(chips, layers, table, *refs):
    count = 2 * chips
    near, far = refs[:count], refs[count : count + 4]
    *halves, attn_out, in_out, out_out, block_out, pair, copied = refs[count + 4 :]
    step = pl.program_id(0)
    moves = []
    for half in halves:
        for deal in range(half.shape[-4]):
            for feature in range(half.shape[-3]):
                index = (slice(None),) + (1,) * (len(half.shape) - 5) + (deal, feature)
                place = len(moves)
                target = block_out.at[feature, place // half.shape[-3]]
                moves.append(pltpu.make_async_copy(half.at[index], target, copied.at[place]))

    @pl.when(step == 0)
    def _():
        for move in moves:
            move.start()
    side, layer = table[count], table[count + 1]
    rows = near[0].shape[2]
    half = far[0].shape[1] // 2

    def owner(other, behind):
        return ((layer + layers - behind) % layers) * 2 + (side ^ other)

    for place in range(count):

        @pl.when(step == place)
        def _():
            core, chip = place // chips, place % chips
            for other in range(2):
                for behind in range(layers):
                    at = owner(other, behind)
                    attn_out[block_of(at, rows)] = near[place][other, behind]
                    part = far[core * 2 + other]
                    pair[block_of(at, half)] = part[chip * layers + behind, :half]
                    out_out[block_of(at, half)] = part[chip * layers + behind, half:]

    in_out[...] = pair[...].T

    @pl.when(step == count - 1)
    def _():
        for move in moves:
            move.wait()


def gather_layers(own_attn, own_ff):
    layers = lax.axis_size("feat") // 2
    nears = [own_attn] + [along_z(own_attn, shift) for shift in range(1, layers)]
    fars = [own_ff] + [along_z(own_ff, shift) for shift in range(1, layers)]
    return jnp.stack(nears), jnp.stack(fars)


def gather_rest(nears, fars, came_halves):
    layers, rows_near, width = nears.shape
    rows_far = fars.shape[1]
    chips = lax.axis_size("task") // 2
    task, place = lax.axis_index("task"), lax.axis_index("feat")
    near = jnp.stack([nears, along_x(nears)])
    far = jnp.concatenate([fars] + [along_y(fars, shift) for shift in range(1, chips)])
    nears = [near] + [along_y(near, shift) for shift in range(1, chips)]
    fars = [far, along_x(far)]
    nears = nears + [other_core(value) for value in nears]
    fars = fars + [other_core(value) for value in fars]
    steps = jnp.arange(2 * chips, dtype=jnp.int32)
    chip = (task // 2 - steps) % chips
    core = (task % 2) ^ (steps // chips)
    table = jnp.concatenate([chip * 2 + core, jnp.stack([place % 2, place // 2])])
    total = 2 * chips
    owned = 2 * layers
    devices, _, local, _, _ = came_halves[-1].shape
    deals = sum(value.shape[-4] for value in came_halves)

    def held(value):
        zeros = (0,) * value.ndim
        return pl.BlockSpec(
            value.shape, lambda step, table: zeros, pipeline_mode=pl.Buffered(1)
        )

    return pl.pallas_call(
        functools.partial(place_copies, chips, layers),
        grid_spec=pltpu.PrefetchScalarGridSpec(
            num_scalar_prefetch=1,
            grid=(total,),
            in_specs=[held(value) for value in nears + fars] + [ANYWHERE] * len(came_halves),
            out_specs=[
                pl.BlockSpec((owned * rows_near, width), lambda step, table: (table[step], 0)),
                pl.BlockSpec(
                    (width, owned * rows_far // 2), lambda step, table: (0, table[step])
                ),
                pl.BlockSpec(
                    (owned * rows_far // 2, width), lambda step, table: (table[step], 0)
                ),
                ANYWHERE,
            ],
            scratch_shapes=[
                pltpu.VMEM((owned * rows_far // 2, width), BF),
                pltpu.SemaphoreType.DMA((deals * local,)),
            ],
        ),
        out_shape=[
            jax.ShapeDtypeStruct((total * owned * rows_near, width), BF),
            jax.ShapeDtypeStruct((width, total * owned * rows_far // 2), BF),
            jax.ShapeDtypeStruct((total * owned * rows_far // 2, width), BF),
            jax.ShapeDtypeStruct((local, deals, devices, BLOCK, width), BF),
        ],
        compiler_params=pltpu.CompilerParams(vmem_limit_bytes=40 * 1024 * 1024),
        name="place_copies",
    )(table.astype(jnp.int32), *nears, *fars, *came_halves)


def total_of(values):
    values = values + other_core(values)
    chips = lax.axis_size("task") // 2
    values = sum([along_y(values, shift) for shift in range(1, chips)], values)
    bit = 1
    while bit < lax.axis_size("feat"):
        values = values + moved_by(values, "feat", lambda place: place ^ bit)
        bit *= 2
    return values


def shards(
    tokens,
    cotangent,
    attn_weights,
    weight_in,
    weight_out,
    norm_params,
    master_attn,
    master_in,
    master_out,
    first_attn,
    first_in,
    first_out,
    first_norms,
    second_attn,
    second_in,
    second_out,
    second_norms,
    sample_count,
    feature_count,
):
    local, samples, width = tokens.shape[1:]
    devices = lax.axis_size("feat")
    tasks = lax.axis_size("task")
    chips = tasks // 2
    place = lax.axis_index("feat")
    deals = samples // (devices * BLOCK)
    counts = jnp.stack(
        [sample_count[0], feature_count[0], place * local, place, lax.axis_index("task") % 2]
    ).astype(jnp.int32)
    weights = attn_weights.reshape(8, width, width)

    early = max(deals // 2, 1)
    late = deals - early
    groups = 1
    own_ff = weight_in.shape[1] // (tasks * devices)
    own_attn = attn_weights.shape[0] // (tasks * devices)

    def dealt(values):
        count = values.shape[1] // (devices * BLOCK)
        values = values.reshape(local, count, devices, BLOCK, width)
        return values.transpose(2, 1, 0, 3, 4)

    came_cot = exchange(dealt(cotangent[0, :, : early * devices * BLOCK]), "feat")
    dealt_x, *rest = run_sample_forward(
        counts, tokens[0], cotangent[0], weights, norm_params, devices, early
    )
    came_cot, dealt_x, *rest = lax.optimization_barrier((came_cot, dealt_x, *rest))
    saved = [tokens[0]] + rest[-4:]
    came_x = exchange(dealt_x, "feat")
    shared = (weights, weight_in, weight_out, norm_params, chips)
    came_both = None
    if late:
        dealt_late, came_x = lax.optimization_barrier((rest[0], came_x))
        came_late = exchange(dealt_late, "feat")
        dealt_both, *held = run_middle(
            counts, (came_x, None), (came_cot, None), *shared, 0, None, 0
        )
        *dealt_d, dealt_y, keep_two, send_two, norms_two = run_middle(
            counts, (came_late, 0), (came_late, 1), *shared, early, held, groups
        )
        came_both = exchange(dealt_both, "feat")
        came_both, dealt_d, dealt_y, keep_two, send_two, norms_two = lax.optimization_barrier(
            (came_both, dealt_d, dealt_y, keep_two, send_two, norms_two)
        )
    else:
        *dealt_d, dealt_y, keep_two, send_two, norms_two = run_middle(
            counts, (came_x, None), (came_cot, None), *shared, 0, None, groups
        )
    came_d = exchange(dealt_d[0], "feat")
    parts_two = plane_parts(reduce_core(keep_two, send_two))
    parts_two, dealt_y, came_d = lax.optimization_barrier((parts_two, dealt_y, came_d))
    came_y = exchange(dealt_y, "feat")
    input_grad, keep_one, send_one, norms_one = run_sample_backward(
        counts, came_both, came_d, saved, weights, norm_params, chips, 0, None, True
    )
    parts_two[0], came_y, input_grad, keep_one, send_one, norms_one = lax.optimization_barrier(
        (parts_two[0], came_y, input_grad, keep_one, send_one, norms_one)
    )
    parts_two = layer_parts(reduce_plane(parts_two))
    parts_two, keep_one, send_one = lax.optimization_barrier((parts_two, keep_one, send_one))
    parts_one = layer_parts(reduce_plane(plane_parts(reduce_core(keep_one, send_one))))
    share_two, parts_one = lax.optimization_barrier((reduce_layers(parts_two), parts_one))
    share_one = reduce_layers(parts_one)
    share_in_turned = share_two[:own_ff]
    share_out = share_two[own_ff : 2 * own_ff]
    local_squares = jnp.sum(share_one * share_one) + jnp.sum(share_two * share_two)
    small = jnp.concatenate(
        [norms_one, norms_two, jnp.full((2, width), local_squares, F32)], axis=0
    )
    small, part_one, part_two = lax.optimization_barrier(
        (small, share_one, share_two[2 * own_ff :])
    )
    share_attn = to_owners(part_one, part_two)
    small, share_attn = lax.optimization_barrier((total_of(small), share_attn))
    total_norms = small[:6]
    squares = small[6, 0] + jnp.sum(total_norms * total_norms)
    grad_norm = jnp.sqrt(squares)
    factor = jnp.minimum(1.0, CLIP_AT / (grad_norm + 1e-06))
    new_attn, moment_attn, square_attn = adam_step(
        master_attn, factor * share_attn, first_attn, second_attn, RATE
    )
    new_in, moment_in, square_in = adam_step(
        master_in, factor * share_in_turned.T, first_in, second_in, RATE
    )
    new_out, moment_out, square_out = adam_step(
        master_out, factor * share_out, first_out, second_out, RATE
    )
    new_norms, moment_norms, square_norms = adam_step(
        norm_params, factor * total_norms, first_norms, second_norms, NORM_RATE
    )
    own_both = jnp.concatenate([new_in.astype(BF).T, new_out.astype(BF)], axis=0)
    nears, fars = gather_layers(new_attn.astype(BF), own_both)
    came_halves = [came_y] if came_both is None else [came_both, came_y]
    copy_attn, copy_in, copy_out, block_out = gather_rest(nears, fars, came_halves)
    block_out = block_out.reshape(1, local, samples, width)
    return (
        block_out,
        input_grad[None],
        grad_norm.reshape(1),
        new_attn,
        new_in,
        new_out,
        new_norms,
        moment_attn,
        moment_in,
        moment_out,
        moment_norms,
        square_attn,
        square_in,
        square_out,
        square_norms,
        copy_attn,
        copy_in,
        copy_out,
    )


def solution(mesh):
    cells = P("task", "feat", None, None)
    rows = P(("task", "feat"), None)
    columns = P(None, ("task", "feat"))
    return jax.shard_map(
        shards,
        mesh=mesh,
        in_specs=(cells, cells, P(), P(), P(), P())
        + (rows, columns, rows)
        + (rows, columns, rows, P())
        + (rows, columns, rows, P())
        + (P("task"), P("task")),
        out_specs=(cells, cells, P())
        + (rows, columns, rows, P())
        + (rows, columns, rows, P())
        + (rows, columns, rows, P())
        + (P(), P(), P()),
        check_vma=False,
    )
```

```python
import functools

import jax
import jax.numpy as jnp
from jax import lax
from jax.experimental import pallas as pl
from jax.experimental.pallas import tpu as pltpu
from jax.sharding import PartitionSpec as P

HEADS = 8
STEP = 5
NEGATIVE = -1e30
LN_EPS = 1e-05
CLIP_AT = 1.0
BETA_ONE = 0.9
BETA_TWO = 0.999
RATE = 0.02
NORM_RATE = 0.25
DECAY = 0.1
ADAM_EPS = 1e-08

BLOCK = 16
UNIT = 128
ROWS = 128
QUERIES = 512
UNROLL = 2
VMEM_BYTES = 60 * 1024 * 1024

BF = jnp.bfloat16
F32 = jnp.float32
NN = ((1,), (0,))
NT = ((1,), (1,))
TN = ((0,), (0,))


def dot(left, right, dims=NN):
    return lax.dot_general(left, right, (dims, ((), ())), preferred_element_type=F32)


def normalize(values):
    center = jnp.mean(values, axis=-1, keepdims=True)
    centred = values - center
    spread = jnp.mean(centred * centred, axis=-1, keepdims=True)
    scale = lax.rsqrt(spread + LN_EPS)
    return centred * scale, scale


def normalize_back(normal, scale, grad, gain):
    d_normal = grad * gain
    mean_one = jnp.mean(d_normal, axis=-1, keepdims=True)
    mean_two = jnp.mean(d_normal * normal, axis=-1, keepdims=True)
    return scale * (d_normal - mean_one - normal * mean_two)


def column_sum(values):
    return jnp.sum(values, axis=0, keepdims=True)


def by_unit(units, one):
    parts = [one(slice(place * UNIT, (place + 1) * UNIT)) for place in range(units)]
    return jnp.concatenate(parts, axis=1)


def scaled(values, head_size):
    return (values.astype(BF).astype(F32) * head_size ** (-0.5)).astype(BF)


def block_of(place, size):
    return pl.ds(pl.multiple_of(place * size, size), size)


def row_index(shape):
    return lax.broadcasted_iota(jnp.int32, shape, 0)


def sample_forward(late, counts, tokens, cotangent, weights, norms, x_out, *rest):
    if late:
        late_out, *rest = rest
    first_out, heads_out, mixed_out, log_out, turned = rest
    samples, width = tokens.shape[1:]
    head_size = width // HEADS
    early = x_out.shape[1]
    dealt = (x_out.shape[0], BLOCK, width)
    group = dealt[0] * BLOCK

    @pl.when(pl.program_id(0) == 0)
    def _():
        for which in range(3):
            turned[which] = weights[which].T

    for low in range(0, samples, ROWS):
        rows = slice(low, low + ROWS)
        normal, _ = normalize(tokens[0, rows].astype(F32))
        first_out[0, rows] = (normal * norms[0:1] + norms[1:2]).astype(BF)
    first = first_out[0]
    heads_out[0, 0] = scaled(dot(turned[0], first, NT), head_size)
    for which in range(1, 3):
        heads_out[0, which] = dot(turned[which], first, NT).astype(BF)
    live = row_index((samples, 1)) < counts[0]
    for head in range(HEADS):
        lanes = slice(head * head_size, (head + 1) * head_size)
        keys = heads_out[0, 1, lanes]
        values = heads_out[0, 2, lanes]
        for low in range(0, samples, QUERIES):
            cols = slice(low, low + QUERIES)
            scores = dot(keys, heads_out[0, 0, lanes, cols], TN)
            scores = jnp.where(live, scores, NEGATIVE)
            top = jnp.max(scores, axis=0, keepdims=True)
            powers = jnp.exp(scores - top)
            total = jnp.sum(powers, axis=0, keepdims=True)
            mixed = dot(values, powers.astype(BF)) * (1.0 / total)
            mixed_out[0, lanes, cols] = mixed.astype(BF)
            log_out[0, head : head + 1, cols] = top + jnp.log(total)
    for low in range(0, samples, group):
        rows = slice(low, low + group)
        part = tokens[0, rows].astype(F32) + dot(mixed_out[0, :, rows], weights[3], TN)
        part = part.astype(BF).reshape(dealt)
        if low // group < early:
            x_out[:, low // group, 0] = part
        else:
            late_out[:, 0, low // group - early, 0] = part
            late_out[:, 1, low // group - early, 0] = cotangent[0, rows].reshape(dealt)


def heads_back(heads, mixed, logs, d_mix, rows, live, d_query, add):
    width = d_mix.shape[0]
    head_size = width // HEADS
    for pair in range(0, HEADS, 2):
        d_keys, d_values = [], []
        for head in (pair, pair + 1):
            lanes = slice(head * head_size, (head + 1) * head_size)
            keys = heads[0, 1, lanes]
            values = heads[0, 2, lanes]
            queries = heads[0, 0, lanes, rows]
            grads = d_mix[lanes]
            shared = column_sum(grads.astype(F32) * mixed[0, lanes, rows].astype(F32))
            scores = jnp.where(live, dot(keys, queries, TN), NEGATIVE)
            probs = jnp.exp(scores - logs[0, head : head + 1, rows])
            d_probs = dot(values, grads, TN)
            d_scores = (probs * (d_probs - shared)).astype(BF)
            d_query[lanes] = (dot(keys, d_scores) * head_size ** (-0.5)).astype(BF)
            d_keys.append(dot(d_scores, queries, NT))
            d_values.append(dot(probs.astype(BF), grads, NT))
        lanes = slice(pair * head_size, (pair + 2) * head_size)
        add(lanes, jnp.concatenate(d_keys, axis=1), jnp.concatenate(d_values, axis=1))


def sample_backward_early(
    counts, d_early, heads, mixed, logs, weights, query_out, sums_out, weight_out, d_rows, d_mix, d_query, total
):
    samples = mixed.shape[2]
    width = d_mix.shape[0]
    group = d_early.shape[0] * BLOCK
    rows = slice(0, d_rows.shape[0])
    step = pl.program_id(0)

    @pl.when(step == 0)
    def _():
        total[...] = jnp.zeros_like(total)

    @pl.when(counts[2] + step < counts[1])
    def _():
        for deal in range(d_early.shape[1]):
            part = d_early[:, deal, 0].reshape(group, width)
            d_rows[deal * group : (deal + 1) * group] = part
        d_mix[...] = dot(weights[3], d_rows[...], NT).astype(BF)
        total[...] += dot(mixed[0, :, rows], d_rows[...])
        live = row_index((samples, 1)) < counts[0]

        def add(lanes, d_keys, d_values):
            sums_out[0, 0, :, lanes] = d_keys
            sums_out[0, 1, :, lanes] = d_values

        heads_back(heads, mixed, logs, d_mix, rows, live, d_query, add)
        query_out[0] = d_query[...].T

    @pl.when(step == pl.num_programs(0) - 1)
    def _():
        weight_out[...] = total[...]


def sample_backward(early, counts, *refs):
    if early:
        d_early, query_held, sums_held, weight_held, *refs = refs
    d_late, tokens, first, heads, mixed, logs, weights, norms, *refs = refs
    grad_out, keep_out, send_out, norm_out, d_rows, d_mix, d_query, d_turned, total, norm_total = refs
    samples, width = tokens.shape[1:]
    group = d_late.shape[0] * BLOCK
    start = early * group
    rows = slice(start, samples)
    step = pl.program_id(0)

    @pl.when(step == 0)
    def _():
        total[...] = jnp.zeros_like(total)
        if early:
            total[3 * width :] = weight_held[...]
        norm_total[...] = jnp.zeros_like(norm_total)

    feature_live = counts[2] + step < counts[1]

    @pl.when(jnp.logical_not(feature_live))
    def _():
        grad_out[...] = jnp.zeros_like(grad_out)

    @pl.when(feature_live)
    def _():
        for low in range(0, samples, group):
            deal = low // group
            part = d_early[:, deal, 0] if deal < early else d_late[:, deal - early, 0]
            d_rows[low : low + group] = part.reshape(group, width)
        d_mix[...] = dot(weights[3], d_rows[rows], NT).astype(BF)
        total[3 * width :] += dot(mixed[0, :, rows], d_rows[rows])
        live = row_index((samples, 1)) < counts[0]

        def add(lanes, d_keys, d_values):
            if early:
                d_keys = d_keys + sums_held[0, 0, :, lanes]
                d_values = d_values + sums_held[0, 1, :, lanes]
            d_turned[1, :, lanes] = d_keys.astype(BF)
            d_turned[2, :, lanes] = d_values.astype(BF)

        heads_back(heads, mixed, logs, d_mix, rows, live, d_query, add)
        d_turned[0, rows] = d_query[...].T
        if early:
            d_turned[0, :start] = query_held[0]
        for which in range(3):
            total[which * width : (which + 1) * width] += dot(first[0], d_turned[which], TN)
        for low in range(0, samples, ROWS):
            part = slice(low, low + ROWS)
            d_first = dot(d_turned[0, part], weights[0], NT)
            d_first = d_first + dot(d_turned[1, part], weights[1], NT)
            d_first = d_first + dot(d_turned[2, part], weights[2], NT)
            normal, scale = normalize(tokens[0, part].astype(F32))
            norm_total[0:1] += column_sum(d_first * normal)
            norm_total[1:2] += column_sum(d_first)
            back = normalize_back(normal, scale, d_first, norms[0:1])
            grad_out[0, part] = (d_rows[part].astype(F32) + back).astype(BF)

    @pl.when(step == pl.num_programs(0) - 1)
    def _():
        attention_parts(keep_out, total, counts[4], 0)
        attention_parts(send_out, total, 1 - counts[4], 0)
        norm_out[...] = norm_total[...]


def gelu_parts(pre):
    root = 0.7978845608028654
    square = pre * pre
    curve = jnp.tanh(root * pre * (1.0 + 0.044715 * square))
    half = 0.5 * (1.0 + curve)
    slope = half + (0.5 * root) * pre * (1.0 - curve * curve) * (1.0 + 3 * 0.044715 * square)
    return pre * half, slope


def part_of(total, chip, core, owners, rows):
    start = pl.multiple_of((chip * 2 + core) * (owners * rows), owners * rows)
    part = total[pl.ds(start, owners * rows)].astype(BF)
    return part.reshape(owners, rows, part.shape[-1])


def attention_parts(where, total, core, low):
    chips, owners = where.shape[:2]
    half = total.shape[0] // (2 * chips * owners)
    for pair in range(chips // 2):
        part = part_of(total, pair, core, owners, 2 * half)
        for piece in range(2):
            rows = part[:, piece * half : (piece + 1) * half]
            where[2 * pair + piece, :, low : low + half] = rows


def middle(offset, opening, closing, groups, counts, *refs):
    refs = list(refs)

    def take(count):
        return [refs.pop(0) for _ in range(count)]

    x_in, cot_in, weights, weight_in, weight_out, norms = take(6)
    if not opening:
        held = take(3)
        (norm_held,) = take(1)
    if closing:
        d_outs = take(groups)
        y_out, keep_out, send_out, norm_out = take(4)
    else:
        (both_out,) = take(1)
        given = take(3)
        (norm_out,) = take(1)
    turned, order, back_order, x_one, normal_one, scale_one, normal_two, scale_two = take(8)
    x_two, low_rows, heads, d_heads, d_turned, mixed, d_mix, probs, live_grad = take(9)
    third, grad_rows, *totals, norm_total, copied = take(7)
    total_attn, total_in, total_out = totals
    if not opening:
        loads = [
            pltpu.make_async_copy(source, target, copied.at[place])
            for place, (source, target) in enumerate(zip(held, totals))
        ]
    devices, _, local, _, width = x_in.shape
    features = devices * local
    cells = features * BLOCK
    head_size = width // HEADS
    score_scale = head_size ** (-0.5)
    hidden_width = weight_in.shape[1]
    step = pl.program_id(0)
    first_sample = ((offset + step) * devices + counts[3]) * BLOCK

    @pl.when(step == 0)
    def _():
        if not opening:
            for load in loads:
                load.start()
        for which in range(3):
            turned[which] = weights[which].T
        here = row_index((cells, cells))
        there = lax.broadcasted_iota(jnp.int32, (cells, cells), 1)
        source = (here % features) * BLOCK + here // features
        order[...] = jnp.where(source == there, 1.0, 0.0).astype(BF)
        source = (here % BLOCK) * features + here // BLOCK
        back_order[...] = jnp.where(source == there, 1.0, 0.0).astype(BF)
        if opening:
            for total in totals:
                total[...] = jnp.zeros_like(total)
            norm_total[...] = jnp.zeros_like(norm_total)
        else:
            norm_total[...] = norm_held[...]

    x_one[...] = dot(order[...], x_in[:, 0].reshape(cells, width))
    for low in range(0, cells, ROWS):
        rows = slice(low, low + ROWS)
        normal, scale = normalize(x_one[rows])
        normal_one[rows] = normal
        scale_one[rows] = scale
        low_rows[rows] = (normal * norms[2:3] + norms[3:4]).astype(BF)
    heads[0] = scaled(dot(turned[0], low_rows[...], NT), head_size)
    for which in range(1, 3):
        heads[which] = dot(turned[which], low_rows[...], NT).astype(BF)

    units = cells // UNIT
    key_row = row_index((UNIT, cells))
    query_row = lax.broadcasted_iota(jnp.int32, (UNIT, cells), 1) % UNIT
    mask = (key_row // features == query_row // features) & (key_row % features < counts[1])
    for head in range(HEADS):
        lanes = slice(head * head_size, (head + 1) * head_size)
        scores = by_unit(units, lambda cols: dot(heads[1, lanes, cols], heads[0, lanes, cols], TN))
        scores = jnp.where(mask, scores, NEGATIVE)
        top = jnp.max(scores, axis=0, keepdims=True)
        powers = jnp.exp(scores - top)
        total = jnp.sum(powers, axis=0, keepdims=True)
        prob = powers * (1.0 / total)
        probs[head] = prob
        prob = prob.astype(BF)
        mixed[lanes] = by_unit(units, lambda cols: dot(heads[2, lanes, cols], prob[:, cols])).astype(BF)
    for low in range(0, cells, ROWS):
        rows = slice(low, low + ROWS)
        part = x_one[rows] + dot(mixed[:, rows], weights[3], TN)
        x_two[rows] = part
        normal, scale = normalize(part)
        normal_two[rows] = normal
        scale_two[rows] = scale
        third[rows] = (normal * norms[4:5] + norms[5:6]).astype(BF)

    if not opening:

        @pl.when(step == 0)
        def _():
            for load in loads:
                load.wait()

    def write_d(values):
        if not closing:
            both_out[:, 0, 0] = values
            return
        count = local // groups
        for place, d_out in enumerate(d_outs):
            d_out[:, 0] = values[:, place * count : (place + 1) * count]

    alive = first_sample < counts[0]

    @pl.when(jnp.logical_not(alive))
    def _():

        @pl.loop(0, hidden_width // width)
        def _(block):
            cols = block_of(block, width)
            hidden, _ = gelu_parts(dot(third[...], weight_in[:, cols]))
            x_two[...] += dot(hidden.astype(BF), weight_out[cols])

        write_d(jnp.zeros((devices, local, BLOCK, width), BF))

    @pl.when(alive)
    def _():
        place = row_index((cells, 1))
        cell_live = (place % features < counts[1]) & (
            first_sample + place // features < counts[0]
        )
        grads = dot(order[...], cot_in[:, 0].reshape(cells, width))
        live_grad[...] = jnp.where(cell_live, grads, 0.0).astype(BF)
        grad_rows[...] = jnp.zeros_like(grad_rows)

        @pl.loop(0, hidden_width // width)
        def _(block):
            cols = block_of(block, width)
            hidden, slope = gelu_parts(dot(third[...], weight_in[:, cols]))
            hidden = hidden.astype(BF)
            x_two[...] += dot(hidden, weight_out[cols])
            total_out[cols] += dot(hidden, live_grad[...], TN)
            d_pre = (dot(live_grad[...], weight_out[cols], NT) * slope).astype(BF)
            total_in[cols] += dot(d_pre, third[...], TN)
            grad_rows[...] += dot(d_pre, weight_in[:, cols], NT)


        for low in range(0, cells, ROWS):
            rows = slice(low, low + ROWS)
            normal = normal_two[rows]
            d_third = grad_rows[rows]
            norm_total[2:3] += column_sum(d_third * normal)
            norm_total[3:4] += column_sum(d_third)
            back = normalize_back(normal, scale_two[rows], d_third, norms[4:5])
            back = back + live_grad[rows].astype(F32)
            grad_rows[rows] = back
            live_grad[rows] = back.astype(BF)
        d_mix[...] = dot(weights[3], live_grad[...], NT).astype(BF)
        total_attn[3 * width :] += dot(mixed[...], live_grad[...])
        for head in range(HEADS):
            lanes = slice(head * head_size, (head + 1) * head_size)
            prob = probs[head]
            grads = d_mix[lanes]
            shared = column_sum(grads.astype(F32) * mixed[lanes].astype(F32))
            d_probs = by_unit(units, lambda cols: dot(heads[2, lanes, cols], grads[:, cols], TN))
            d_scores = (prob * (d_probs - shared)).astype(BF)
            low_prob = prob.astype(BF)
            d_query = by_unit(units, lambda cols: dot(heads[1, lanes, cols], d_scores[:, cols]))
            d_heads[0, lanes] = (d_query * score_scale).astype(BF)
            d_key = by_unit(units, lambda cols: dot(heads[0, lanes, cols], d_scores[:, cols], NT))
            d_heads[1, lanes] = d_key.astype(BF)
            d_value = by_unit(units, lambda cols: dot(grads[:, cols], low_prob[:, cols], NT))
            d_heads[2, lanes] = d_value.astype(BF)
        for which in range(3):
            d_turned[which] = d_heads[which].T
        for which in range(3):
            total_attn[which * width : (which + 1) * width] += dot(low_rows[...], d_turned[which], TN)
        for low in range(0, cells, ROWS):
            rows = slice(low, low + ROWS)
            d_second = dot(d_turned[0, rows], weights[0], NT)
            d_second = d_second + dot(d_turned[1, rows], weights[1], NT)
            d_second = d_second + dot(d_turned[2, rows], weights[2], NT)
            normal = normal_one[rows]
            norm_total[0:1] += column_sum(d_second * normal)
            norm_total[1:2] += column_sum(d_second)
            back = normalize_back(normal, scale_one[rows], d_second, norms[2:3])
            live_grad[rows] = (grad_rows[rows] + back).astype(BF)
        moved = dot(back_order[...], live_grad[...]).astype(BF)
        write_d(moved.reshape(devices, local, BLOCK, width))

    moved = dot(back_order[...], x_two[...].astype(BF)).astype(BF)
    moved = moved.reshape(devices, local, BLOCK, width)
    if closing:
        y_out[:, 0] = moved
    else:
        both_out[:, 1, 0] = moved

    @pl.when(step == pl.num_programs(0) - 1)
    def _():
        if closing:
            chips, owners, rows, _ = keep_out.shape
            own_ff = hidden_width // (2 * chips * owners)
            for where, core in ((keep_out, counts[4]), (send_out, 1 - counts[4])):
                for chip in range(chips):
                    for which, total in ((0, total_in), (1, total_out)):
                        part = part_of(total, chip, core, owners, own_ff)
                        where[chip, :, which * own_ff : (which + 1) * own_ff] = part
                attention_parts(where, total_attn, core, 2 * own_ff)
        else:
            stores = [
                pltpu.make_async_copy(source, target, copied.at[place])
                for place, (source, target) in enumerate(zip(totals, given))
            ]
            for store in stores:
                store.start()
            for store in stores:
                store.wait()
        norm_out[...] = norm_total[...]


def whole(shape):
    zeros = (0,) * len(shape)
    return pl.BlockSpec(shape, lambda step: zeros, pipeline_mode=pl.Buffered(1))


def half(shape, which):
    return pl.BlockSpec(
        (shape[0] // 2,) + tuple(shape[1:]),
        lambda step: (which, 0, 0),
        pipeline_mode=pl.Buffered(1),
    )


def once(shape):
    zeros = (0,) * len(shape)
    return pl.BlockSpec(shape, lambda step: zeros)


def lead(shape):
    zeros = (0,) * (len(shape) - 1)
    return pl.BlockSpec((1,) + tuple(shape[1:]), lambda step: (step,) + zeros)


def call(body, grid, ins, outs, scratch, nanoseconds, name, aliases=None):
    return pl.pallas_call(
        body,
        grid=(grid,),
        in_specs=[pl.BlockSpec(memory_space=pltpu.SMEM)] + [spec for spec, _ in ins[1:]],
        out_specs=[spec for spec, _, _ in outs],
        out_shape=[jax.ShapeDtypeStruct(shape, kind) for _, shape, kind in outs],
        scratch_shapes=[
            pltpu.SemaphoreType.DMA((3,)) if kind is None else pltpu.VMEM(shape, kind)
            for shape, kind in scratch
        ],
        input_output_aliases=aliases or {},
        compiler_params=pltpu.CompilerParams(vmem_limit_bytes=VMEM_BYTES),
        cost_estimate=pl.CostEstimate(
            flops=nanoseconds * 1150000, bytes_accessed=1 << 24, transcendentals=0
        ),
        name=name,
    )(ins[0][1], *[value for _, value in ins[1:]])


ANYWHERE = pl.BlockSpec(memory_space=pl.ANY)


def run_sample_forward(counts, tokens, cotangent, weights, norms, devices, early):
    local, samples, width = tokens.shape
    late = samples // (devices * BLOCK) - early
    square = (local, samples, width)
    three = (local, 3, width, samples)
    stats = (local, HEADS, samples)
    outs = [
        (
            pl.BlockSpec((devices, early, 1, BLOCK, width), lambda step: (0, 0, step, 0, 0)),
            (devices, early, local, BLOCK, width),
            BF,
        )
    ]
    if late:
        outs.append(
            (
                pl.BlockSpec(
                    (devices, 2, late, 1, BLOCK, width), lambda step: (0, 0, 0, step, 0, 0)
                ),
                (devices, 2, late, local, BLOCK, width),
                BF,
            )
        )
    outs = outs + [
        (lead(square), square, BF),
        (lead(three), three, BF),
        (lead(square), (local, width, samples), BF),
        (lead(stats), stats, F32),
    ]
    return call(
        functools.partial(sample_forward, late),
        local,
        [
            (None, counts),
            (lead(square), tokens),
            (lead(square), cotangent),
            (half(weights.shape, 0), weights),
            (whole(norms.shape), norms),
        ],
        outs,
        [((3, width, width), BF)],
        25000,
        "sample_forward",
    )


def run_middle(counts, x_dealt, cot_dealt, weights, weight_in, weight_out, norms, chips, offset, held, groups):
    array, which = x_dealt
    devices = array.shape[0]
    deals, local, _, width = array.shape[-4:]
    cells = devices * local * BLOCK
    hidden_width = weight_in.shape[1]
    parts = (chips, devices, (hidden_width + 2 * width) // (chips * devices), width)

    def dealt(which):
        if which is None:
            return pl.BlockSpec(
                (devices, 1, local, BLOCK, width), lambda step: (0, step, 0, 0, 0)
            )
        return pl.BlockSpec(
            (devices, None, 1, local, BLOCK, width),
            lambda step: (0, which, step, 0, 0, 0),
        )

    ins = [
        (None, counts),
        (dealt(x_dealt[1]), x_dealt[0]),
        (dealt(cot_dealt[1]), cot_dealt[0]),
        (half(weights.shape, 1), weights),
        (whole(weight_in.shape), weight_in),
        (whole(weight_out.shape), weight_out),
        (whole(norms.shape), norms),
    ]
    sums = [(4 * width, width), (hidden_width, width), (hidden_width, width)]
    norm_sums = (4, width)
    if held is not None:
        ins = ins + [(ANYWHERE, value) for value in held[:3]] + [(whole(norm_sums), held[3])]
    if groups:
        few = (devices, deals, local // groups, BLOCK, width)
        piece = pl.BlockSpec((devices, 1) + few[2:], lambda step: (0, step, 0, 0, 0))
        outs = [(piece, few, BF)] * groups + [
            (dealt(None), (devices, deals, local, BLOCK, width), BF),
            (once(parts), parts, BF),
            (once(parts), parts, BF),
        ]
    else:
        outs = [
            (
                pl.BlockSpec(
                    (devices, 2, 1, local, BLOCK, width), lambda step: (0, 0, step, 0, 0, 0)
                ),
                (devices, 2, deals, local, BLOCK, width),
                BF,
            )
        ] + [(ANYWHERE, shape, F32) for shape in sums]
    outs.append((once(norm_sums), norm_sums, F32))
    square = (cells, width)
    turned = (width, cells)
    return call(
        functools.partial(middle, offset, held is None, bool(groups), groups),
        deals,
        ins,
        outs,
        [
            ((3, width, width), BF),
            ((cells, cells), BF),
            ((cells, cells), BF),
            (square, F32),
            (square, F32),
            ((cells, 1), F32),
            (square, F32),
            ((cells, 1), F32),
            (square, F32),
            (square, BF),
            ((3,) + turned, BF),
            ((3,) + turned, BF),
            ((3,) + square, BF),
            (turned, BF),
            (turned, BF),
            ((HEADS, UNIT, cells), F32),
            (square, BF),
            (square, BF),
            (square, F32),
        ]
        + [(shape, F32) for shape in sums]
        + [(norm_sums, F32), ((3,), None)],
        deals * 23000,
        "middle",
    )


def run_sample_backward_early(counts, both, saved, weights):
    devices, _, early, local, _, width = both.shape
    _, _, heads, mixed, logs = saved
    samples = mixed.shape[2]
    queries = (local, early * devices * BLOCK, width)
    sums = (local, 2, samples, width)
    return call(
        sample_backward_early,
        local,
        [(None, counts), (early_spec(both), both)]
        + [(lead(value.shape), value) for value in (heads, mixed, logs)]
        + [(half(weights.shape, 0), weights)],
        [
            (lead(queries), queries, BF),
            (lead(sums), sums, F32),
            (once((width, width)), (width, width), F32),
        ],
        [
            (queries[1:], BF),
            ((width, queries[1]), BF),
            ((width, queries[1]), BF),
            ((width, width), F32),
        ],
        22000,
        "sample_backward_early",
    )


def early_spec(both):
    devices, _, early, _, _, width = both.shape
    return pl.BlockSpec(
        (devices, None, early, 1, BLOCK, width), lambda step: (0, 0, 0, step, 0, 0)
    )


def run_sample_backward(counts, both, held, d_late, saved, weights, norms, chips):
    devices, late, local, _, width = d_late.shape
    tokens = saved[0]
    samples = tokens.shape[1]
    early = 0 if both is None else both.shape[2]
    start = early * devices * BLOCK
    parts = (chips, devices, 4 * width // (2 * chips * devices), width)
    ins = [(None, counts)]
    if early:
        query, sums, weight = held
        ins = ins + [(early_spec(both), both), (lead(query.shape), query), (lead(sums.shape), sums)]
        ins.append((whole(weight.shape), weight))
    ins.append(
        (
            pl.BlockSpec((devices, late, 1, BLOCK, width), lambda step: (0, 0, step, 0, 0)),
            d_late,
        )
    )
    ins = ins + [(lead(value.shape), value) for value in saved]
    ins = ins + [(half(weights.shape, 0), weights), (whole(norms.shape), norms)]
    return call(
        functools.partial(sample_backward, early),
        local,
        ins,
        [
            (lead(tokens.shape), tokens.shape, BF),
            (once(parts), parts, BF),
            (once(parts), parts, BF),
            (once((2, width)), (2, width), F32),
        ],
        [
            ((samples, width), BF),
            ((width, samples - start), BF),
            ((width, samples - start), BF),
            ((3, samples, width), BF),
            ((4 * width, width), F32),
            ((2, width), F32),
        ],
        30000,
        "sample_backward",
    )


def adam_step(weight, grad, first_m, second_m, rate):
    moment = BETA_ONE * first_m + (1.0 - BETA_ONE) * grad
    square = BETA_TWO * second_m + (1.0 - BETA_TWO) * grad * grad
    fix_one = 1.0 - BETA_ONE**STEP
    fix_two = 1.0 - BETA_TWO**STEP
    fresh = weight - rate * (
        moment / fix_one / (jnp.sqrt(square / fix_two) + ADAM_EPS) + DECAY * weight
    )
    return (fresh, moment, square)


def exchange(values, axis, groups=None):
    return lax.all_to_all(values, axis, 0, 0, axis_index_groups=groups, tiled=True)


def moved_by(values, axis, hop):
    pairs = [(place, hop(place)) for place in range(lax.axis_size(axis))]
    return lax.ppermute(values, axis, pairs)


def other_core(values):
    return moved_by(values, "task", lambda place: place ^ 1)


def along_y(values, shift):
    tasks = lax.axis_size("task")
    return moved_by(values, "task", lambda place: (place + 2 * shift) % tasks)


def along_x(values):
    return moved_by(values, "feat", lambda place: place ^ 1)


def along_z(values, shift):
    devices = lax.axis_size("feat")
    return moved_by(values, "feat", lambda place: (place + 2 * shift) % devices)


def reduce_core(keep, send):
    came = other_core(send)
    return (keep.astype(F32) + came.astype(F32)).astype(BF)


def in_plane(values, up, across):
    tasks, devices = lax.axis_size("task"), lax.axis_size("feat")
    pairs = [
        (task * devices + place, (task + 2 * up) % tasks * devices + (place ^ across))
        for task in range(tasks)
        for place in range(devices)
    ]
    return lax.ppermute(values, ("task", "feat"), pairs)


def plane_parts(values):
    chips, devices = values.shape[:2]
    values = values.reshape((chips, devices // 2, 2) + values.shape[2:])
    chip, side = lax.axis_index("task") // 2, lax.axis_index("feat") % 2
    parts = []
    for up in range(chips):
        part = lax.dynamic_index_in_dim(values, (chip + up) % chips, 0, keepdims=False)
        for across in range(2):
            parts.append(lax.dynamic_index_in_dim(part, side ^ across, 1, keepdims=False))
    return parts


def reduce_plane(parts):
    total = parts[0].astype(F32)
    for place, part in enumerate(parts[1:], 1):
        total = total + in_plane(part, place // 2, place % 2).astype(F32)
    return total.astype(BF)


def layer_parts(values):
    layers = values.shape[0]
    layer = lax.axis_index("feat") // 2
    return [
        lax.dynamic_index_in_dim(values, (layer + shift) % layers, 0, keepdims=False)
        for shift in range(layers)
    ]


def reduce_layers(parts):
    total = parts[0].astype(F32)
    for shift, part in enumerate(parts[1:], 1):
        total = total + along_z(part, shift).astype(F32)
    return total


def to_owners(one, two):
    chips = lax.axis_size("task") // 2
    chip = lax.axis_index("task") // 2
    even = chip % 2 == 0
    stay, leave = jnp.where(even, one, two), jnp.where(even, two, one)

    def target(chip, second):
        return chip // 2 + (chips // 2 if second else 0)

    def send(values, odd_second):
        return moved_by(
            values,
            "task",
            lambda place: 2 * target(place // 2, (place // 2 % 2 == 1) == odd_second) + place % 2,
        )

    if chips > 2:
        stay = send(stay, True)
    leave = send(leave, False)
    early = chip < chips // 2
    return jnp.concatenate(
        [jnp.where(early, stay, leave), jnp.where(early, leave, stay)], axis=0
    )


def place_copies(chips, layers, table, *refs):
    count = 2 * chips
    near, far = refs[:count], refs[count : count + 4]
    *halves, attn_out, in_out, out_out, block_out, pair, copied = refs[count + 4 :]
    step = pl.program_id(0)
    moves = []
    for half in halves:
        for deal in range(half.shape[-4]):
            for feature in range(half.shape[-3]):
                index = (slice(None),) + (1,) * (len(half.shape) - 5) + (deal, feature)
                place = len(moves)
                target = block_out.at[feature, place // half.shape[-3]]
                moves.append(pltpu.make_async_copy(half.at[index], target, copied.at[place]))

    @pl.when(step == 0)
    def _():
        for move in moves:
            move.start()
    side, layer = table[count], table[count + 1]
    rows = near[0].shape[2]
    half = far[0].shape[1] // 2

    def owner(other, behind):
        return ((layer + layers - behind) % layers) * 2 + (side ^ other)

    for place in range(count):

        @pl.when(step == place)
        def _():
            core, chip = place // chips, place % chips
            for other in range(2):
                for behind in range(layers):
                    at = owner(other, behind)
                    attn_out[block_of(at, rows)] = near[place][other, behind]
                    part = far[core * 2 + other]
                    pair[block_of(at, half)] = part[chip * layers + behind, :half]
                    out_out[block_of(at, half)] = part[chip * layers + behind, half:]

    in_out[...] = pair[...].T

    @pl.when(step == count - 1)
    def _():
        for move in moves:
            move.wait()


def gather_layers(own_attn, own_ff):
    layers = lax.axis_size("feat") // 2
    nears = [own_attn] + [along_z(own_attn, shift) for shift in range(1, layers)]
    fars = [own_ff] + [along_z(own_ff, shift) for shift in range(1, layers)]
    return jnp.stack(nears), jnp.stack(fars)


def gather_rest(nears, fars, came_halves):
    layers, rows_near, width = nears.shape
    rows_far = fars.shape[1]
    chips = lax.axis_size("task") // 2
    task, place = lax.axis_index("task"), lax.axis_index("feat")
    near = jnp.stack([nears, along_x(nears)])
    far = jnp.concatenate([fars] + [along_y(fars, shift) for shift in range(1, chips)])
    nears = [near] + [along_y(near, shift) for shift in range(1, chips)]
    fars = [far, along_x(far)]
    nears = nears + [other_core(value) for value in nears]
    fars = fars + [other_core(value) for value in fars]
    steps = jnp.arange(2 * chips, dtype=jnp.int32)
    chip = (task // 2 - steps) % chips
    core = (task % 2) ^ (steps // chips)
    table = jnp.concatenate([chip * 2 + core, jnp.stack([place % 2, place // 2])])
    total = 2 * chips
    owned = 2 * layers
    devices, _, local, _, _ = came_halves[-1].shape
    deals = sum(value.shape[-4] for value in came_halves)

    def held(value):
        zeros = (0,) * value.ndim
        return pl.BlockSpec(
            value.shape, lambda step, table: zeros, pipeline_mode=pl.Buffered(1)
        )

    return pl.pallas_call(
        functools.partial(place_copies, chips, layers),
        grid_spec=pltpu.PrefetchScalarGridSpec(
            num_scalar_prefetch=1,
            grid=(total,),
            in_specs=[held(value) for value in nears + fars] + [ANYWHERE] * len(came_halves),
            out_specs=[
                pl.BlockSpec((owned * rows_near, width), lambda step, table: (table[step], 0)),
                pl.BlockSpec(
                    (width, owned * rows_far // 2), lambda step, table: (0, table[step])
                ),
                pl.BlockSpec(
                    (owned * rows_far // 2, width), lambda step, table: (table[step], 0)
                ),
                ANYWHERE,
            ],
            scratch_shapes=[
                pltpu.VMEM((owned * rows_far // 2, width), BF),
                pltpu.SemaphoreType.DMA((deals * local,)),
            ],
        ),
        out_shape=[
            jax.ShapeDtypeStruct((total * owned * rows_near, width), BF),
            jax.ShapeDtypeStruct((width, total * owned * rows_far // 2), BF),
            jax.ShapeDtypeStruct((total * owned * rows_far // 2, width), BF),
            jax.ShapeDtypeStruct((local, deals, devices, BLOCK, width), BF),
        ],
        compiler_params=pltpu.CompilerParams(vmem_limit_bytes=40 * 1024 * 1024),
        name="place_copies",
    )(table.astype(jnp.int32), *nears, *fars, *came_halves)


def total_of(values):
    values = values + other_core(values)
    chips = lax.axis_size("task") // 2
    values = sum([along_y(values, shift) for shift in range(1, chips)], values)
    bit = 1
    while bit < lax.axis_size("feat"):
        values = values + moved_by(values, "feat", lambda place: place ^ bit)
        bit *= 2
    return values


def shards(
    tokens,
    cotangent,
    attn_weights,
    weight_in,
    weight_out,
    norm_params,
    master_attn,
    master_in,
    master_out,
    first_attn,
    first_in,
    first_out,
    first_norms,
    second_attn,
    second_in,
    second_out,
    second_norms,
    sample_count,
    feature_count,
):
    local, samples, width = tokens.shape[1:]
    devices = lax.axis_size("feat")
    tasks = lax.axis_size("task")
    chips = tasks // 2
    place = lax.axis_index("feat")
    deals = samples // (devices * BLOCK)
    counts = jnp.stack(
        [sample_count[0], feature_count[0], place * local, place, lax.axis_index("task") % 2]
    ).astype(jnp.int32)
    weights = attn_weights.reshape(8, width, width)

    early = max(deals // 2, 1)
    late = deals - early
    groups = 1
    own_ff = weight_in.shape[1] // (tasks * devices)
    own_attn = attn_weights.shape[0] // (tasks * devices)

    def dealt(values):
        count = values.shape[1] // (devices * BLOCK)
        values = values.reshape(local, count, devices, BLOCK, width)
        return values.transpose(2, 1, 0, 3, 4)

    came_cot = exchange(dealt(cotangent[0, :, : early * devices * BLOCK]), "feat")
    dealt_x, *rest = run_sample_forward(
        counts, tokens[0], cotangent[0], weights, norm_params, devices, early
    )
    came_cot, dealt_x, *rest = lax.optimization_barrier((came_cot, dealt_x, *rest))
    saved = [tokens[0]] + rest[-4:]
    came_x = exchange(dealt_x, "feat")
    shared = (weights, weight_in, weight_out, norm_params, chips)
    came_both = None
    if late:
        dealt_late, came_x = lax.optimization_barrier((rest[0], came_x))
        came_late = exchange(dealt_late, "feat")
        dealt_both, *held = run_middle(
            counts, (came_x, None), (came_cot, None), *shared, 0, None, 0
        )
        *dealt_d, dealt_y, keep_two, send_two, norms_two = run_middle(
            counts, (came_late, 0), (came_late, 1), *shared, early, held, groups
        )
        came_both = exchange(dealt_both, "feat")
        came_both, dealt_d, dealt_y, keep_two, send_two, norms_two = lax.optimization_barrier(
            (came_both, dealt_d, dealt_y, keep_two, send_two, norms_two)
        )
    else:
        *dealt_d, dealt_y, keep_two, send_two, norms_two = run_middle(
            counts, (came_x, None), (came_cot, None), *shared, 0, None, groups
        )
    came_d = exchange(dealt_d[0], "feat")
    parts_two = plane_parts(reduce_core(keep_two, send_two))
    held = None
    if late:
        came_both, _ = lax.optimization_barrier((came_both, parts_two))
        held = run_sample_backward_early(counts, came_both, saved, weights)
    dealt_y, came_d, held = lax.optimization_barrier((dealt_y, came_d, held))
    came_y = exchange(dealt_y, "feat")
    input_grad, keep_one, send_one, norms_one = run_sample_backward(
        counts, came_both, held, came_d, saved, weights, norm_params, chips
    )
    parts_two[0], came_y, input_grad, keep_one, send_one, norms_one = lax.optimization_barrier(
        (parts_two[0], came_y, input_grad, keep_one, send_one, norms_one)
    )
    parts_two = layer_parts(reduce_plane(parts_two))
    parts_two, keep_one, send_one = lax.optimization_barrier((parts_two, keep_one, send_one))
    parts_one = layer_parts(reduce_plane(plane_parts(reduce_core(keep_one, send_one))))
    share_two, parts_one = lax.optimization_barrier((reduce_layers(parts_two), parts_one))
    share_one = reduce_layers(parts_one)
    share_in_turned = share_two[:own_ff]
    share_out = share_two[own_ff : 2 * own_ff]
    local_squares = jnp.sum(share_one * share_one) + jnp.sum(share_two * share_two)
    small = jnp.concatenate(
        [norms_one, norms_two, jnp.full((2, width), local_squares, F32)], axis=0
    )
    small, part_one, part_two = lax.optimization_barrier(
        (small, share_one, share_two[2 * own_ff :])
    )
    share_attn = to_owners(part_one, part_two)
    small, share_attn = lax.optimization_barrier((total_of(small), share_attn))
    total_norms = small[:6]
    squares = small[6, 0] + jnp.sum(total_norms * total_norms)
    grad_norm = jnp.sqrt(squares)
    factor = jnp.minimum(1.0, CLIP_AT / (grad_norm + 1e-06))
    new_attn, moment_attn, square_attn = adam_step(
        master_attn, factor * share_attn, first_attn, second_attn, RATE
    )
    new_in, moment_in, square_in = adam_step(
        master_in, factor * share_in_turned.T, first_in, second_in, RATE
    )
    new_out, moment_out, square_out = adam_step(
        master_out, factor * share_out, first_out, second_out, RATE
    )
    new_norms, moment_norms, square_norms = adam_step(
        norm_params, factor * total_norms, first_norms, second_norms, NORM_RATE
    )
    own_both = jnp.concatenate([new_in.astype(BF).T, new_out.astype(BF)], axis=0)
    nears, fars = gather_layers(new_attn.astype(BF), own_both)
    came_halves = [came_y] if came_both is None else [came_both, came_y]
    copy_attn, copy_in, copy_out, block_out = gather_rest(nears, fars, came_halves)
    block_out = block_out.reshape(1, local, samples, width)
    return (
        block_out,
        input_grad[None],
        grad_norm.reshape(1),
        new_attn,
        new_in,
        new_out,
        new_norms,
        moment_attn,
        moment_in,
        moment_out,
        moment_norms,
        square_attn,
        square_in,
        square_out,
        square_norms,
        copy_attn,
        copy_in,
        copy_out,
    )


def solution(mesh):
    cells = P("task", "feat", None, None)
    rows = P(("task", "feat"), None)
    columns = P(None, ("task", "feat"))
    return jax.shard_map(
        shards,
        mesh=mesh,
        in_specs=(cells, cells, P(), P(), P(), P())
        + (rows, columns, rows)
        + (rows, columns, rows, P())
        + (rows, columns, rows, P())
        + (P("task"), P("task")),
        out_specs=(cells, cells, P())
        + (rows, columns, rows, P())
        + (rows, columns, rows, P())
        + (rows, columns, rows, P())
        + (P(), P(), P()),
        check_vma=False,
    )
```

```python
import functools

import jax
import jax.numpy as jnp
from jax import lax
from jax.experimental import pallas as pl
from jax.experimental.pallas import tpu as pltpu
from jax.sharding import PartitionSpec as P

HEADS = 8
STEP = 5
NEGATIVE = -1e30
LN_EPS = 1e-05
CLIP_AT = 1.0
BETA_ONE = 0.9
BETA_TWO = 0.999
RATE = 0.02
NORM_RATE = 0.25
DECAY = 0.1
ADAM_EPS = 1e-08

BLOCK = 16
UNIT = 128
ROWS = 128
QUERIES = 512
UNROLL = 2
VMEM_BYTES = 60 * 1024 * 1024

BF = jnp.bfloat16
F32 = jnp.float32
NN = ((1,), (0,))
NT = ((1,), (1,))
TN = ((0,), (0,))


def dot(left, right, dims=NN):
    return lax.dot_general(left, right, (dims, ((), ())), preferred_element_type=F32)


def normalize(values):
    center = jnp.mean(values, axis=-1, keepdims=True)
    centred = values - center
    spread = jnp.mean(centred * centred, axis=-1, keepdims=True)
    scale = lax.rsqrt(spread + LN_EPS)
    return centred * scale, scale


def normalize_back(normal, scale, grad, gain):
    d_normal = grad * gain
    mean_one = jnp.mean(d_normal, axis=-1, keepdims=True)
    mean_two = jnp.mean(d_normal * normal, axis=-1, keepdims=True)
    return scale * (d_normal - mean_one - normal * mean_two)


def column_sum(values):
    return jnp.sum(values, axis=0, keepdims=True)


def by_unit(units, one):
    parts = [one(slice(place * UNIT, (place + 1) * UNIT)) for place in range(units)]
    return jnp.concatenate(parts, axis=1)


def scaled(values, head_size):
    return (values.astype(BF).astype(F32) * head_size ** (-0.5)).astype(BF)


def block_of(place, size):
    return pl.ds(pl.multiple_of(place * size, size), size)


def row_index(shape):
    return lax.broadcasted_iota(jnp.int32, shape, 0)


def sample_forward(late, counts, tokens, cotangent, weights, norms, x_out, *rest):
    if late:
        late_out, *rest = rest
    first_out, heads_out, mixed_out, log_out, turned = rest
    samples, width = tokens.shape[1:]
    head_size = width // HEADS
    early = x_out.shape[1]
    dealt = (x_out.shape[0], BLOCK, width)
    group = dealt[0] * BLOCK

    @pl.when(pl.program_id(0) == 0)
    def _():
        for which in range(3):
            turned[which] = weights[which].T

    for low in range(0, samples, ROWS):
        rows = slice(low, low + ROWS)
        normal, _ = normalize(tokens[0, rows].astype(F32))
        first_out[0, rows] = (normal * norms[0:1] + norms[1:2]).astype(BF)
    first = first_out[0]
    heads_out[0, 0] = scaled(dot(turned[0], first, NT), head_size)
    for which in range(1, 3):
        heads_out[0, which] = dot(turned[which], first, NT).astype(BF)
    live = row_index((samples, 1)) < counts[0]
    for head in range(HEADS):
        lanes = slice(head * head_size, (head + 1) * head_size)
        keys = heads_out[0, 1, lanes]
        values = heads_out[0, 2, lanes]
        for low in range(0, samples, QUERIES):
            cols = slice(low, low + QUERIES)
            scores = dot(keys, heads_out[0, 0, lanes, cols], TN)
            scores = jnp.where(live, scores, NEGATIVE)
            top = jnp.max(scores, axis=0, keepdims=True)
            powers = jnp.exp(scores - top)
            total = jnp.sum(powers, axis=0, keepdims=True)
            mixed = dot(values, powers.astype(BF)) * (1.0 / total)
            mixed_out[0, lanes, cols] = mixed.astype(BF)
            log_out[0, head : head + 1, cols] = top + jnp.log(total)
    for low in range(0, samples, group):
        rows = slice(low, low + group)
        part = tokens[0, rows].astype(F32) + dot(mixed_out[0, :, rows], weights[3], TN)
        part = part.astype(BF).reshape(dealt)
        if low // group < early:
            x_out[:, low // group, 0] = part
        else:
            late_out[:, 0, low // group - early, 0] = part
            late_out[:, 1, low // group - early, 0] = cotangent[0, rows].reshape(dealt)


def heads_back(heads, mixed, logs, d_mix, rows, live, d_query, add):
    width = d_mix.shape[0]
    head_size = width // HEADS
    for pair in range(0, HEADS, 2):
        d_keys, d_values = [], []
        for head in (pair, pair + 1):
            lanes = slice(head * head_size, (head + 1) * head_size)
            keys = heads[0, 1, lanes]
            values = heads[0, 2, lanes]
            queries = heads[0, 0, lanes, rows]
            grads = d_mix[lanes]
            shared = column_sum(grads.astype(F32) * mixed[0, lanes, rows].astype(F32))
            scores = jnp.where(live, dot(keys, queries, TN), NEGATIVE)
            probs = jnp.exp(scores - logs[0, head : head + 1, rows])
            d_probs = dot(values, grads, TN)
            d_scores = (probs * (d_probs - shared)).astype(BF)
            d_query[lanes] = (dot(keys, d_scores) * head_size ** (-0.5)).astype(BF)
            d_keys.append(dot(d_scores, queries, NT))
            d_values.append(dot(probs.astype(BF), grads, NT))
        lanes = slice(pair * head_size, (pair + 2) * head_size)
        add(lanes, jnp.concatenate(d_keys, axis=1), jnp.concatenate(d_values, axis=1))


def sample_backward_early(
    counts, d_early, heads, mixed, logs, weights, query_out, sums_out, weight_out, d_rows, d_mix, d_query, total
):
    samples = mixed.shape[2]
    width = d_mix.shape[0]
    group = d_early.shape[0] * BLOCK
    rows = slice(0, d_rows.shape[0])
    step = pl.program_id(0)

    @pl.when(step == 0)
    def _():
        total[...] = jnp.zeros_like(total)

    @pl.when(counts[2] + step < counts[1])
    def _():
        for deal in range(d_early.shape[1]):
            part = d_early[:, deal, 0].reshape(group, width)
            d_rows[deal * group : (deal + 1) * group] = part
        d_mix[...] = dot(weights[3], d_rows[...], NT).astype(BF)
        total[...] += dot(mixed[0, :, rows], d_rows[...])
        live = row_index((samples, 1)) < counts[0]

        def add(lanes, d_keys, d_values):
            sums_out[0, 0, :, lanes] = d_keys
            sums_out[0, 1, :, lanes] = d_values

        heads_back(heads, mixed, logs, d_mix, rows, live, d_query, add)
        query_out[0] = d_query[...].T

    @pl.when(step == pl.num_programs(0) - 1)
    def _():
        weight_out[...] = total[...]


def sample_backward(early, counts, *refs):
    if early:
        d_early, query_held, sums_held, weight_held, *refs = refs
    d_late, tokens, first, heads, mixed, logs, weights, norms, *refs = refs
    grad_out, keep_out, send_out, norm_out, d_rows, d_mix, d_query, d_turned, total, norm_total = refs
    samples, width = tokens.shape[1:]
    group = d_late.shape[0] * BLOCK
    start = early * group
    rows = slice(start, samples)
    step = pl.program_id(0)

    @pl.when(step == 0)
    def _():
        total[...] = jnp.zeros_like(total)
        if early:
            total[3 * width :] = weight_held[...]
        norm_total[...] = jnp.zeros_like(norm_total)

    feature_live = counts[2] + step < counts[1]

    @pl.when(jnp.logical_not(feature_live))
    def _():
        grad_out[...] = jnp.zeros_like(grad_out)

    @pl.when(feature_live)
    def _():
        for low in range(0, samples, group):
            deal = low // group
            part = d_early[:, deal, 0] if deal < early else d_late[:, deal - early, 0]
            d_rows[low : low + group] = part.reshape(group, width)
        d_mix[...] = dot(weights[3], d_rows[rows], NT).astype(BF)
        total[3 * width :] += dot(mixed[0, :, rows], d_rows[rows])
        live = row_index((samples, 1)) < counts[0]

        def add(lanes, d_keys, d_values):
            if early:
                d_keys = d_keys + sums_held[0, 0, :, lanes]
                d_values = d_values + sums_held[0, 1, :, lanes]
            d_turned[1, :, lanes] = d_keys.astype(BF)
            d_turned[2, :, lanes] = d_values.astype(BF)

        heads_back(heads, mixed, logs, d_mix, rows, live, d_query, add)
        d_turned[0, rows] = d_query[...].T
        if early:
            d_turned[0, :start] = query_held[0]
        for which in range(3):
            total[which * width : (which + 1) * width] += dot(first[0], d_turned[which], TN)
        for low in range(0, samples, ROWS):
            part = slice(low, low + ROWS)
            d_first = dot(d_turned[0, part], weights[0], NT)
            d_first = d_first + dot(d_turned[1, part], weights[1], NT)
            d_first = d_first + dot(d_turned[2, part], weights[2], NT)
            normal, scale = normalize(tokens[0, part].astype(F32))
            norm_total[0:1] += column_sum(d_first * normal)
            norm_total[1:2] += column_sum(d_first)
            back = normalize_back(normal, scale, d_first, norms[0:1])
            grad_out[0, part] = (d_rows[part].astype(F32) + back).astype(BF)

    @pl.when(step == pl.num_programs(0) - 1)
    def _():
        attention_parts(keep_out, total, counts[4], 0)
        attention_parts(send_out, total, 1 - counts[4], 0)
        norm_out[...] = norm_total[...]


def gelu_parts(pre):
    root = 0.7978845608028654
    square = pre * pre
    curve = jnp.tanh(root * pre * (1.0 + 0.044715 * square))
    half = 0.5 * (1.0 + curve)
    slope = half + (0.5 * root) * pre * (1.0 - curve * curve) * (1.0 + 3 * 0.044715 * square)
    return pre * half, slope


def part_of(total, chip, core, owners, rows):
    start = pl.multiple_of((chip * 2 + core) * (owners * rows), owners * rows)
    part = total[pl.ds(start, owners * rows)].astype(BF)
    return part.reshape(owners, rows, part.shape[-1])


def attention_parts(where, total, core, low):
    chips, owners = where.shape[:2]
    half = total.shape[0] // (2 * chips * owners)
    for pair in range(chips // 2):
        part = part_of(total, pair, core, owners, 2 * half)
        for piece in range(2):
            rows = part[:, piece * half : (piece + 1) * half]
            where[2 * pair + piece, :, low : low + half] = rows


def middle(offset, opening, closing, groups, counts, *refs):
    refs = list(refs)

    def take(count):
        return [refs.pop(0) for _ in range(count)]

    step = pl.program_id(0)
    x_in, cot_in, weights, weight_in, weight_out, norms = take(6)
    if not opening:
        held = take(3)
        (norm_held,) = take(1)
    if closing:
        d_outs = take(groups)
        y_out, keep_out, send_out, norm_out = take(4)
    else:
        (both_out,) = take(1)
        given = take(3)
        (norm_out,) = take(1)
    turned, order, back_order, x_one, normal_one, scale_one, normal_two, scale_two = take(8)
    x_two, low_rows, heads, d_heads, d_turned, mixed, d_mix, probs, live_grad = take(9)
    third, grad_rows, *totals, norm_total, copied = take(7)
    total_attn, total_in, total_out = totals
    if not opening:
        loads = [
            pltpu.make_async_copy(source, target, copied.at[place])
            for place, (source, target) in enumerate(zip(held, totals))
        ]
    if not closing:
        stores = [
            pltpu.make_async_copy(source, target, copied.at[place])
            for place, (source, target) in enumerate(zip(totals, given))
        ]
        last = step == pl.num_programs(0) - 1
    devices, _, local, _, width = x_in.shape
    features = devices * local
    cells = features * BLOCK
    head_size = width // HEADS
    score_scale = head_size ** (-0.5)
    hidden_width = weight_in.shape[1]
    first_sample = ((offset + step) * devices + counts[3]) * BLOCK

    @pl.when(step == 0)
    def _():
        if not opening:
            for load in loads:
                load.start()
        for which in range(3):
            turned[which] = weights[which].T
        here = row_index((cells, cells))
        there = lax.broadcasted_iota(jnp.int32, (cells, cells), 1)
        source = (here % features) * BLOCK + here // features
        order[...] = jnp.where(source == there, 1.0, 0.0).astype(BF)
        source = (here % BLOCK) * features + here // BLOCK
        back_order[...] = jnp.where(source == there, 1.0, 0.0).astype(BF)
        if opening:
            for total in totals:
                total[...] = jnp.zeros_like(total)
            norm_total[...] = jnp.zeros_like(norm_total)
        else:
            norm_total[...] = norm_held[...]

    x_one[...] = dot(order[...], x_in[:, 0].reshape(cells, width))
    for low in range(0, cells, ROWS):
        rows = slice(low, low + ROWS)
        normal, scale = normalize(x_one[rows])
        normal_one[rows] = normal
        scale_one[rows] = scale
        low_rows[rows] = (normal * norms[2:3] + norms[3:4]).astype(BF)
    heads[0] = scaled(dot(turned[0], low_rows[...], NT), head_size)
    for which in range(1, 3):
        heads[which] = dot(turned[which], low_rows[...], NT).astype(BF)

    units = cells // UNIT
    key_row = row_index((UNIT, cells))
    query_row = lax.broadcasted_iota(jnp.int32, (UNIT, cells), 1) % UNIT
    mask = (key_row // features == query_row // features) & (key_row % features < counts[1])
    for head in range(HEADS):
        lanes = slice(head * head_size, (head + 1) * head_size)
        scores = by_unit(units, lambda cols: dot(heads[1, lanes, cols], heads[0, lanes, cols], TN))
        scores = jnp.where(mask, scores, NEGATIVE)
        top = jnp.max(scores, axis=0, keepdims=True)
        powers = jnp.exp(scores - top)
        total = jnp.sum(powers, axis=0, keepdims=True)
        prob = powers * (1.0 / total)
        probs[head] = prob
        prob = prob.astype(BF)
        mixed[lanes] = by_unit(units, lambda cols: dot(heads[2, lanes, cols], prob[:, cols])).astype(BF)
    for low in range(0, cells, ROWS):
        rows = slice(low, low + ROWS)
        part = x_one[rows] + dot(mixed[:, rows], weights[3], TN)
        x_two[rows] = part
        normal, scale = normalize(part)
        normal_two[rows] = normal
        scale_two[rows] = scale
        third[rows] = (normal * norms[4:5] + norms[5:6]).astype(BF)

    if not opening:

        @pl.when(step == 0)
        def _():
            for load in loads:
                load.wait()

    def write_d(values):
        if not closing:
            both_out[:, 0, 0] = values
            return
        count = local // groups
        for place, d_out in enumerate(d_outs):
            d_out[:, 0] = values[:, place * count : (place + 1) * count]

    alive = first_sample < counts[0]

    @pl.when(jnp.logical_not(alive))
    def _():

        @pl.loop(0, hidden_width // width)
        def _(block):
            cols = block_of(block, width)
            hidden, _ = gelu_parts(dot(third[...], weight_in[:, cols]))
            x_two[...] += dot(hidden.astype(BF), weight_out[cols])

        write_d(jnp.zeros((devices, local, BLOCK, width), BF))
        if not closing:

            @pl.when(last)
            def _():
                for store in stores[1:]:
                    store.start()

    @pl.when(alive)
    def _():
        place = row_index((cells, 1))
        cell_live = (place % features < counts[1]) & (
            first_sample + place // features < counts[0]
        )
        grads = dot(order[...], cot_in[:, 0].reshape(cells, width))
        live_grad[...] = jnp.where(cell_live, grads, 0.0).astype(BF)
        grad_rows[...] = jnp.zeros_like(grad_rows)

        @pl.loop(0, hidden_width // width)
        def _(block):
            cols = block_of(block, width)
            hidden, slope = gelu_parts(dot(third[...], weight_in[:, cols]))
            hidden = hidden.astype(BF)
            x_two[...] += dot(hidden, weight_out[cols])
            total_out[cols] += dot(hidden, live_grad[...], TN)
            d_pre = (dot(live_grad[...], weight_out[cols], NT) * slope).astype(BF)
            total_in[cols] += dot(d_pre, third[...], TN)
            grad_rows[...] += dot(d_pre, weight_in[:, cols], NT)

        if not closing:

            @pl.when(last)
            def _():
                for store in stores[1:]:
                    store.start()


        for low in range(0, cells, ROWS):
            rows = slice(low, low + ROWS)
            normal = normal_two[rows]
            d_third = grad_rows[rows]
            norm_total[2:3] += column_sum(d_third * normal)
            norm_total[3:4] += column_sum(d_third)
            back = normalize_back(normal, scale_two[rows], d_third, norms[4:5])
            back = back + live_grad[rows].astype(F32)
            grad_rows[rows] = back
            live_grad[rows] = back.astype(BF)
        d_mix[...] = dot(weights[3], live_grad[...], NT).astype(BF)
        total_attn[3 * width :] += dot(mixed[...], live_grad[...])
        for head in range(HEADS):
            lanes = slice(head * head_size, (head + 1) * head_size)
            prob = probs[head]
            grads = d_mix[lanes]
            shared = column_sum(grads.astype(F32) * mixed[lanes].astype(F32))
            d_probs = by_unit(units, lambda cols: dot(heads[2, lanes, cols], grads[:, cols], TN))
            d_scores = (prob * (d_probs - shared)).astype(BF)
            low_prob = prob.astype(BF)
            d_query = by_unit(units, lambda cols: dot(heads[1, lanes, cols], d_scores[:, cols]))
            d_heads[0, lanes] = (d_query * score_scale).astype(BF)
            d_key = by_unit(units, lambda cols: dot(heads[0, lanes, cols], d_scores[:, cols], NT))
            d_heads[1, lanes] = d_key.astype(BF)
            d_value = by_unit(units, lambda cols: dot(grads[:, cols], low_prob[:, cols], NT))
            d_heads[2, lanes] = d_value.astype(BF)
        for which in range(3):
            d_turned[which] = d_heads[which].T
        for which in range(3):
            total_attn[which * width : (which + 1) * width] += dot(low_rows[...], d_turned[which], TN)
        for low in range(0, cells, ROWS):
            rows = slice(low, low + ROWS)
            d_second = dot(d_turned[0, rows], weights[0], NT)
            d_second = d_second + dot(d_turned[1, rows], weights[1], NT)
            d_second = d_second + dot(d_turned[2, rows], weights[2], NT)
            normal = normal_one[rows]
            norm_total[0:1] += column_sum(d_second * normal)
            norm_total[1:2] += column_sum(d_second)
            back = normalize_back(normal, scale_one[rows], d_second, norms[2:3])
            live_grad[rows] = (grad_rows[rows] + back).astype(BF)
        moved = dot(back_order[...], live_grad[...]).astype(BF)
        write_d(moved.reshape(devices, local, BLOCK, width))

    moved = dot(back_order[...], x_two[...].astype(BF)).astype(BF)
    moved = moved.reshape(devices, local, BLOCK, width)
    if closing:
        y_out[:, 0] = moved
    else:
        both_out[:, 1, 0] = moved

    @pl.when(step == pl.num_programs(0) - 1)
    def _():
        if closing:
            chips, owners, rows, _ = keep_out.shape
            own_ff = hidden_width // (2 * chips * owners)
            for where, core in ((keep_out, counts[4]), (send_out, 1 - counts[4])):
                for chip in range(chips):
                    for which, total in ((0, total_in), (1, total_out)):
                        part = part_of(total, chip, core, owners, own_ff)
                        where[chip, :, which * own_ff : (which + 1) * own_ff] = part
                attention_parts(where, total_attn, core, 2 * own_ff)
        else:
            stores[0].start()
            for store in stores:
                store.wait()
        norm_out[...] = norm_total[...]


def whole(shape):
    zeros = (0,) * len(shape)
    return pl.BlockSpec(shape, lambda step: zeros, pipeline_mode=pl.Buffered(1))


def half(shape, which):
    return pl.BlockSpec(
        (shape[0] // 2,) + tuple(shape[1:]),
        lambda step: (which, 0, 0),
        pipeline_mode=pl.Buffered(1),
    )


def once(shape):
    zeros = (0,) * len(shape)
    return pl.BlockSpec(shape, lambda step: zeros)


def lead(shape):
    zeros = (0,) * (len(shape) - 1)
    return pl.BlockSpec((1,) + tuple(shape[1:]), lambda step: (step,) + zeros)


def call(body, grid, ins, outs, scratch, nanoseconds, name, aliases=None):
    return pl.pallas_call(
        body,
        grid=(grid,),
        in_specs=[pl.BlockSpec(memory_space=pltpu.SMEM)] + [spec for spec, _ in ins[1:]],
        out_specs=[spec for spec, _, _ in outs],
        out_shape=[jax.ShapeDtypeStruct(shape, kind) for _, shape, kind in outs],
        scratch_shapes=[
            pltpu.SemaphoreType.DMA((3,)) if kind is None else pltpu.VMEM(shape, kind)
            for shape, kind in scratch
        ],
        input_output_aliases=aliases or {},
        compiler_params=pltpu.CompilerParams(vmem_limit_bytes=VMEM_BYTES),
        cost_estimate=pl.CostEstimate(
            flops=nanoseconds * 1150000, bytes_accessed=1 << 24, transcendentals=0
        ),
        name=name,
    )(ins[0][1], *[value for _, value in ins[1:]])


ANYWHERE = pl.BlockSpec(memory_space=pl.ANY)


def run_sample_forward(counts, tokens, cotangent, weights, norms, devices, early):
    local, samples, width = tokens.shape
    late = samples // (devices * BLOCK) - early
    square = (local, samples, width)
    three = (local, 3, width, samples)
    stats = (local, HEADS, samples)
    outs = [
        (
            pl.BlockSpec((devices, early, 1, BLOCK, width), lambda step: (0, 0, step, 0, 0)),
            (devices, early, local, BLOCK, width),
            BF,
        )
    ]
    if late:
        outs.append(
            (
                pl.BlockSpec(
                    (devices, 2, late, 1, BLOCK, width), lambda step: (0, 0, 0, step, 0, 0)
                ),
                (devices, 2, late, local, BLOCK, width),
                BF,
            )
        )
    outs = outs + [
        (lead(square), square, BF),
        (lead(three), three, BF),
        (lead(square), (local, width, samples), BF),
        (lead(stats), stats, F32),
    ]
    return call(
        functools.partial(sample_forward, late),
        local,
        [
            (None, counts),
            (lead(square), tokens),
            (lead(square), cotangent),
            (half(weights.shape, 0), weights),
            (whole(norms.shape), norms),
        ],
        outs,
        [((3, width, width), BF)],
        25000,
        "sample_forward",
    )


def run_middle(counts, x_dealt, cot_dealt, weights, weight_in, weight_out, norms, chips, offset, held, groups):
    array, which = x_dealt
    devices = array.shape[0]
    deals, local, _, width = array.shape[-4:]
    cells = devices * local * BLOCK
    hidden_width = weight_in.shape[1]
    parts = (chips, devices, (hidden_width + 2 * width) // (chips * devices), width)

    def dealt(which):
        if which is None:
            return pl.BlockSpec(
                (devices, 1, local, BLOCK, width), lambda step: (0, step, 0, 0, 0)
            )
        return pl.BlockSpec(
            (devices, None, 1, local, BLOCK, width),
            lambda step: (0, which, step, 0, 0, 0),
        )

    ins = [
        (None, counts),
        (dealt(x_dealt[1]), x_dealt[0]),
        (dealt(cot_dealt[1]), cot_dealt[0]),
        (half(weights.shape, 1), weights),
        (whole(weight_in.shape), weight_in),
        (whole(weight_out.shape), weight_out),
        (whole(norms.shape), norms),
    ]
    sums = [(4 * width, width), (hidden_width, width), (hidden_width, width)]
    norm_sums = (4, width)
    if held is not None:
        ins = ins + [(ANYWHERE, value) for value in held[:3]] + [(whole(norm_sums), held[3])]
    if groups:
        few = (devices, deals, local // groups, BLOCK, width)
        piece = pl.BlockSpec((devices, 1) + few[2:], lambda step: (0, step, 0, 0, 0))
        outs = [(piece, few, BF)] * groups + [
            (dealt(None), (devices, deals, local, BLOCK, width), BF),
            (once(parts), parts, BF),
            (once(parts), parts, BF),
        ]
    else:
        outs = [
            (
                pl.BlockSpec(
                    (devices, 2, 1, local, BLOCK, width), lambda step: (0, 0, step, 0, 0, 0)
                ),
                (devices, 2, deals, local, BLOCK, width),
                BF,
            )
        ] + [(ANYWHERE, shape, F32) for shape in sums]
    outs.append((once(norm_sums), norm_sums, F32))
    square = (cells, width)
    turned = (width, cells)
    return call(
        functools.partial(middle, offset, held is None, bool(groups), groups),
        deals,
        ins,
        outs,
        [
            ((3, width, width), BF),
            ((cells, cells), BF),
            ((cells, cells), BF),
            (square, F32),
            (square, F32),
            ((cells, 1), F32),
            (square, F32),
            ((cells, 1), F32),
            (square, F32),
            (square, BF),
            ((3,) + turned, BF),
            ((3,) + turned, BF),
            ((3,) + square, BF),
            (turned, BF),
            (turned, BF),
            ((HEADS, UNIT, cells), F32),
            (square, BF),
            (square, BF),
            (square, F32),
        ]
        + [(shape, F32) for shape in sums]
        + [(norm_sums, F32), ((3,), None)],
        deals * 23000,
        "middle",
    )


def run_sample_backward_early(counts, both, saved, weights):
    devices, _, early, local, _, width = both.shape
    _, _, heads, mixed, logs = saved
    samples = mixed.shape[2]
    queries = (local, early * devices * BLOCK, width)
    sums = (local, 2, samples, width)
    return call(
        sample_backward_early,
        local,
        [(None, counts), (early_spec(both), both)]
        + [(lead(value.shape), value) for value in (heads, mixed, logs)]
        + [(half(weights.shape, 0), weights)],
        [
            (lead(queries), queries, BF),
            (lead(sums), sums, F32),
            (once((width, width)), (width, width), F32),
        ],
        [
            (queries[1:], BF),
            ((width, queries[1]), BF),
            ((width, queries[1]), BF),
            ((width, width), F32),
        ],
        22000,
        "sample_backward_early",
    )


def early_spec(both):
    devices, _, early, _, _, width = both.shape
    return pl.BlockSpec(
        (devices, None, early, 1, BLOCK, width), lambda step: (0, 0, 0, step, 0, 0)
    )


def run_sample_backward(counts, both, held, d_late, saved, weights, norms, chips):
    devices, late, local, _, width = d_late.shape
    tokens = saved[0]
    samples = tokens.shape[1]
    early = 0 if both is None else both.shape[2]
    start = early * devices * BLOCK
    parts = (chips, devices, 4 * width // (2 * chips * devices), width)
    ins = [(None, counts)]
    if early:
        query, sums, weight = held
        ins = ins + [(early_spec(both), both), (lead(query.shape), query), (lead(sums.shape), sums)]
        ins.append((whole(weight.shape), weight))
    ins.append(
        (
            pl.BlockSpec((devices, late, 1, BLOCK, width), lambda step: (0, 0, step, 0, 0)),
            d_late,
        )
    )
    ins = ins + [(lead(value.shape), value) for value in saved]
    ins = ins + [(half(weights.shape, 0), weights), (whole(norms.shape), norms)]
    return call(
        functools.partial(sample_backward, early),
        local,
        ins,
        [
            (lead(tokens.shape), tokens.shape, BF),
            (once(parts), parts, BF),
            (once(parts), parts, BF),
            (once((2, width)), (2, width), F32),
        ],
        [
            ((samples, width), BF),
            ((width, samples - start), BF),
            ((width, samples - start), BF),
            ((3, samples, width), BF),
            ((4 * width, width), F32),
            ((2, width), F32),
        ],
        30000,
        "sample_backward",
    )


def adam_step(weight, grad, first_m, second_m, rate):
    moment = BETA_ONE * first_m + (1.0 - BETA_ONE) * grad
    square = BETA_TWO * second_m + (1.0 - BETA_TWO) * grad * grad
    fix_one = 1.0 - BETA_ONE**STEP
    fix_two = 1.0 - BETA_TWO**STEP
    fresh = weight - rate * (
        moment / fix_one / (jnp.sqrt(square / fix_two) + ADAM_EPS) + DECAY * weight
    )
    return (fresh, moment, square)


def exchange(values, axis, groups=None):
    return lax.all_to_all(values, axis, 0, 0, axis_index_groups=groups, tiled=True)


def moved_by(values, axis, hop):
    pairs = [(place, hop(place)) for place in range(lax.axis_size(axis))]
    return lax.ppermute(values, axis, pairs)


def other_core(values):
    return moved_by(values, "task", lambda place: place ^ 1)


def along_y(values, shift):
    tasks = lax.axis_size("task")
    return moved_by(values, "task", lambda place: (place + 2 * shift) % tasks)


def along_x(values):
    return moved_by(values, "feat", lambda place: place ^ 1)


def along_z(values, shift):
    devices = lax.axis_size("feat")
    return moved_by(values, "feat", lambda place: (place + 2 * shift) % devices)


def reduce_core(keep, send):
    came = other_core(send)
    return (keep.astype(F32) + came.astype(F32)).astype(BF)


def in_plane(values, up, across):
    tasks, devices = lax.axis_size("task"), lax.axis_size("feat")
    pairs = [
        (task * devices + place, (task + 2 * up) % tasks * devices + (place ^ across))
        for task in range(tasks)
        for place in range(devices)
    ]
    return lax.ppermute(values, ("task", "feat"), pairs)


def plane_parts(values):
    chips, devices = values.shape[:2]
    values = values.reshape((chips, devices // 2, 2) + values.shape[2:])
    chip, side = lax.axis_index("task") // 2, lax.axis_index("feat") % 2
    parts = []
    for up in range(chips):
        part = lax.dynamic_index_in_dim(values, (chip + up) % chips, 0, keepdims=False)
        for across in range(2):
            parts.append(lax.dynamic_index_in_dim(part, side ^ across, 1, keepdims=False))
    return parts


def reduce_plane(parts):
    total = parts[0].astype(F32)
    for place, part in enumerate(parts[1:], 1):
        total = total + in_plane(part, place // 2, place % 2).astype(F32)
    return total.astype(BF)


def layer_parts(values):
    layers = values.shape[0]
    layer = lax.axis_index("feat") // 2
    return [
        lax.dynamic_index_in_dim(values, (layer + shift) % layers, 0, keepdims=False)
        for shift in range(layers)
    ]


def reduce_layers(parts):
    total = parts[0].astype(F32)
    for shift, part in enumerate(parts[1:], 1):
        total = total + along_z(part, shift).astype(F32)
    return total


def to_owners(one, two):
    chips = lax.axis_size("task") // 2
    chip = lax.axis_index("task") // 2
    even = chip % 2 == 0
    stay, leave = jnp.where(even, one, two), jnp.where(even, two, one)

    def target(chip, second):
        return chip // 2 + (chips // 2 if second else 0)

    def send(values, odd_second):
        return moved_by(
            values,
            "task",
            lambda place: 2 * target(place // 2, (place // 2 % 2 == 1) == odd_second) + place % 2,
        )

    if chips > 2:
        stay = send(stay, True)
    leave = send(leave, False)
    early = chip < chips // 2
    return jnp.concatenate(
        [jnp.where(early, stay, leave), jnp.where(early, leave, stay)], axis=0
    )


def place_copies(chips, layers, table, *refs):
    count = 2 * chips
    near, far = refs[:count], refs[count : count + 4]
    *halves, attn_out, in_out, out_out, block_out, pair, copied = refs[count + 4 :]
    step = pl.program_id(0)
    moves = []
    for half in halves:
        for deal in range(half.shape[-4]):
            for feature in range(half.shape[-3]):
                index = (slice(None),) + (1,) * (len(half.shape) - 5) + (deal, feature)
                place = len(moves)
                target = block_out.at[feature, place // half.shape[-3]]
                moves.append(pltpu.make_async_copy(half.at[index], target, copied.at[place]))

    @pl.when(step == 0)
    def _():
        for move in moves:
            move.start()
    side, layer = table[count], table[count + 1]
    rows = near[0].shape[2]
    half = far[0].shape[1] // 2

    def owner(other, behind):
        return ((layer + layers - behind) % layers) * 2 + (side ^ other)

    for place in range(count):

        @pl.when(step == place)
        def _():
            core, chip = place // chips, place % chips
            for other in range(2):
                for behind in range(layers):
                    at = owner(other, behind)
                    attn_out[block_of(at, rows)] = near[place][other, behind]
                    part = far[core * 2 + other]
                    pair[block_of(at, half)] = part[chip * layers + behind, :half]
                    out_out[block_of(at, half)] = part[chip * layers + behind, half:]

    in_out[...] = pair[...].T

    @pl.when(step == count - 1)
    def _():
        for move in moves:
            move.wait()


def gather_layers(own_attn, own_ff):
    layers = lax.axis_size("feat") // 2
    nears = [own_attn] + [along_z(own_attn, shift) for shift in range(1, layers)]
    fars = [own_ff] + [along_z(own_ff, shift) for shift in range(1, layers)]
    return jnp.stack(nears), jnp.stack(fars)


def gather_rest(nears, fars, came_halves):
    layers, rows_near, width = nears.shape
    rows_far = fars.shape[1]
    chips = lax.axis_size("task") // 2
    task, place = lax.axis_index("task"), lax.axis_index("feat")
    near = jnp.stack([nears, along_x(nears)])
    far = jnp.concatenate([fars] + [along_y(fars, shift) for shift in range(1, chips)])
    nears = [near] + [along_y(near, shift) for shift in range(1, chips)]
    fars = [far, along_x(far)]
    nears = nears + [other_core(value) for value in nears]
    fars = fars + [other_core(value) for value in fars]
    steps = jnp.arange(2 * chips, dtype=jnp.int32)
    chip = (task // 2 - steps) % chips
    core = (task % 2) ^ (steps // chips)
    table = jnp.concatenate([chip * 2 + core, jnp.stack([place % 2, place // 2])])
    total = 2 * chips
    owned = 2 * layers
    devices, _, local, _, _ = came_halves[-1].shape
    deals = sum(value.shape[-4] for value in came_halves)

    def held(value):
        zeros = (0,) * value.ndim
        return pl.BlockSpec(
            value.shape, lambda step, table: zeros, pipeline_mode=pl.Buffered(1)
        )

    return pl.pallas_call(
        functools.partial(place_copies, chips, layers),
        grid_spec=pltpu.PrefetchScalarGridSpec(
            num_scalar_prefetch=1,
            grid=(total,),
            in_specs=[held(value) for value in nears + fars] + [ANYWHERE] * len(came_halves),
            out_specs=[
                pl.BlockSpec((owned * rows_near, width), lambda step, table: (table[step], 0)),
                pl.BlockSpec(
                    (width, owned * rows_far // 2), lambda step, table: (0, table[step])
                ),
                pl.BlockSpec(
                    (owned * rows_far // 2, width), lambda step, table: (table[step], 0)
                ),
                ANYWHERE,
            ],
            scratch_shapes=[
                pltpu.VMEM((owned * rows_far // 2, width), BF),
                pltpu.SemaphoreType.DMA((deals * local,)),
            ],
        ),
        out_shape=[
            jax.ShapeDtypeStruct((total * owned * rows_near, width), BF),
            jax.ShapeDtypeStruct((width, total * owned * rows_far // 2), BF),
            jax.ShapeDtypeStruct((total * owned * rows_far // 2, width), BF),
            jax.ShapeDtypeStruct((local, deals, devices, BLOCK, width), BF),
        ],
        compiler_params=pltpu.CompilerParams(vmem_limit_bytes=40 * 1024 * 1024),
        name="place_copies",
    )(table.astype(jnp.int32), *nears, *fars, *came_halves)


def by_halves(parts):
    while len(parts) > 1:
        half_way = len(parts) // 2
        parts = [one + two for one, two in zip(parts[:half_way], parts[half_way:])]
    return parts[0]


def total_of(values):
    chips, layers = lax.axis_size("task") // 2, lax.axis_size("feat") // 2
    values = values + other_core(values)
    rows = []
    for up in range(chips):
        near = in_plane(values, up, 0) if up else values
        rows.append(near + in_plane(values, up, 1))
    values = by_halves(rows)
    return by_halves([values] + [along_z(values, shift) for shift in range(1, layers)])


def shards(
    tokens,
    cotangent,
    attn_weights,
    weight_in,
    weight_out,
    norm_params,
    master_attn,
    master_in,
    master_out,
    first_attn,
    first_in,
    first_out,
    first_norms,
    second_attn,
    second_in,
    second_out,
    second_norms,
    sample_count,
    feature_count,
):
    local, samples, width = tokens.shape[1:]
    devices = lax.axis_size("feat")
    tasks = lax.axis_size("task")
    chips = tasks // 2
    place = lax.axis_index("feat")
    deals = samples // (devices * BLOCK)
    counts = jnp.stack(
        [sample_count[0], feature_count[0], place * local, place, lax.axis_index("task") % 2]
    ).astype(jnp.int32)
    weights = attn_weights.reshape(8, width, width)

    early = max(deals // 2, 1)
    late = deals - early
    groups = 1
    own_ff = weight_in.shape[1] // (tasks * devices)
    own_attn = attn_weights.shape[0] // (tasks * devices)

    def dealt(values):
        count = values.shape[1] // (devices * BLOCK)
        values = values.reshape(local, count, devices, BLOCK, width)
        return values.transpose(2, 1, 0, 3, 4)

    came_cot = exchange(dealt(cotangent[0, :, : early * devices * BLOCK]), "feat")
    dealt_x, *rest = run_sample_forward(
        counts, tokens[0], cotangent[0], weights, norm_params, devices, early
    )
    came_cot, dealt_x, *rest = lax.optimization_barrier((came_cot, dealt_x, *rest))
    saved = [tokens[0]] + rest[-4:]
    came_x = exchange(dealt_x, "feat")
    shared = (weights, weight_in, weight_out, norm_params, chips)
    came_both = None
    if late:
        dealt_late, came_x = lax.optimization_barrier((rest[0], came_x))
        came_late = exchange(dealt_late, "feat")
        dealt_both, *held = run_middle(
            counts, (came_x, None), (came_cot, None), *shared, 0, None, 0
        )
        *dealt_d, dealt_y, keep_two, send_two, norms_two = run_middle(
            counts, (came_late, 0), (came_late, 1), *shared, early, held, groups
        )
        came_both = exchange(dealt_both, "feat")
        came_both, dealt_d, dealt_y, keep_two, send_two, norms_two = lax.optimization_barrier(
            (came_both, dealt_d, dealt_y, keep_two, send_two, norms_two)
        )
    else:
        *dealt_d, dealt_y, keep_two, send_two, norms_two = run_middle(
            counts, (came_x, None), (came_cot, None), *shared, 0, None, groups
        )
    came_d = exchange(dealt_d[0], "feat")
    parts_two = plane_parts(reduce_core(keep_two, send_two))
    held = None
    if late:
        came_both, _ = lax.optimization_barrier((came_both, parts_two))
        held = run_sample_backward_early(counts, came_both, saved, weights)
    dealt_y, came_d, held = lax.optimization_barrier((dealt_y, came_d, held))
    came_y = exchange(dealt_y, "feat")
    input_grad, keep_one, send_one, norms_one = run_sample_backward(
        counts, came_both, held, came_d, saved, weights, norm_params, chips
    )
    parts_two[0], came_y, input_grad, keep_one, send_one, norms_one = lax.optimization_barrier(
        (parts_two[0], came_y, input_grad, keep_one, send_one, norms_one)
    )
    parts_two = layer_parts(reduce_plane(parts_two))
    parts_two, keep_one, send_one = lax.optimization_barrier((parts_two, keep_one, send_one))
    parts_one = layer_parts(reduce_plane(plane_parts(reduce_core(keep_one, send_one))))
    share_two, parts_one = lax.optimization_barrier((reduce_layers(parts_two), parts_one))
    share_one = reduce_layers(parts_one)
    share_in_turned = share_two[:own_ff]
    share_out = share_two[own_ff : 2 * own_ff]
    local_squares = jnp.sum(share_one * share_one) + jnp.sum(share_two * share_two)
    small = jnp.concatenate(
        [norms_one, norms_two, jnp.full((2, width), local_squares, F32)], axis=0
    )
    small, part_one, part_two = lax.optimization_barrier(
        (small, share_one, share_two[2 * own_ff :])
    )
    share_attn = to_owners(part_one, part_two)
    small, share_attn = lax.optimization_barrier((total_of(small), share_attn))
    total_norms = small[:6]
    squares = small[6, 0] + jnp.sum(total_norms * total_norms)
    grad_norm = jnp.sqrt(squares)
    factor = jnp.minimum(1.0, CLIP_AT / (grad_norm + 1e-06))
    new_attn, moment_attn, square_attn = adam_step(
        master_attn, factor * share_attn, first_attn, second_attn, RATE
    )
    new_in, moment_in, square_in = adam_step(
        master_in, factor * share_in_turned.T, first_in, second_in, RATE
    )
    new_out, moment_out, square_out = adam_step(
        master_out, factor * share_out, first_out, second_out, RATE
    )
    new_norms, moment_norms, square_norms = adam_step(
        norm_params, factor * total_norms, first_norms, second_norms, NORM_RATE
    )
    own_both = jnp.concatenate([new_in.astype(BF).T, new_out.astype(BF)], axis=0)
    nears, fars = gather_layers(new_attn.astype(BF), own_both)
    came_halves = [came_y] if came_both is None else [came_both, came_y]
    copy_attn, copy_in, copy_out, block_out = gather_rest(nears, fars, came_halves)
    block_out = block_out.reshape(1, local, samples, width)
    return (
        block_out,
        input_grad[None],
        grad_norm.reshape(1),
        new_attn,
        new_in,
        new_out,
        new_norms,
        moment_attn,
        moment_in,
        moment_out,
        moment_norms,
        square_attn,
        square_in,
        square_out,
        square_norms,
        copy_attn,
        copy_in,
        copy_out,
    )


def solution(mesh):
    cells = P("task", "feat", None, None)
    rows = P(("task", "feat"), None)
    columns = P(None, ("task", "feat"))
    return jax.shard_map(
        shards,
        mesh=mesh,
        in_specs=(cells, cells, P(), P(), P(), P())
        + (rows, columns, rows)
        + (rows, columns, rows, P())
        + (rows, columns, rows, P())
        + (P("task"), P("task")),
        out_specs=(cells, cells, P())
        + (rows, columns, rows, P())
        + (rows, columns, rows, P())
        + (rows, columns, rows, P())
        + (P(), P(), P()),
        check_vma=False,
    )
```

```python
import functools

import jax
import jax.numpy as jnp
from jax import lax
from jax.experimental import pallas as pl
from jax.experimental.pallas import tpu as pltpu
from jax.sharding import PartitionSpec as P

HEADS = 8
STEP = 5
NEGATIVE = -1e30
LN_EPS = 1e-05
CLIP_AT = 1.0
BETA_ONE = 0.9
BETA_TWO = 0.999
RATE = 0.02
NORM_RATE = 0.25
DECAY = 0.1
ADAM_EPS = 1e-08

BLOCK = 16
UNIT = 128
ROWS = 128
QUERIES = 512
UNROLL = 2
VMEM_BYTES = 60 * 1024 * 1024

BF = jnp.bfloat16
F32 = jnp.float32
NN = ((1,), (0,))
NT = ((1,), (1,))
TN = ((0,), (0,))


def dot(left, right, dims=NN):
    return lax.dot_general(left, right, (dims, ((), ())), preferred_element_type=F32)


def normalize(values):
    center = jnp.mean(values, axis=-1, keepdims=True)
    centred = values - center
    spread = jnp.mean(centred * centred, axis=-1, keepdims=True)
    scale = lax.rsqrt(spread + LN_EPS)
    return centred * scale, scale


def normalize_back(normal, scale, grad, gain):
    d_normal = grad * gain
    mean_one = jnp.mean(d_normal, axis=-1, keepdims=True)
    mean_two = jnp.mean(d_normal * normal, axis=-1, keepdims=True)
    return scale * (d_normal - mean_one - normal * mean_two)


def column_sum(values):
    return jnp.sum(values, axis=0, keepdims=True)


def by_unit(units, one):
    parts = [one(slice(place * UNIT, (place + 1) * UNIT)) for place in range(units)]
    return jnp.concatenate(parts, axis=1)


def scaled(values, head_size):
    return (values.astype(BF).astype(F32) * head_size ** (-0.5)).astype(BF)


def block_of(place, size):
    return pl.ds(pl.multiple_of(place * size, size), size)


def row_index(shape):
    return lax.broadcasted_iota(jnp.int32, shape, 0)


def sample_forward(late, counts, tokens, cotangent, weights, norms, x_out, *rest):
    if late:
        late_out, *rest = rest
    first_out, heads_out, mixed_out, log_out, turned = rest
    samples, width = tokens.shape[1:]
    head_size = width // HEADS
    early = x_out.shape[1]
    dealt = (x_out.shape[0], BLOCK, width)
    group = dealt[0] * BLOCK

    @pl.when(pl.program_id(0) == 0)
    def _():
        for which in range(3):
            turned[which] = weights[which].T

    for low in range(0, samples, ROWS):
        rows = slice(low, low + ROWS)
        normal, _ = normalize(tokens[0, rows].astype(F32))
        first_out[0, rows] = (normal * norms[0:1] + norms[1:2]).astype(BF)
    first = first_out[0]
    heads_out[0, 0] = scaled(dot(turned[0], first, NT), head_size)
    for which in range(1, 3):
        heads_out[0, which] = dot(turned[which], first, NT).astype(BF)
    live = row_index((samples, 1)) < counts[0]
    for head in range(HEADS):
        lanes = slice(head * head_size, (head + 1) * head_size)
        keys = heads_out[0, 1, lanes]
        values = heads_out[0, 2, lanes]
        for low in range(0, samples, QUERIES):
            cols = slice(low, low + QUERIES)
            scores = dot(keys, heads_out[0, 0, lanes, cols], TN)
            scores = jnp.where(live, scores, NEGATIVE)
            top = jnp.max(scores, axis=0, keepdims=True)
            powers = jnp.exp(scores - top)
            total = jnp.sum(powers, axis=0, keepdims=True)
            mixed = dot(values, powers.astype(BF)) * (1.0 / total)
            mixed_out[0, lanes, cols] = mixed.astype(BF)
            log_out[0, head : head + 1, cols] = top + jnp.log(total)
    for low in range(0, samples, group):
        rows = slice(low, low + group)
        part = tokens[0, rows].astype(F32) + dot(mixed_out[0, :, rows], weights[3], TN)
        part = part.astype(BF).reshape(dealt)
        if low // group < early:
            x_out[:, low // group, 0] = part
        else:
            late_out[:, 0, low // group - early, 0] = part
            late_out[:, 1, low // group - early, 0] = cotangent[0, rows].reshape(dealt)


def heads_back(heads, mixed, logs, d_mix, rows, live, d_query, add):
    width = d_mix.shape[0]
    head_size = width // HEADS
    for pair in range(0, HEADS, 2):
        d_keys, d_values = [], []
        for head in (pair, pair + 1):
            lanes = slice(head * head_size, (head + 1) * head_size)
            keys = heads[0, 1, lanes]
            values = heads[0, 2, lanes]
            queries = heads[0, 0, lanes, rows]
            grads = d_mix[lanes]
            shared = column_sum(grads.astype(F32) * mixed[0, lanes, rows].astype(F32))
            scores = jnp.where(live, dot(keys, queries, TN), NEGATIVE)
            probs = jnp.exp(scores - logs[0, head : head + 1, rows])
            d_probs = dot(values, grads, TN)
            d_scores = (probs * (d_probs - shared)).astype(BF)
            d_query[lanes] = (dot(keys, d_scores) * head_size ** (-0.5)).astype(BF)
            d_keys.append(dot(d_scores, queries, NT))
            d_values.append(dot(probs.astype(BF), grads, NT))
        lanes = slice(pair * head_size, (pair + 2) * head_size)
        add(lanes, jnp.concatenate(d_keys, axis=1), jnp.concatenate(d_values, axis=1))


def sample_backward_early(
    counts, d_early, heads, mixed, logs, weights, query_out, sums_out, weight_out, d_rows, d_mix, d_query, total
):
    samples = mixed.shape[2]
    width = d_mix.shape[0]
    group = d_early.shape[0] * BLOCK
    rows = slice(0, d_rows.shape[0])
    step = pl.program_id(0)

    @pl.when(step == 0)
    def _():
        total[...] = jnp.zeros_like(total)

    @pl.when(counts[2] + step < counts[1])
    def _():
        for deal in range(d_early.shape[1]):
            part = d_early[:, deal, 0].reshape(group, width)
            d_rows[deal * group : (deal + 1) * group] = part
        d_mix[...] = dot(weights[3], d_rows[...], NT).astype(BF)
        total[...] += dot(mixed[0, :, rows], d_rows[...])
        live = row_index((samples, 1)) < counts[0]

        def add(lanes, d_keys, d_values):
            sums_out[0, 0, :, lanes] = d_keys
            sums_out[0, 1, :, lanes] = d_values

        heads_back(heads, mixed, logs, d_mix, rows, live, d_query, add)
        query_out[0] = d_query[...].T

    @pl.when(step == pl.num_programs(0) - 1)
    def _():
        weight_out[...] = total[...]


def sample_backward(early, counts, *refs):
    if early:
        d_early, query_held, sums_held, weight_held, *refs = refs
    d_late, first, heads, mixed, logs, weights, *refs = refs
    heads_out, keep_out, send_out, d_rows, d_mix, d_query, d_turned, total = refs
    samples, width = first.shape[1:]
    group = d_late.shape[0] * BLOCK
    start = early * group
    rows = slice(start, samples)
    step = pl.program_id(0)

    @pl.when(step == 0)
    def _():
        total[...] = jnp.zeros_like(total)
        if early:
            total[3 * width :] = weight_held[...]

    feature_live = counts[2] + step < counts[1]

    @pl.when(feature_live)
    def _():
        for low in range(0, samples, group):
            deal = low // group
            part = d_early[:, deal, 0] if deal < early else d_late[:, deal - early, 0]
            d_rows[low : low + group] = part.reshape(group, width)
        d_mix[...] = dot(weights[3], d_rows[rows], NT).astype(BF)
        total[3 * width :] += dot(mixed[0, :, rows], d_rows[rows])
        live = row_index((samples, 1)) < counts[0]

        def add(lanes, d_keys, d_values):
            if early:
                d_keys = d_keys + sums_held[0, 0, :, lanes]
                d_values = d_values + sums_held[0, 1, :, lanes]
            d_turned[1, :, lanes] = d_keys.astype(BF)
            d_turned[2, :, lanes] = d_values.astype(BF)

        heads_back(heads, mixed, logs, d_mix, rows, live, d_query, add)
        d_turned[0, rows] = d_query[...].T
        if early:
            d_turned[0, :start] = query_held[0]
        for which in range(3):
            total[which * width : (which + 1) * width] += dot(first[0], d_turned[which], TN)
            heads_out[0, which] = d_turned[which]

    @pl.when(step == pl.num_programs(0) - 1)
    def _():
        attention_parts(keep_out, total, counts[4], 0)
        attention_parts(send_out, total, 1 - counts[4], 0)


def input_backward(early, counts, *refs):
    if early:
        d_early, *refs = refs
    d_late, d_heads, tokens, weights, norms, grad_out, norm_out, d_rows, norm_total = refs
    samples, width = tokens.shape[1:]
    group = d_late.shape[0] * BLOCK
    step = pl.program_id(0)

    @pl.when(step == 0)
    def _():
        norm_total[...] = jnp.zeros_like(norm_total)

    feature_live = counts[2] + step < counts[1]

    @pl.when(jnp.logical_not(feature_live))
    def _():
        grad_out[...] = jnp.zeros_like(grad_out)

    @pl.when(feature_live)
    def _():
        for low in range(0, samples, group):
            deal = low // group
            part = d_early[:, deal, 0] if deal < early else d_late[:, deal - early, 0]
            d_rows[low : low + group] = part.reshape(group, width)
        for low in range(0, samples, ROWS):
            part = slice(low, low + ROWS)
            d_first = dot(d_heads[0, 0, part], weights[0], NT)
            d_first = d_first + dot(d_heads[0, 1, part], weights[1], NT)
            d_first = d_first + dot(d_heads[0, 2, part], weights[2], NT)
            normal, scale = normalize(tokens[0, part].astype(F32))
            norm_total[0:1] += column_sum(d_first * normal)
            norm_total[1:2] += column_sum(d_first)
            back = normalize_back(normal, scale, d_first, norms[0:1])
            grad_out[0, part] = (d_rows[part].astype(F32) + back).astype(BF)

    @pl.when(step == pl.num_programs(0) - 1)
    def _():
        norm_out[...] = norm_total[...]


def gelu_parts(pre):
    root = 0.7978845608028654
    square = pre * pre
    curve = jnp.tanh(root * pre * (1.0 + 0.044715 * square))
    half = 0.5 * (1.0 + curve)
    slope = half + (0.5 * root) * pre * (1.0 - curve * curve) * (1.0 + 3 * 0.044715 * square)
    return pre * half, slope


def part_of(total, chip, core, owners, rows):
    start = pl.multiple_of((chip * 2 + core) * (owners * rows), owners * rows)
    part = total[pl.ds(start, owners * rows)].astype(BF)
    return part.reshape(owners, rows, part.shape[-1])


def attention_parts(where, total, core, low):
    chips, owners = where.shape[:2]
    half = total.shape[0] // (2 * chips * owners)
    for pair in range(chips // 2):
        part = part_of(total, pair, core, owners, 2 * half)
        for piece in range(2):
            rows = part[:, piece * half : (piece + 1) * half]
            where[2 * pair + piece, :, low : low + half] = rows


def middle(offset, opening, closing, groups, counts, *refs):
    refs = list(refs)

    def take(count):
        return [refs.pop(0) for _ in range(count)]

    step = pl.program_id(0)
    x_in, cot_in, weights, weight_in, weight_out, norms = take(6)
    if not opening:
        held = take(3)
        (norm_held,) = take(1)
    if closing:
        d_outs = take(groups)
        y_out, keep_out, send_out, norm_out = take(4)
    else:
        (both_out,) = take(1)
        given = take(3)
        (norm_out,) = take(1)
    turned, order, back_order, x_one, normal_one, scale_one, normal_two, scale_two = take(8)
    x_two, low_rows, heads, d_heads, d_turned, mixed, d_mix, probs, live_grad = take(9)
    third, grad_rows, *totals, norm_total, copied = take(7)
    total_attn, total_in, total_out = totals
    if not opening:
        loads = [
            pltpu.make_async_copy(source, target, copied.at[place])
            for place, (source, target) in enumerate(zip(held, totals))
        ]
    if not closing:
        stores = [
            pltpu.make_async_copy(source, target, copied.at[place])
            for place, (source, target) in enumerate(zip(totals, given))
        ]
        last = step == pl.num_programs(0) - 1
    devices, _, local, _, width = x_in.shape
    features = devices * local
    cells = features * BLOCK
    head_size = width // HEADS
    score_scale = head_size ** (-0.5)
    hidden_width = weight_in.shape[1]
    first_sample = ((offset + step) * devices + counts[3]) * BLOCK

    @pl.when(step == 0)
    def _():
        if not opening:
            for load in loads:
                load.start()
        for which in range(3):
            turned[which] = weights[which].T
        here = row_index((cells, cells))
        there = lax.broadcasted_iota(jnp.int32, (cells, cells), 1)
        source = (here % features) * BLOCK + here // features
        order[...] = jnp.where(source == there, 1.0, 0.0).astype(BF)
        source = (here % BLOCK) * features + here // BLOCK
        back_order[...] = jnp.where(source == there, 1.0, 0.0).astype(BF)
        if opening:
            for total in totals:
                total[...] = jnp.zeros_like(total)
            norm_total[...] = jnp.zeros_like(norm_total)
        else:
            norm_total[...] = norm_held[...]

    x_one[...] = dot(order[...], x_in[:, 0].reshape(cells, width))
    for low in range(0, cells, ROWS):
        rows = slice(low, low + ROWS)
        normal, scale = normalize(x_one[rows])
        normal_one[rows] = normal
        scale_one[rows] = scale
        low_rows[rows] = (normal * norms[2:3] + norms[3:4]).astype(BF)
    heads[0] = scaled(dot(turned[0], low_rows[...], NT), head_size)
    for which in range(1, 3):
        heads[which] = dot(turned[which], low_rows[...], NT).astype(BF)

    units = cells // UNIT
    key_row = row_index((UNIT, cells))
    query_row = lax.broadcasted_iota(jnp.int32, (UNIT, cells), 1) % UNIT
    mask = (key_row // features == query_row // features) & (key_row % features < counts[1])
    for head in range(HEADS):
        lanes = slice(head * head_size, (head + 1) * head_size)
        scores = by_unit(units, lambda cols: dot(heads[1, lanes, cols], heads[0, lanes, cols], TN))
        scores = jnp.where(mask, scores, NEGATIVE)
        top = jnp.max(scores, axis=0, keepdims=True)
        powers = jnp.exp(scores - top)
        total = jnp.sum(powers, axis=0, keepdims=True)
        prob = powers * (1.0 / total)
        probs[head] = prob
        prob = prob.astype(BF)
        mixed[lanes] = by_unit(units, lambda cols: dot(heads[2, lanes, cols], prob[:, cols])).astype(BF)
    for low in range(0, cells, ROWS):
        rows = slice(low, low + ROWS)
        part = x_one[rows] + dot(mixed[:, rows], weights[3], TN)
        x_two[rows] = part
        normal, scale = normalize(part)
        normal_two[rows] = normal
        scale_two[rows] = scale
        third[rows] = (normal * norms[4:5] + norms[5:6]).astype(BF)

    if not opening:

        @pl.when(step == 0)
        def _():
            for load in loads:
                load.wait()

    def write_d(values):
        if not closing:
            both_out[:, 0, 0] = values
            return
        count = local // groups
        for place, d_out in enumerate(d_outs):
            d_out[:, 0] = values[:, place * count : (place + 1) * count]

    alive = first_sample < counts[0]

    @pl.when(jnp.logical_not(alive))
    def _():

        @pl.loop(0, hidden_width // width)
        def _(block):
            cols = block_of(block, width)
            hidden, _ = gelu_parts(dot(third[...], weight_in[:, cols]))
            x_two[...] += dot(hidden.astype(BF), weight_out[cols])

        write_d(jnp.zeros((devices, local, BLOCK, width), BF))
        if not closing:

            @pl.when(last)
            def _():
                for store in stores[1:]:
                    store.start()

    @pl.when(alive)
    def _():
        place = row_index((cells, 1))
        cell_live = (place % features < counts[1]) & (
            first_sample + place // features < counts[0]
        )
        grads = dot(order[...], cot_in[:, 0].reshape(cells, width))
        live_grad[...] = jnp.where(cell_live, grads, 0.0).astype(BF)
        grad_rows[...] = jnp.zeros_like(grad_rows)

        @pl.loop(0, hidden_width // width)
        def _(block):
            cols = block_of(block, width)
            hidden, slope = gelu_parts(dot(third[...], weight_in[:, cols]))
            hidden = hidden.astype(BF)
            x_two[...] += dot(hidden, weight_out[cols])
            total_out[cols] += dot(hidden, live_grad[...], TN)
            d_pre = (dot(live_grad[...], weight_out[cols], NT) * slope).astype(BF)
            total_in[cols] += dot(d_pre, third[...], TN)
            grad_rows[...] += dot(d_pre, weight_in[:, cols], NT)

        if not closing:

            @pl.when(last)
            def _():
                for store in stores[1:]:
                    store.start()


        for low in range(0, cells, ROWS):
            rows = slice(low, low + ROWS)
            normal = normal_two[rows]
            d_third = grad_rows[rows]
            norm_total[2:3] += column_sum(d_third * normal)
            norm_total[3:4] += column_sum(d_third)
            back = normalize_back(normal, scale_two[rows], d_third, norms[4:5])
            back = back + live_grad[rows].astype(F32)
            grad_rows[rows] = back
            live_grad[rows] = back.astype(BF)
        d_mix[...] = dot(weights[3], live_grad[...], NT).astype(BF)
        total_attn[3 * width :] += dot(mixed[...], live_grad[...])
        for head in range(HEADS):
            lanes = slice(head * head_size, (head + 1) * head_size)
            prob = probs[head]
            grads = d_mix[lanes]
            shared = column_sum(grads.astype(F32) * mixed[lanes].astype(F32))
            d_probs = by_unit(units, lambda cols: dot(heads[2, lanes, cols], grads[:, cols], TN))
            d_scores = (prob * (d_probs - shared)).astype(BF)
            low_prob = prob.astype(BF)
            d_query = by_unit(units, lambda cols: dot(heads[1, lanes, cols], d_scores[:, cols]))
            d_heads[0, lanes] = (d_query * score_scale).astype(BF)
            d_key = by_unit(units, lambda cols: dot(heads[0, lanes, cols], d_scores[:, cols], NT))
            d_heads[1, lanes] = d_key.astype(BF)
            d_value = by_unit(units, lambda cols: dot(grads[:, cols], low_prob[:, cols], NT))
            d_heads[2, lanes] = d_value.astype(BF)
        for which in range(3):
            d_turned[which] = d_heads[which].T
        for which in range(3):
            total_attn[which * width : (which + 1) * width] += dot(low_rows[...], d_turned[which], TN)
        for low in range(0, cells, ROWS):
            rows = slice(low, low + ROWS)
            d_second = dot(d_turned[0, rows], weights[0], NT)
            d_second = d_second + dot(d_turned[1, rows], weights[1], NT)
            d_second = d_second + dot(d_turned[2, rows], weights[2], NT)
            normal = normal_one[rows]
            norm_total[0:1] += column_sum(d_second * normal)
            norm_total[1:2] += column_sum(d_second)
            back = normalize_back(normal, scale_one[rows], d_second, norms[2:3])
            live_grad[rows] = (grad_rows[rows] + back).astype(BF)
        moved = dot(back_order[...], live_grad[...]).astype(BF)
        write_d(moved.reshape(devices, local, BLOCK, width))

    moved = dot(back_order[...], x_two[...].astype(BF)).astype(BF)
    moved = moved.reshape(devices, local, BLOCK, width)
    if closing:
        y_out[:, 0] = moved
    else:
        both_out[:, 1, 0] = moved

    @pl.when(step == pl.num_programs(0) - 1)
    def _():
        if closing:
            chips, owners, rows, _ = keep_out.shape
            own_ff = hidden_width // (2 * chips * owners)
            for where, core in ((keep_out, counts[4]), (send_out, 1 - counts[4])):
                for chip in range(chips):
                    for which, total in ((0, total_in), (1, total_out)):
                        part = part_of(total, chip, core, owners, own_ff)
                        where[chip, :, which * own_ff : (which + 1) * own_ff] = part
                attention_parts(where, total_attn, core, 2 * own_ff)
        else:
            stores[0].start()
            for store in stores:
                store.wait()
        norm_out[...] = norm_total[...]


def whole(shape):
    zeros = (0,) * len(shape)
    return pl.BlockSpec(shape, lambda step: zeros, pipeline_mode=pl.Buffered(1))


def half(shape, which):
    return pl.BlockSpec(
        (shape[0] // 2,) + tuple(shape[1:]),
        lambda step: (which, 0, 0),
        pipeline_mode=pl.Buffered(1),
    )


def once(shape):
    zeros = (0,) * len(shape)
    return pl.BlockSpec(shape, lambda step: zeros)


def lead(shape):
    zeros = (0,) * (len(shape) - 1)
    return pl.BlockSpec((1,) + tuple(shape[1:]), lambda step: (step,) + zeros)


def call(body, grid, ins, outs, scratch, nanoseconds, name, aliases=None):
    return pl.pallas_call(
        body,
        grid=(grid,),
        in_specs=[pl.BlockSpec(memory_space=pltpu.SMEM)] + [spec for spec, _ in ins[1:]],
        out_specs=[spec for spec, _, _ in outs],
        out_shape=[jax.ShapeDtypeStruct(shape, kind) for _, shape, kind in outs],
        scratch_shapes=[
            pltpu.SemaphoreType.DMA((3,)) if kind is None else pltpu.VMEM(shape, kind)
            for shape, kind in scratch
        ],
        input_output_aliases=aliases or {},
        compiler_params=pltpu.CompilerParams(vmem_limit_bytes=VMEM_BYTES),
        cost_estimate=pl.CostEstimate(
            flops=nanoseconds * 1150000, bytes_accessed=1 << 24, transcendentals=0
        ),
        name=name,
    )(ins[0][1], *[value for _, value in ins[1:]])


ANYWHERE = pl.BlockSpec(memory_space=pl.ANY)


def run_sample_forward(counts, tokens, cotangent, weights, norms, devices, early):
    local, samples, width = tokens.shape
    late = samples // (devices * BLOCK) - early
    square = (local, samples, width)
    three = (local, 3, width, samples)
    stats = (local, HEADS, samples)
    outs = [
        (
            pl.BlockSpec((devices, early, 1, BLOCK, width), lambda step: (0, 0, step, 0, 0)),
            (devices, early, local, BLOCK, width),
            BF,
        )
    ]
    if late:
        outs.append(
            (
                pl.BlockSpec(
                    (devices, 2, late, 1, BLOCK, width), lambda step: (0, 0, 0, step, 0, 0)
                ),
                (devices, 2, late, local, BLOCK, width),
                BF,
            )
        )
    outs = outs + [
        (lead(square), square, BF),
        (lead(three), three, BF),
        (lead(square), (local, width, samples), BF),
        (lead(stats), stats, F32),
    ]
    return call(
        functools.partial(sample_forward, late),
        local,
        [
            (None, counts),
            (lead(square), tokens),
            (lead(square), cotangent),
            (half(weights.shape, 0), weights),
            (whole(norms.shape), norms),
        ],
        outs,
        [((3, width, width), BF)],
        25000,
        "sample_forward",
    )


def run_middle(counts, x_dealt, cot_dealt, weights, weight_in, weight_out, norms, chips, offset, held, groups):
    array, which = x_dealt
    devices = array.shape[0]
    deals, local, _, width = array.shape[-4:]
    cells = devices * local * BLOCK
    hidden_width = weight_in.shape[1]
    parts = (chips, devices, (hidden_width + 2 * width) // (chips * devices), width)

    def dealt(which):
        if which is None:
            return pl.BlockSpec(
                (devices, 1, local, BLOCK, width), lambda step: (0, step, 0, 0, 0)
            )
        return pl.BlockSpec(
            (devices, None, 1, local, BLOCK, width),
            lambda step: (0, which, step, 0, 0, 0),
        )

    ins = [
        (None, counts),
        (dealt(x_dealt[1]), x_dealt[0]),
        (dealt(cot_dealt[1]), cot_dealt[0]),
        (half(weights.shape, 1), weights),
        (whole(weight_in.shape), weight_in),
        (whole(weight_out.shape), weight_out),
        (whole(norms.shape), norms),
    ]
    sums = [(4 * width, width), (hidden_width, width), (hidden_width, width)]
    norm_sums = (4, width)
    if held is not None:
        ins = ins + [(ANYWHERE, value) for value in held[:3]] + [(whole(norm_sums), held[3])]
    if groups:
        few = (devices, deals, local // groups, BLOCK, width)
        piece = pl.BlockSpec((devices, 1) + few[2:], lambda step: (0, step, 0, 0, 0))
        outs = [(piece, few, BF)] * groups + [
            (dealt(None), (devices, deals, local, BLOCK, width), BF),
            (once(parts), parts, BF),
            (once(parts), parts, BF),
        ]
    else:
        outs = [
            (
                pl.BlockSpec(
                    (devices, 2, 1, local, BLOCK, width), lambda step: (0, 0, step, 0, 0, 0)
                ),
                (devices, 2, deals, local, BLOCK, width),
                BF,
            )
        ] + [(ANYWHERE, shape, F32) for shape in sums]
    outs.append((once(norm_sums), norm_sums, F32))
    square = (cells, width)
    turned = (width, cells)
    return call(
        functools.partial(middle, offset, held is None, bool(groups), groups),
        deals,
        ins,
        outs,
        [
            ((3, width, width), BF),
            ((cells, cells), BF),
            ((cells, cells), BF),
            (square, F32),
            (square, F32),
            ((cells, 1), F32),
            (square, F32),
            ((cells, 1), F32),
            (square, F32),
            (square, BF),
            ((3,) + turned, BF),
            ((3,) + turned, BF),
            ((3,) + square, BF),
            (turned, BF),
            (turned, BF),
            ((HEADS, UNIT, cells), F32),
            (square, BF),
            (square, BF),
            (square, F32),
        ]
        + [(shape, F32) for shape in sums]
        + [(norm_sums, F32), ((3,), None)],
        deals * 23000,
        "middle",
    )


def run_sample_backward_early(counts, both, saved, weights):
    devices, _, early, local, _, width = both.shape
    _, _, heads, mixed, logs = saved
    samples = mixed.shape[2]
    queries = (local, early * devices * BLOCK, width)
    sums = (local, 2, samples, width)
    return call(
        sample_backward_early,
        local,
        [(None, counts), (early_spec(both), both)]
        + [(lead(value.shape), value) for value in (heads, mixed, logs)]
        + [(half(weights.shape, 0), weights)],
        [
            (lead(queries), queries, BF),
            (lead(sums), sums, F32),
            (once((width, width)), (width, width), F32),
        ],
        [
            (queries[1:], BF),
            ((width, queries[1]), BF),
            ((width, queries[1]), BF),
            ((width, width), F32),
        ],
        22000,
        "sample_backward_early",
    )


def early_spec(both):
    devices, _, early, _, _, width = both.shape
    return pl.BlockSpec(
        (devices, None, early, 1, BLOCK, width), lambda step: (0, 0, 0, step, 0, 0)
    )


def run_sample_backward(counts, both, held, d_late, saved, weights, chips):
    devices, _, local, _, width = d_late.shape
    samples = saved[0].shape[1]
    early = 0 if both is None else both.shape[2]
    start = early * devices * BLOCK
    parts = (chips, devices, 4 * width // (2 * chips * devices), width)
    ins = [(None, counts)]
    if early:
        query, sums, weight = held
        ins = ins + [(early_spec(both), both), (lead(query.shape), query), (lead(sums.shape), sums)]
        ins.append((whole(weight.shape), weight))
    ins.append((late_spec(d_late), d_late))
    ins = ins + [(lead(value.shape), value) for value in saved[1:]]
    ins.append((half(weights.shape, 0), weights))
    heads = (local, 3, samples, width)
    return call(
        functools.partial(sample_backward, early),
        local,
        ins,
        [
            (lead(heads), heads, BF),
            (once(parts), parts, BF),
            (once(parts), parts, BF),
        ],
        [
            ((samples, width), BF),
            ((width, samples - start), BF),
            ((width, samples - start), BF),
            ((3, samples, width), BF),
            ((4 * width, width), F32),
        ],
        25000,
        "sample_backward",
    )


def late_spec(d_late):
    devices, late, _, _, width = d_late.shape
    return pl.BlockSpec((devices, late, 1, BLOCK, width), lambda step: (0, 0, step, 0, 0))


def run_input_backward(counts, both, d_late, d_heads, tokens, weights, norms):
    early = 0 if both is None else both.shape[2]
    local, samples, width = tokens.shape
    ins = [(None, counts)] + ([(early_spec(both), both)] if early else [])
    ins = ins + [
        (late_spec(d_late), d_late),
        (lead(d_heads.shape), d_heads),
        (lead(tokens.shape), tokens),
        (half(weights.shape, 0), weights),
        (whole(norms.shape), norms),
    ]
    return call(
        functools.partial(input_backward, early),
        local,
        ins,
        [
            (lead(tokens.shape), tokens.shape, BF),
            (once((2, width)), (2, width), F32),
        ],
        [((samples, width), BF), ((2, width), F32)],
        11000,
        "input_backward",
    )


def adam_step(weight, grad, first_m, second_m, rate):
    moment = BETA_ONE * first_m + (1.0 - BETA_ONE) * grad
    square = BETA_TWO * second_m + (1.0 - BETA_TWO) * grad * grad
    fix_one = 1.0 - BETA_ONE**STEP
    fix_two = 1.0 - BETA_TWO**STEP
    fresh = weight - rate * (
        moment / fix_one / (jnp.sqrt(square / fix_two) + ADAM_EPS) + DECAY * weight
    )
    return (fresh, moment, square)


def exchange(values, axis, groups=None):
    return lax.all_to_all(values, axis, 0, 0, axis_index_groups=groups, tiled=True)


def moved_by(values, axis, hop):
    pairs = [(place, hop(place)) for place in range(lax.axis_size(axis))]
    return lax.ppermute(values, axis, pairs)


def other_core(values):
    return moved_by(values, "task", lambda place: place ^ 1)


def along_y(values, shift):
    tasks = lax.axis_size("task")
    return moved_by(values, "task", lambda place: (place + 2 * shift) % tasks)


def along_x(values):
    return moved_by(values, "feat", lambda place: place ^ 1)


def along_z(values, shift):
    devices = lax.axis_size("feat")
    return moved_by(values, "feat", lambda place: (place + 2 * shift) % devices)


def reduce_core(keep, send):
    came = other_core(send)
    return (keep.astype(F32) + came.astype(F32)).astype(BF)


def in_plane(values, up, across):
    tasks, devices = lax.axis_size("task"), lax.axis_size("feat")
    pairs = [
        (task * devices + place, (task + 2 * up) % tasks * devices + (place ^ across))
        for task in range(tasks)
        for place in range(devices)
    ]
    return lax.ppermute(values, ("task", "feat"), pairs)


def plane_parts(values):
    chips, devices = values.shape[:2]
    values = values.reshape((chips, devices // 2, 2) + values.shape[2:])
    chip, side = lax.axis_index("task") // 2, lax.axis_index("feat") % 2
    parts = []
    for up in range(chips):
        part = lax.dynamic_index_in_dim(values, (chip + up) % chips, 0, keepdims=False)
        for across in range(2):
            parts.append(lax.dynamic_index_in_dim(part, side ^ across, 1, keepdims=False))
    return parts


def reduce_plane(parts):
    total = parts[0].astype(F32)
    for place, part in enumerate(parts[1:], 1):
        total = total + in_plane(part, place // 2, place % 2).astype(F32)
    return total.astype(BF)


def layer_parts(values):
    layers = values.shape[0]
    layer = lax.axis_index("feat") // 2
    return [
        lax.dynamic_index_in_dim(values, (layer + shift) % layers, 0, keepdims=False)
        for shift in range(layers)
    ]


def reduce_layers(parts):
    total = parts[0].astype(F32)
    for shift, part in enumerate(parts[1:], 1):
        total = total + along_z(part, shift).astype(F32)
    return total


def to_owners(one, two):
    chips = lax.axis_size("task") // 2
    chip = lax.axis_index("task") // 2
    even = chip % 2 == 0
    stay, leave = jnp.where(even, one, two), jnp.where(even, two, one)

    def target(chip, second):
        return chip // 2 + (chips // 2 if second else 0)

    def send(values, odd_second):
        return moved_by(
            values,
            "task",
            lambda place: 2 * target(place // 2, (place // 2 % 2 == 1) == odd_second) + place % 2,
        )

    if chips > 2:
        stay = send(stay, True)
    leave = send(leave, False)
    early = chip < chips // 2
    return jnp.concatenate(
        [jnp.where(early, stay, leave), jnp.where(early, leave, stay)], axis=0
    )


def place_copies(chips, layers, table, *refs):
    count = 2 * chips
    near, far = refs[:count], refs[count : count + 4]
    *halves, attn_out, in_out, out_out, block_out, pair, copied = refs[count + 4 :]
    step = pl.program_id(0)
    moves = []
    for half in halves:
        for deal in range(half.shape[-4]):
            for feature in range(half.shape[-3]):
                index = (slice(None),) + (1,) * (len(half.shape) - 5) + (deal, feature)
                place = len(moves)
                target = block_out.at[feature, place // half.shape[-3]]
                moves.append(pltpu.make_async_copy(half.at[index], target, copied.at[place]))

    @pl.when(step == 0)
    def _():
        for move in moves:
            move.start()
    side, layer = table[count], table[count + 1]
    rows = near[0].shape[2]
    half = far[0].shape[1] // 2

    def owner(other, behind):
        return ((layer + layers - behind) % layers) * 2 + (side ^ other)

    for place in range(count):

        @pl.when(step == place)
        def _():
            core, chip = place // chips, place % chips
            for other in range(2):
                for behind in range(layers):
                    at = owner(other, behind)
                    attn_out[block_of(at, rows)] = near[place][other, behind]
                    part = far[core * 2 + other]
                    pair[block_of(at, half)] = part[chip * layers + behind, :half]
                    out_out[block_of(at, half)] = part[chip * layers + behind, half:]

    in_out[...] = pair[...].T

    @pl.when(step == count - 1)
    def _():
        for move in moves:
            move.wait()


def gather_layers(own_attn, own_ff):
    layers = lax.axis_size("feat") // 2
    nears = [own_attn] + [along_z(own_attn, shift) for shift in range(1, layers)]
    fars = [own_ff] + [along_z(own_ff, shift) for shift in range(1, layers)]
    return jnp.stack(nears), jnp.stack(fars)


def gather_rest(nears, fars, came_halves):
    layers, rows_near, width = nears.shape
    rows_far = fars.shape[1]
    chips = lax.axis_size("task") // 2
    task, place = lax.axis_index("task"), lax.axis_index("feat")
    near = jnp.stack([nears, along_x(nears)])
    far = jnp.concatenate([fars] + [along_y(fars, shift) for shift in range(1, chips)])
    nears = [near] + [along_y(near, shift) for shift in range(1, chips)]
    fars = [far, along_x(far)]
    nears = nears + [other_core(value) for value in nears]
    fars = fars + [other_core(value) for value in fars]
    steps = jnp.arange(2 * chips, dtype=jnp.int32)
    chip = (task // 2 - steps) % chips
    core = (task % 2) ^ (steps // chips)
    table = jnp.concatenate([chip * 2 + core, jnp.stack([place % 2, place // 2])])
    total = 2 * chips
    owned = 2 * layers
    devices, _, local, _, _ = came_halves[-1].shape
    deals = sum(value.shape[-4] for value in came_halves)

    def held(value):
        zeros = (0,) * value.ndim
        return pl.BlockSpec(
            value.shape, lambda step, table: zeros, pipeline_mode=pl.Buffered(1)
        )

    return pl.pallas_call(
        functools.partial(place_copies, chips, layers),
        grid_spec=pltpu.PrefetchScalarGridSpec(
            num_scalar_prefetch=1,
            grid=(total,),
            in_specs=[held(value) for value in nears + fars] + [ANYWHERE] * len(came_halves),
            out_specs=[
                pl.BlockSpec((owned * rows_near, width), lambda step, table: (table[step], 0)),
                pl.BlockSpec(
                    (width, owned * rows_far // 2), lambda step, table: (0, table[step])
                ),
                pl.BlockSpec(
                    (owned * rows_far // 2, width), lambda step, table: (table[step], 0)
                ),
                ANYWHERE,
            ],
            scratch_shapes=[
                pltpu.VMEM((owned * rows_far // 2, width), BF),
                pltpu.SemaphoreType.DMA((deals * local,)),
            ],
        ),
        out_shape=[
            jax.ShapeDtypeStruct((total * owned * rows_near, width), BF),
            jax.ShapeDtypeStruct((width, total * owned * rows_far // 2), BF),
            jax.ShapeDtypeStruct((total * owned * rows_far // 2, width), BF),
            jax.ShapeDtypeStruct((local, deals, devices, BLOCK, width), BF),
        ],
        compiler_params=pltpu.CompilerParams(vmem_limit_bytes=40 * 1024 * 1024),
        name="place_copies",
    )(table.astype(jnp.int32), *nears, *fars, *came_halves)


def by_halves(parts):
    while len(parts) > 1:
        half_way = len(parts) // 2
        parts = [one + two for one, two in zip(parts[:half_way], parts[half_way:])]
    return parts[0]


def total_of(values):
    chips, layers = lax.axis_size("task") // 2, lax.axis_size("feat") // 2
    values = values + other_core(values)
    rows = []
    for up in range(chips):
        near = in_plane(values, up, 0) if up else values
        rows.append(near + in_plane(values, up, 1))
    values = by_halves(rows)
    return by_halves([values] + [along_z(values, shift) for shift in range(1, layers)])


def shards(
    tokens,
    cotangent,
    attn_weights,
    weight_in,
    weight_out,
    norm_params,
    master_attn,
    master_in,
    master_out,
    first_attn,
    first_in,
    first_out,
    first_norms,
    second_attn,
    second_in,
    second_out,
    second_norms,
    sample_count,
    feature_count,
):
    local, samples, width = tokens.shape[1:]
    devices = lax.axis_size("feat")
    tasks = lax.axis_size("task")
    chips = tasks // 2
    place = lax.axis_index("feat")
    deals = samples // (devices * BLOCK)
    counts = jnp.stack(
        [sample_count[0], feature_count[0], place * local, place, lax.axis_index("task") % 2]
    ).astype(jnp.int32)
    weights = attn_weights.reshape(8, width, width)

    early = max(deals // 2, 1)
    late = deals - early
    groups = 1
    own_ff = weight_in.shape[1] // (tasks * devices)
    own_attn = attn_weights.shape[0] // (tasks * devices)

    def dealt(values):
        count = values.shape[1] // (devices * BLOCK)
        values = values.reshape(local, count, devices, BLOCK, width)
        return values.transpose(2, 1, 0, 3, 4)

    came_cot = exchange(dealt(cotangent[0, :, : early * devices * BLOCK]), "feat")
    dealt_x, *rest = run_sample_forward(
        counts, tokens[0], cotangent[0], weights, norm_params, devices, early
    )
    came_cot, dealt_x, *rest = lax.optimization_barrier((came_cot, dealt_x, *rest))
    saved = [tokens[0]] + rest[-4:]
    came_x = exchange(dealt_x, "feat")
    shared = (weights, weight_in, weight_out, norm_params, chips)
    came_both = None
    if late:
        dealt_late, came_x = lax.optimization_barrier((rest[0], came_x))
        came_late = exchange(dealt_late, "feat")
        dealt_both, *held = run_middle(
            counts, (came_x, None), (came_cot, None), *shared, 0, None, 0
        )
        *dealt_d, dealt_y, keep_two, send_two, norms_two = run_middle(
            counts, (came_late, 0), (came_late, 1), *shared, early, held, groups
        )
        came_both = exchange(dealt_both, "feat")
        came_both, dealt_d, dealt_y, keep_two, send_two, norms_two = lax.optimization_barrier(
            (came_both, dealt_d, dealt_y, keep_two, send_two, norms_two)
        )
    else:
        *dealt_d, dealt_y, keep_two, send_two, norms_two = run_middle(
            counts, (came_x, None), (came_cot, None), *shared, 0, None, groups
        )
    came_d = exchange(dealt_d[0], "feat")
    parts_two = plane_parts(reduce_core(keep_two, send_two))
    held = None
    if late:
        came_both, _ = lax.optimization_barrier((came_both, parts_two))
        held = run_sample_backward_early(counts, came_both, saved, weights)
    dealt_y, came_d, held = lax.optimization_barrier((dealt_y, came_d, held))
    came_y = exchange(dealt_y, "feat")
    d_heads, keep_one, send_one = run_sample_backward(
        counts, came_both, held, came_d, saved, weights, chips
    )
    parts_two[0], came_y, d_heads, keep_one, send_one = lax.optimization_barrier(
        (parts_two[0], came_y, d_heads, keep_one, send_one)
    )
    parts_two = layer_parts(reduce_plane(parts_two))
    parts_two, keep_one, send_one = lax.optimization_barrier((parts_two, keep_one, send_one))
    plane_one = plane_parts(reduce_core(keep_one, send_one))
    plane_one, d_heads = lax.optimization_barrier((plane_one, d_heads))
    input_grad, norms_one = run_input_backward(
        counts, came_both, came_d, d_heads, tokens[0], weights, norm_params
    )
    plane_one[0], parts_two[0], input_grad, norms_one = lax.optimization_barrier(
        (plane_one[0], parts_two[0], input_grad, norms_one)
    )
    parts_one = layer_parts(reduce_plane(plane_one))
    share_two, parts_one = lax.optimization_barrier((reduce_layers(parts_two), parts_one))
    share_one = reduce_layers(parts_one)
    share_in_turned = share_two[:own_ff]
    share_out = share_two[own_ff : 2 * own_ff]
    local_squares = jnp.sum(share_one * share_one) + jnp.sum(share_two * share_two)
    small = jnp.concatenate(
        [norms_one, norms_two, jnp.full((2, width), local_squares, F32)], axis=0
    )
    small, part_one, part_two = lax.optimization_barrier(
        (small, share_one, share_two[2 * own_ff :])
    )
    share_attn = to_owners(part_one, part_two)
    small, share_attn = lax.optimization_barrier((total_of(small), share_attn))
    total_norms = small[:6]
    squares = small[6, 0] + jnp.sum(total_norms * total_norms)
    grad_norm = jnp.sqrt(squares)
    factor = jnp.minimum(1.0, CLIP_AT / (grad_norm + 1e-06))
    new_attn, moment_attn, square_attn = adam_step(
        master_attn, factor * share_attn, first_attn, second_attn, RATE
    )
    new_in, moment_in, square_in = adam_step(
        master_in, factor * share_in_turned.T, first_in, second_in, RATE
    )
    new_out, moment_out, square_out = adam_step(
        master_out, factor * share_out, first_out, second_out, RATE
    )
    new_norms, moment_norms, square_norms = adam_step(
        norm_params, factor * total_norms, first_norms, second_norms, NORM_RATE
    )
    own_both = jnp.concatenate([new_in.astype(BF).T, new_out.astype(BF)], axis=0)
    nears, fars = gather_layers(new_attn.astype(BF), own_both)
    came_halves = [came_y] if came_both is None else [came_both, came_y]
    copy_attn, copy_in, copy_out, block_out = gather_rest(nears, fars, came_halves)
    block_out = block_out.reshape(1, local, samples, width)
    return (
        block_out,
        input_grad[None],
        grad_norm.reshape(1),
        new_attn,
        new_in,
        new_out,
        new_norms,
        moment_attn,
        moment_in,
        moment_out,
        moment_norms,
        square_attn,
        square_in,
        square_out,
        square_norms,
        copy_attn,
        copy_in,
        copy_out,
    )


def solution(mesh):
    cells = P("task", "feat", None, None)
    rows = P(("task", "feat"), None)
    columns = P(None, ("task", "feat"))
    return jax.shard_map(
        shards,
        mesh=mesh,
        in_specs=(cells, cells, P(), P(), P(), P())
        + (rows, columns, rows)
        + (rows, columns, rows, P())
        + (rows, columns, rows, P())
        + (P("task"), P("task")),
        out_specs=(cells, cells, P())
        + (rows, columns, rows, P())
        + (rows, columns, rows, P())
        + (rows, columns, rows, P())
        + (P(), P(), P()),
        check_vma=False,
    )
```
